32 devices in a mesh: ctx: 16 (over z, x, core), tp: 2 (over y).
Axes of the slice: x: 2, y: 2, z: 4, core: 2. Of those that a mesh axis runs over, the one named last changes fastest.
Arguments:
- queries: bfloat16 [4096, 8192], P('ctx', 'tp'), may hold values from -6 to 6
- key_vectors: bfloat16 [4096, 1024], P(('ctx', 'tp')), may hold values from -6 to 6
- value_vectors: bfloat16 [4096, 1024], P(('ctx', 'tp')), may hold values from -6 to 6
- output_gradient: bfloat16 [4096, 8192], P('ctx', 'tp'), may hold values from -6 to 6
- doc_lengths: int32 [8], replicated, may hold values from 1 to 1793, 4096 in all
Outputs:
- attn_output: bfloat16 [4096, 8192], P('ctx', 'tp')
- grad_queries: bfloat16 [4096, 8192], P('ctx', 'tp')
- key_gradient: bfloat16 [4096, 1024], P(('ctx', 'tp'))
- value_gradient: bfloat16 [4096, 1024], P(('ctx', 'tp'))
The draws below stay inside these ranges and needn't reach their ends.
All inputs are finite; a program needn't handle non-finite values.
Results may differ from the reference program's by a relative error of at most 0.02.
Values may be sent and summed in bfloat16 or wider, within the bound.
No kernel may reach another device: no remote copies, remote signals or barrier semaphores. Data moves between devices by JAX's collectives and lax.ppermute only.
A program may use at most 128 MiB of HBM per device.

```python
import math
from functools import partial
import jax
import jax.numpy as jnp
import numpy as np
from jax import lax

QUERY_HEADS = 64
KEY_VALUE_HEADS = 8
HEAD_SIZE = 128
CONTEXT_TOKENS = 256
WINDOW = 8
PACKED_TOKENS = 4096
DOC_MAX = 1793
NDOCS = 8
N_CTX = 16


def draw_key_vectors(key, part):
    local_key_block = jax.random.fold_in(key, 11)
    unpadded_result = jnp.clip(jax.random.normal(local_key_block, (PACKED_TOKENS, KEY_VALUE_HEADS, HEAD_SIZE), jnp.float32), -6.0, 6.0)
    return unpadded_result.reshape(PACKED_TOKENS, KEY_VALUE_HEADS * HEAD_SIZE).astype(jnp.bfloat16)


def draw_queries(key, part):
    local_key_block = jax.random.fold_in(key, 23)
    heads_per_group = QUERY_HEADS // KEY_VALUE_HEADS
    unpadded_result = jnp.clip(jax.random.normal(local_key_block, (PACKED_TOKENS, KEY_VALUE_HEADS, heads_per_group, HEAD_SIZE), jnp.float32), -6.0, 6.0)
    return unpadded_result.reshape(PACKED_TOKENS, QUERY_HEADS * HEAD_SIZE).astype(jnp.bfloat16)


def block_scale(rng, shape, shards, least, high):
    loudness, own = 1.0, jax.random.fold_in(rng, 6)
    for dim, shards_of in shards:
        draws = jnp.exp(jax.random.uniform(jax.random.fold_in(own, dim), (shards_of,), jnp.float32, least / len(shards), high / len(shards)))
        loudness = loudness * jnp.repeat(draws, shape[dim] // shards_of).reshape([-1 if axis == dim else 1 for axis in range(len(shape))])
    return loudness


def split_up(number_of, total, bound, skew):
    loads = [(1 << 20) // math.isqrt(standing ** skew) + 1 for standing in range(2, number_of + 1)]
    rest, holding = total - bound - (number_of - 1), [1] * (number_of - 1)
    while rest > 0:
        candidates = [i for i in range(number_of - 1) if holding[i] < bound]
        mass, remaining = sum([loads[i] for i in candidates]), rest
        for i in candidates:
            addition = min(bound - holding[i], max(1, remaining * loads[i] // mass), rest)
            holding[i] = holding[i] + addition
            rest = rest - addition
    return np.array([bound] + holding)


def ragged_sizes(rng, amount, total, bound, skew):
    if amount == 2:
        one = jax.random.randint(rng, (), max(1, total - bound), min(bound, total - 1) + 1)
        return jnp.stack([one, total - one])
    lengths = jnp.asarray(split_up(amount, total, bound, skew), jnp.int32)
    couples = (amount - 1) // 2
    source_of, sink = lengths[1:1 + 2 * couples:2], lengths[2:2 + 2 * couples:2]
    slack = jnp.minimum(source_of - 1, bound - sink)
    moved = jax.random.randint(jax.random.fold_in(rng, 1), (couples,), 0, 1 << 20) % (slack + 1)
    lengths = lengths.at[1:1 + 2 * couples:2].set(source_of - moved).at[2:2 + 2 * couples:2].set(sink + moved)
    return lengths[jax.random.permutation(jax.random.fold_in(rng, 2), amount)]


def bell_draw(own_key, shape, scale, reach, shards=(), kind=jnp.bfloat16):
    factor_of = block_scale(own_key, shape, shards, -0.22, 0.18) if shards else 1.0
    result = jax.random.normal(own_key, shape, jnp.float32) * scale * factor_of
    return jnp.minimum(jnp.maximum(result, -reach), reach).astype(kind)


def setup_inputs(seed: int = 0) -> dict:
    streams_of = jax.random.split(jax.random.key(seed), 6)
    return {
        "queries": draw_queries(jax.random.fold_in(streams_of[5], 71), 0),
        "key_vectors": draw_key_vectors(jax.random.fold_in(streams_of[5], 71), 0),
        "value_vectors": bell_draw(streams_of[2], (PACKED_TOKENS, KEY_VALUE_HEADS * HEAD_SIZE), 1.0, 6.0, ((0, 32),)),
        "output_gradient": bell_draw(streams_of[3], (PACKED_TOKENS, QUERY_HEADS * HEAD_SIZE), 1.0, 6.0, ((0, 16), (1, 2))),
        "doc_lengths": ragged_sizes(streams_of[4], NDOCS, PACKED_TOKENS, DOC_MAX, 2).astype(jnp.int32),
    }


def doc_index_of(positions, doc_starts):
    above = (positions[:, None] >= doc_starts[None, :]).astype(jnp.int32)
    return lax.optimization_barrier(jnp.sum(above, axis=1)).astype(jnp.int32) - 1

def attend_all(block_q, block_g, key_block, value_block, allowed, score_scale):
    query_f = block_q.astype(jnp.float32)
    grad_f = block_g.astype(jnp.float32)
    key_f = key_block.astype(jnp.float32)
    value_f = value_block.astype(jnp.float32)
    scores = jnp.einsum('tgjd,kgd->gjtk', query_f, key_f) * score_scale
    scores = jnp.where(allowed[None, None], scores, -1e+30)
    row_top = lax.optimization_barrier(jnp.max(scores, axis=3, keepdims=True))
    row_total = lax.optimization_barrier(jnp.sum(jnp.exp(scores - row_top), axis=3, keepdims=True))
    log_total = row_top + jnp.log(row_total)
    weights = jnp.exp(scores - log_total)
    weights_low = weights.astype(jnp.bfloat16)
    low_f = weights_low.astype(jnp.float32)
    output = jnp.einsum('gjtk,kgd->tgjd', low_f, value_f).astype(jnp.bfloat16)
    row_delta = lax.optimization_barrier(jnp.sum(output.astype(jnp.float32) * grad_f, axis=3))
    row_delta = jnp.transpose(row_delta, (1, 2, 0))[..., None]
    grad_weights = jnp.einsum('tgjd,kgd->gjtk', grad_f, value_f)
    grad_scores = (weights * (grad_weights - row_delta) * score_scale).astype(jnp.bfloat16)
    scores_f = grad_scores.astype(jnp.float32)
    grad_query = jnp.einsum('gjtk,kgd->tgjd', scores_f, key_f).astype(jnp.bfloat16)
    grad_key = jnp.einsum('gjtk,tgjd->kgd', scores_f, query_f)
    grad_value = jnp.einsum('gjtk,tgjd->kgd', low_f, grad_f)
    return (output, grad_query, grad_key, grad_value)

def reference(queries, key_vectors, value_vectors, output_gradient, doc_lengths):
    heads_per_group = QUERY_HEADS // KEY_VALUE_HEADS
    score_scale = 1.0 / math.sqrt(HEAD_SIZE)
    reshaped_query = queries.reshape(N_CTX, CONTEXT_TOKENS, KEY_VALUE_HEADS, heads_per_group, HEAD_SIZE)
    reshaped_gradient = output_gradient.reshape(N_CTX, CONTEXT_TOKENS, KEY_VALUE_HEADS, heads_per_group, HEAD_SIZE)
    leading_rows = (WINDOW - 1) * CONTEXT_TOKENS
    key_padded = jnp.concatenate([jnp.zeros((leading_rows, KEY_VALUE_HEADS, HEAD_SIZE), jnp.bfloat16), key_vectors.reshape(PACKED_TOKENS, KEY_VALUE_HEADS, HEAD_SIZE)], axis=0)
    value_padded = jnp.concatenate([jnp.zeros((leading_rows, KEY_VALUE_HEADS, HEAD_SIZE), jnp.bfloat16), value_vectors.reshape(PACKED_TOKENS, KEY_VALUE_HEADS, HEAD_SIZE)], axis=0)
    doc_starts = jnp.cumsum(doc_lengths, dtype=jnp.int32) - doc_lengths
    local_pos = jnp.arange(CONTEXT_TOKENS, dtype=jnp.int32)
    complete_rows = WINDOW * CONTEXT_TOKENS

    def shard_step(grads, shard):
        first_pos = (shard * CONTEXT_TOKENS).astype(jnp.int32)
        query_pos = first_pos + local_pos
        query_doc = doc_index_of(query_pos, doc_starts)
        doc_start = jnp.max(jnp.where(doc_starts <= first_pos, doc_starts, 0))
        needed = jnp.clip(shard - doc_start // CONTEXT_TOKENS + 1, 1, WINDOW).astype(jnp.int32)
        block_q = lax.dynamic_index_in_dim(reshaped_query, shard, 0, keepdims=False)
        block_g = lax.dynamic_index_in_dim(reshaped_gradient, shard, 0, keepdims=False)

        def branch(slot_count):
            key_total_count = slot_count * CONTEXT_TOKENS
            begin = ((shard + WINDOW - slot_count) * CONTEXT_TOKENS).astype(jnp.int32)
            key_block = lax.dynamic_slice_in_dim(key_padded, begin, key_total_count, 0)
            value_block = lax.dynamic_slice_in_dim(value_padded, begin, key_total_count, 0)
            key_pos = first_pos + CONTEXT_TOKENS - key_total_count + jnp.arange(key_total_count, dtype=jnp.int32)
            key_doc = doc_index_of(key_pos, doc_starts)
            allowed = (query_doc[:, None] == key_doc[None, :]) & (key_pos[None, :] <= query_pos[:, None])
            output, grad_query, grad_key, grad_value = attend_all(block_q, block_g, key_block, value_block, allowed, score_scale)
            padded_width = jnp.zeros((complete_rows - key_total_count, KEY_VALUE_HEADS, HEAD_SIZE), jnp.float32)
            return (output, grad_query, jnp.concatenate([padded_width, grad_key], axis=0), jnp.concatenate([padded_width, grad_value], axis=0))
        output, grad_query, grad_key, grad_value = lax.switch(needed - 1, [partial(branch, count_slots) for count_slots in range(1, WINDOW + 1)])
        key_running_sum, value_running_sum = grads
        base_row = (shard * CONTEXT_TOKENS).astype(jnp.int32)
        key_running_sum = lax.dynamic_update_slice_in_dim(key_running_sum, lax.dynamic_slice_in_dim(key_running_sum, base_row, complete_rows, 0) + grad_key, base_row, 0)
        value_running_sum = lax.dynamic_update_slice_in_dim(value_running_sum, lax.dynamic_slice_in_dim(value_running_sum, base_row, complete_rows, 0) + grad_value, base_row, 0)
        return ((key_running_sum, value_running_sum), (output, grad_query))
    initial_state = (jnp.zeros((leading_rows + PACKED_TOKENS, KEY_VALUE_HEADS, HEAD_SIZE), jnp.float32), jnp.zeros((leading_rows + PACKED_TOKENS, KEY_VALUE_HEADS, HEAD_SIZE), jnp.float32))
    (key_running_sum, value_running_sum), (outputs, grad_qs) = lax.scan(shard_step, initial_state, jnp.arange(N_CTX, dtype=jnp.int32))
    attn_output = outputs.reshape(PACKED_TOKENS, QUERY_HEADS * HEAD_SIZE)
    grad_queries = grad_qs.reshape(PACKED_TOKENS, QUERY_HEADS * HEAD_SIZE)
    key_gradient = key_running_sum[leading_rows:].astype(jnp.bfloat16).reshape(PACKED_TOKENS, KEY_VALUE_HEADS * HEAD_SIZE)
    value_gradient = value_running_sum[leading_rows:].astype(jnp.bfloat16).reshape(PACKED_TOKENS, KEY_VALUE_HEADS * HEAD_SIZE)
    return (attn_output, grad_queries, key_gradient, value_gradient)
```

```python
import functools
import math

import jax
import jax.numpy as jnp
from jax import lax
from jax.experimental import pallas as pl
from jax.experimental.pallas import tpu as pltpu
from jax.sharding import PartitionSpec as P

HEAD_SIZE = 128
WINDOW = 8
SCORE_SCALE = 1.0 / math.sqrt(HEAD_SIZE)
LOG2E = math.log2(math.e)
MASKED = -1e30

NT = (((1,), (1,)), ((), ()))
NN = (((1,), (0,)), ((), ()))


def dot(a, b, dims=NN):
    return lax.dot_general(a, b, dims, preferred_element_type=jnp.float32)


def attend_window(slots, heads, info, q_ref, g_ref, kv_ref, low_ref, out_ref, dq_ref, dkv_ref, scratch):
    k_win, v_win, bias, dk_acc, dv_acc = scratch
    rows = q_ref.shape[0]
    keys = slots * rows
    own = info[0]
    for slot in range(slots):
        shard = jnp.maximum(own - (slots - 1) + slot, 0)
        pair = kv_ref[shard]
        k_win[pl.ds(slot * rows, rows), :] = pair[:, :HEAD_SIZE]
        v_win[pl.ds(slot * rows, rows), :HEAD_SIZE] = pair[:, HEAD_SIZE:]
    v_win[pl.ds(0, keys), HEAD_SIZE:] = jnp.ones((keys, HEAD_SIZE), jnp.bfloat16)

    first = own * rows
    query_pos = first + lax.broadcasted_iota(jnp.int32, (rows, HEAD_SIZE), 0)
    low = low_ref[...]
    for block in range(keys // HEAD_SIZE):
        key_pos = (
            first + rows - keys + block * HEAD_SIZE
            + lax.broadcasted_iota(jnp.int32, (rows, HEAD_SIZE), 1)
        )
        allowed = (key_pos >= low) & (key_pos <= query_pos)
        bias[:, pl.ds(block * HEAD_SIZE, HEAD_SIZE)] = jnp.where(allowed, 0.0, MASKED)
    dk_acc[:, pl.ds(0, keys)] = jnp.zeros((HEAD_SIZE, keys), jnp.float32)
    dv_acc[:, pl.ds(0, keys)] = jnp.zeros((HEAD_SIZE, keys), jnp.float32)

    def one_head(head, carry):
        column = pl.multiple_of(head * HEAD_SIZE, HEAD_SIZE)
        query = q_ref[:, pl.ds(column, HEAD_SIZE)]
        grad = g_ref[:, pl.ds(column, HEAD_SIZE)].astype(jnp.float32)
        key_block = k_win[pl.ds(0, keys), :]
        value_block = v_win[pl.ds(0, keys), :]
        scores = dot(query, key_block, NT) * (SCORE_SCALE * LOG2E) + bias[:, pl.ds(0, keys)]
        top = jnp.max(scores, axis=1, keepdims=True)
        weights = jnp.exp2(scores - top).astype(jnp.bfloat16)
        summed = dot(weights, value_block)
        inverse = 1.0 / summed[:, HEAD_SIZE:]
        output = (summed[:, :HEAD_SIZE] * inverse).astype(jnp.bfloat16)
        out_ref[:, pl.ds(column, HEAD_SIZE)] = output
        scaled = (grad * inverse).astype(jnp.bfloat16)
        delta = jnp.sum(output.astype(jnp.float32) * scaled.astype(jnp.float32), axis=1, keepdims=True)
        grad_weights = dot(scaled, value_block[:, :HEAD_SIZE], NT)
        grad_scores = (weights.astype(jnp.float32) * (grad_weights - delta)).astype(jnp.bfloat16)
        dq_ref[:, pl.ds(column, HEAD_SIZE)] = (dot(grad_scores, key_block) * SCORE_SCALE).astype(jnp.bfloat16)
        dk_acc[:, pl.ds(0, keys)] += dot(query.T, grad_scores)
        dv_acc[:, pl.ds(0, keys)] += dot(scaled.T, weights)
        return carry

    lax.fori_loop(0, heads, one_head, 0)

    dkv_ref[...] = jnp.zeros_like(dkv_ref)
    for slot in range(slots):
        shard = own - (slots - 1) + slot
        span = pl.ds(slot * rows, rows)

        @pl.when(shard >= 0)
        def _():
            dkv_ref[shard, :, :HEAD_SIZE] = (dk_acc[:, span] * SCORE_SCALE).T.astype(jnp.bfloat16)
            dkv_ref[shard, :, HEAD_SIZE:] = dv_acc[:, span].T.astype(jnp.bfloat16)


def group_kernel(heads, aliased, info, q_ref, g_ref, kv_ref, low_ref, *rest):
    out_ref, dq_ref, dkv_ref, *scratch = rest[aliased:]
    needed = info[1]
    sizes = (2, 4, WINDOW)
    for place, slots in enumerate(sizes):
        least = sizes[place - 1] if place else 0

        @pl.when((needed > least) & (needed <= slots))
        def _(slots=slots):
            attend_window(
                slots, heads, info, q_ref, g_ref, kv_ref, low_ref, out_ref, dq_ref, dkv_ref, scratch
            )


def attend_group(group, groups, info, queries, gradient, kv_all, low, buffers):
    rows, width = queries.shape
    columns = width // groups
    heads = columns // HEAD_SIZE
    keys = WINDOW * rows
    whole = lambda shape: pl.BlockSpec(shape, lambda i, info: (0,) * len(shape))
    block = pl.BlockSpec((rows, columns), lambda i, info: (0, group))
    aliased = len(buffers)
    flops = 6 * 2 * heads * rows * keys * HEAD_SIZE
    return pl.pallas_call(
        functools.partial(group_kernel, heads, aliased),
        grid_spec=pltpu.PrefetchScalarGridSpec(
            num_scalar_prefetch=1,
            grid=(1,),
            in_specs=[block, block, whole(kv_all.shape), whole(low.shape)]
            + [pl.BlockSpec(memory_space=pl.ANY)] * aliased,
            out_specs=[block, block, whole(kv_all.shape)],
            scratch_shapes=[
                pltpu.VMEM((keys, HEAD_SIZE), jnp.bfloat16),
                pltpu.VMEM((keys, 2 * HEAD_SIZE), jnp.bfloat16),
                pltpu.VMEM((rows, keys), jnp.float32),
                pltpu.VMEM((HEAD_SIZE, keys), jnp.float32),
                pltpu.VMEM((HEAD_SIZE, keys), jnp.float32),
            ],
        ),
        out_shape=[
            jax.ShapeDtypeStruct(queries.shape, jnp.bfloat16),
            jax.ShapeDtypeStruct(queries.shape, jnp.bfloat16),
            jax.ShapeDtypeStruct(kv_all.shape, jnp.bfloat16),
        ],
        input_output_aliases={5 + place: place for place in range(aliased)},
        compiler_params=pltpu.CompilerParams(vmem_limit_bytes=56 * 1024 * 1024),
        cost_estimate=pl.CostEstimate(
            flops=flops, bytes_accessed=4 * rows * columns * 2 + 4 * kv_all.size, transcendentals=heads * rows * keys
        ),
        name=f"attend_group_{group}",
    )(info, queries, gradient, kv_all, low, *buffers)


def body(queries, key_vectors, value_vectors, output_gradient, doc_lengths):
    own = lax.axis_index("ctx")
    rows = queries.shape[0]
    local = key_vectors.shape[0]
    all_groups = key_vectors.shape[1] // HEAD_SIZE
    pairs = jnp.concatenate(
        [
            key_vectors.reshape(local, all_groups, HEAD_SIZE),
            value_vectors.reshape(local, all_groups, HEAD_SIZE),
        ],
        axis=2,
    )
    pairs = lax.all_to_all(pairs, "tp", split_axis=1, concat_axis=0, tiled=True)
    groups = pairs.shape[1]

    doc_starts = jnp.cumsum(doc_lengths, dtype=jnp.int32) - doc_lengths
    first = own * rows
    query_pos = first + jnp.arange(rows, dtype=jnp.int32)
    low = jnp.max(jnp.where(doc_starts[None, :] <= query_pos[:, None], doc_starts[None, :], 0), axis=1)
    needed = jnp.clip(own - low[0] // rows + 1, 1, WINDOW)
    info = jnp.stack([own, needed]).astype(jnp.int32)
    low = jnp.broadcast_to(low[:, None], (rows, HEAD_SIZE))

    gathered = [lax.all_gather(pairs[:, group], "ctx", axis=0) for group in range(groups)]
    buffers = ()
    owned = []
    for group in range(groups):
        *buffers, partial_grads = attend_group(
            group, groups, info, queries, output_gradient, gathered[group], low, buffers
        )
        owned.append(lax.psum_scatter(partial_grads, "ctx", scatter_dimension=0, tiled=False))
    out, dq = buffers
    grads = jnp.stack(owned, axis=1)
    grads = lax.all_to_all(grads, "tp", split_axis=0, concat_axis=1, tiled=True)
    dk = grads[:, :, :HEAD_SIZE].reshape(local, all_groups * HEAD_SIZE)
    dv = grads[:, :, HEAD_SIZE:].reshape(local, all_groups * HEAD_SIZE)
    return out, dq, dk, dv


def solution(mesh):
    tokens = P(("ctx", "tp"), None)
    heads = P("ctx", "tp")
    return jax.shard_map(
        body,
        mesh=mesh,
        in_specs=(heads, tokens, tokens, heads, P()),
        out_specs=(heads, heads, tokens, tokens),
        check_vma=False,
    )
```

```python
import functools
import math

import jax
import jax.numpy as jnp
from jax import lax
from jax.experimental import pallas as pl
from jax.experimental.pallas import tpu as pltpu
from jax.sharding import PartitionSpec as P

HEAD_SIZE = 128
WINDOW = 8
CHUNKS = 2
SCORE_SCALE = 1.0 / math.sqrt(HEAD_SIZE)
LOG2E = math.log2(math.e)
MASKED = -1e30

NT = (((1,), (1,)), ((), ()))
NN = (((1,), (0,)), ((), ()))


def dot(a, b, dims=NN):
    return lax.dot_general(a, b, dims, preferred_element_type=jnp.float32)


def attend_window(slots, heads, own, q_ref, g_ref, window_refs, low_ref, out_ref, dq_ref, even_ref, odd_ref, scratch):
    k_win, v_win, bias, dk_acc, dv_acc = scratch
    rows = q_ref.shape[0]
    keys = slots * rows
    for slot in range(slots):
        pair = window_refs[slots - 1 - slot][...]
        k_win[pl.ds(slot * rows, rows), :] = pair[:, :HEAD_SIZE]
        v_win[pl.ds(slot * rows, rows), :HEAD_SIZE] = pair[:, HEAD_SIZE:]
    v_win[pl.ds(0, keys), HEAD_SIZE:] = jnp.ones((keys, HEAD_SIZE), jnp.bfloat16)

    first = own * rows
    query_pos = first + lax.broadcasted_iota(jnp.int32, (rows, HEAD_SIZE), 0)
    low = low_ref[...]
    for block in range(keys // HEAD_SIZE):
        key_pos = (
            first + rows - keys + block * HEAD_SIZE
            + lax.broadcasted_iota(jnp.int32, (rows, HEAD_SIZE), 1)
        )
        allowed = (key_pos >= low) & (key_pos <= query_pos)
        bias[:, pl.ds(block * HEAD_SIZE, HEAD_SIZE)] = jnp.where(allowed, 0.0, MASKED)
    dk_acc[:, pl.ds(0, keys)] = jnp.zeros((HEAD_SIZE, keys), jnp.float32)
    dv_acc[:, pl.ds(0, keys)] = jnp.zeros((HEAD_SIZE, keys), jnp.float32)

    def one_head(head, carry):
        column = pl.multiple_of(head * HEAD_SIZE, HEAD_SIZE)
        query = q_ref[:, pl.ds(column, HEAD_SIZE)]
        grad = g_ref[:, pl.ds(column, HEAD_SIZE)].astype(jnp.float32)
        key_block = k_win[pl.ds(0, keys), :]
        value_block = v_win[pl.ds(0, keys), :]
        scores = dot(query, key_block, NT) * (SCORE_SCALE * LOG2E) + bias[:, pl.ds(0, keys)]
        top = jnp.max(scores, axis=1, keepdims=True)
        weights = jnp.exp2(scores - top).astype(jnp.bfloat16)
        summed = dot(weights, value_block)
        inverse = 1.0 / summed[:, HEAD_SIZE:]
        output = (summed[:, :HEAD_SIZE] * inverse).astype(jnp.bfloat16)
        out_ref[:, pl.ds(column, HEAD_SIZE)] = output
        scaled = (grad * inverse).astype(jnp.bfloat16)
        delta = jnp.sum(output.astype(jnp.float32) * scaled.astype(jnp.float32), axis=1, keepdims=True)
        grad_weights = dot(scaled, value_block[:, :HEAD_SIZE], NT)
        grad_scores = (weights.astype(jnp.float32) * (grad_weights - delta)).astype(jnp.bfloat16)
        dq_ref[:, pl.ds(column, HEAD_SIZE)] = (dot(grad_scores, key_block) * SCORE_SCALE).astype(jnp.bfloat16)
        dk_acc[:, pl.ds(0, keys)] += dot(query.T, grad_scores)
        dv_acc[:, pl.ds(0, keys)] += dot(scaled.T, weights)
        return carry

    lax.fori_loop(0, heads, one_head, 0)

    for offset in range(WINDOW):
        target = (odd_ref if offset % 2 else even_ref).at[offset // 2]
        if offset < slots:
            span = pl.ds((slots - 1 - offset) * rows, rows)
            target[:, :HEAD_SIZE] = (dk_acc[:, span] * SCORE_SCALE).T.astype(jnp.bfloat16)
            target[:, HEAD_SIZE:] = dv_acc[:, span].T.astype(jnp.bfloat16)
        else:
            target[...] = jnp.zeros(target.shape, jnp.bfloat16)


def group_kernel(heads, aliased, info, q_ref, g_ref, own_ref, far_ref, x_ref, c_ref, low_ref, *rest):
    out_ref, dq_ref, even_ref, odd_ref, *scratch = rest[aliased:]
    needed = info[1]
    window_refs = [
        own_ref, c_ref.at[0], x_ref.at[0], c_ref.at[1], far_ref, c_ref.at[2], x_ref.at[1], c_ref.at[3]
    ]
    sizes = (2, 4, WINDOW)
    for place, slots in enumerate(sizes):
        least = sizes[place - 1] if place else 0

        @pl.when((needed > least) & (needed <= slots))
        def _(slots=slots):
            attend_window(
                slots, heads, info[0], q_ref, g_ref, window_refs, low_ref,
                out_ref, dq_ref, even_ref, odd_ref, scratch,
            )


def attend_groups(first_group, count, groups, info, queries, gradient, window, low, buffers):
    rows, width = queries.shape
    columns = width // groups
    heads = columns // HEAD_SIZE
    keys = WINDOW * rows
    pair = 2 * HEAD_SIZE
    block = pl.BlockSpec((rows, columns), lambda i, info: (0, first_group + i))
    shard = pl.BlockSpec((rows, pair), lambda i, info: (0, i))
    several = lambda number: pl.BlockSpec((number, rows, pair), lambda i, info: (0, 0, i))
    half = WINDOW // 2
    aliased = len(buffers)
    flops = 6 * 2 * heads * rows * keys * HEAD_SIZE * count
    grads = jax.ShapeDtypeStruct((half, rows, pair * count), jnp.bfloat16)
    return pl.pallas_call(
        functools.partial(group_kernel, heads, aliased),
        grid_spec=pltpu.PrefetchScalarGridSpec(
            num_scalar_prefetch=1,
            grid=(count,),
            in_specs=[block, block, shard, shard, several(half // 2), several(half)]
            + [pl.BlockSpec(low.shape, lambda i, info: (0, 0))]
            + [pl.BlockSpec(memory_space=pl.ANY)] * aliased,
            out_specs=[block, block, several(half), several(half)],
            scratch_shapes=[
                pltpu.VMEM((keys, HEAD_SIZE), jnp.bfloat16),
                pltpu.VMEM((keys, pair), jnp.bfloat16),
                pltpu.VMEM((rows, keys), jnp.float32),
                pltpu.VMEM((HEAD_SIZE, keys), jnp.float32),
                pltpu.VMEM((HEAD_SIZE, keys), jnp.float32),
            ],
        ),
        out_shape=[
            jax.ShapeDtypeStruct(queries.shape, jnp.bfloat16),
            jax.ShapeDtypeStruct(queries.shape, jnp.bfloat16),
            grads,
            grads,
        ],
        input_output_aliases={8 + place: place for place in range(aliased)},
        compiler_params=pltpu.CompilerParams(vmem_limit_bytes=56 * 1024 * 1024),
        cost_estimate=pl.CostEstimate(
            flops=flops,
            bytes_accessed=count * (8 * rows * columns + 8 * keys * HEAD_SIZE),
            transcendentals=count * heads * rows * keys,
        ),
        name=f"attend_groups_{first_group}",
    )(info, queries, gradient, *window, low, *buffers)


def shifted(value, steps):
    count = lax.axis_size("ctx")
    sources = range(max(0, -steps), min(count, count - steps))
    return lax.ppermute(value, "ctx", [(source, source + steps) for source in sources])


def swapped(value, bit):
    return lax.ppermute(value, "ctx", [(place, place ^ bit) for place in range(lax.axis_size("ctx"))])


def tp_exchange(block_for):
    count = lax.axis_size("tp")
    own = lax.axis_index("tp")
    received = [block_for(own)]
    for step in range(1, count):
        sent = block_for(lax.rem(own + step, count))
        received.append(lax.ppermute(sent, "tp", [(place, (place + step) % count) for place in range(count)]))
    return [
        functools.reduce(
            lambda rest, step: jnp.where(lax.rem(own - step + count, count) == place, received[step], rest),
            range(1, count),
            received[0],
        )
        for place in range(count)
    ]


def gather_window(own_pair, own):
    far = shifted(own_pair, WINDOW // 2)
    beyond = shifted(far, WINDOW // 2)
    low_x = (own // 2) % 2 == 0
    low_c = own % 2 == 0
    x_sent = jnp.stack([jnp.where(low_x, own_pair, far), jnp.where(low_x, far, beyond)])
    x_pairs = swapped(x_sent, 2)
    evens = [own_pair, x_pairs[0], far, x_pairs[1], beyond]
    c_sent = jnp.stack([jnp.where(low_c, evens[place], evens[place + 1]) for place in range(WINDOW // 2)])
    c_pairs = swapped(c_sent, 1)
    return own_pair, far, x_pairs, c_pairs


def reduce_window(even, odd, own):
    wide = lambda part: part.astype(jnp.float32)
    low_x = (own // 2) % 2 == 0
    low_c = own % 2 == 0
    got = wide(swapped(odd, 1))
    even = wide(even)
    nothing = jnp.zeros_like(got[0])
    sums = [even[0] + jnp.where(low_c, got[0], nothing)]
    for place in range(1, WINDOW // 2):
        sums.append(even[place] + jnp.where(low_c, got[place], got[place - 1]))
    sums.append(jnp.where(low_c, nothing, got[WINDOW // 2 - 1]))
    got = wide(swapped(jnp.stack([sums[1], sums[3]]).astype(jnp.bfloat16), 2))
    near = sums[0] + jnp.where(low_x, got[0], nothing)
    far = sums[2] + jnp.where(low_x, got[1], got[0])
    beyond = sums[4] + jnp.where(low_x, nothing, got[1])
    far = far + wide(shifted(beyond.astype(jnp.bfloat16), -(WINDOW // 2)))
    near = near + wide(shifted(far.astype(jnp.bfloat16), -(WINDOW // 2)))
    return near.astype(jnp.bfloat16)


def body(queries, key_vectors, value_vectors, output_gradient, doc_lengths):
    own = lax.axis_index("ctx")
    rows = queries.shape[0]
    local = key_vectors.shape[0]
    all_groups = key_vectors.shape[1] // HEAD_SIZE
    groups = all_groups // lax.axis_size("tp")
    pair = 2 * HEAD_SIZE
    columns = groups * HEAD_SIZE

    def pairs_for(place):
        keys = lax.dynamic_slice_in_dim(key_vectors, place * columns, columns, 1)
        values = lax.dynamic_slice_in_dim(value_vectors, place * columns, columns, 1)
        joined = [
            part[:, group * HEAD_SIZE : (group + 1) * HEAD_SIZE] for group in range(groups) for part in (keys, values)
        ]
        return jnp.concatenate(joined, axis=1)

    pairs = jnp.concatenate(tp_exchange(pairs_for), axis=0)

    doc_starts = jnp.cumsum(doc_lengths, dtype=jnp.int32) - doc_lengths
    query_pos = own * rows + jnp.arange(rows, dtype=jnp.int32)
    low = jnp.max(jnp.where(doc_starts[None, :] <= query_pos[:, None], doc_starts[None, :], 0), axis=1)
    needed = jnp.clip(own - low[0] // rows + 1, 1, WINDOW)
    info = jnp.stack([own, needed]).astype(jnp.int32)
    low = jnp.broadcast_to(low[:, None], (rows, HEAD_SIZE))

    count = max(1, groups // CHUNKS)
    starts = range(0, groups, count)
    windows = [gather_window(pairs[:, start * pair : (start + count) * pair], own) for start in starts]
    buffers = ()
    sums = []
    for start, window in zip(starts, windows):
        *buffers, even, odd = attend_groups(
            start, count, groups, info, queries, output_gradient, window, low, buffers
        )
        total = reduce_window(even, odd, own)
        sums.append(
            tp_exchange(lambda place: lax.dynamic_slice_in_dim(total, place * local, local, 0))
        )
    out, dq = buffers

    def output(first):
        parts = [
            sums[group // count][place][:, (group % count) * pair + first :][:, :HEAD_SIZE]
            for place in range(lax.axis_size("tp"))
            for group in range(groups)
        ]
        return jnp.concatenate(parts, axis=1)

    return out, dq, output(0), output(HEAD_SIZE)


def solution(mesh):
    tokens = P(("ctx", "tp"), None)
    heads = P("ctx", "tp")
    return jax.shard_map(
        body,
        mesh=mesh,
        in_specs=(heads, tokens, tokens, heads, P()),
        out_specs=(heads, heads, tokens, tokens),
        check_vma=False,
    )
```

```python
import functools
import math

import jax
import jax.numpy as jnp
from jax import lax
from jax.experimental import pallas as pl
from jax.experimental.pallas import tpu as pltpu
from jax.sharding import PartitionSpec as P

HEAD_SIZE = 128
WINDOW = 8
SCORE_SCALE = 1.0 / math.sqrt(HEAD_SIZE)
LOG2E = math.log2(math.e)
MASKED = -1e30

NT = (((1,), (1,)), ((), ()))
NN = (((1,), (0,)), ((), ()))


def dot(a, b, dims=NN):
    return lax.dot_general(a, b, dims, preferred_element_type=jnp.float32)


def attend_window(slots, heads, own, q_ref, g_ref, window_refs, low_ref, out_ref, dq_ref, even_ref, odd_ref, scratch):
    k_win, v_win, bias, dk_acc, dv_acc = scratch
    rows = q_ref.shape[0]
    keys = slots * rows
    for slot in range(slots):
        source = window_refs[slots - 1 - slot]
        k_win[pl.ds(slot * rows, rows), :] = source[0]
        v_win[pl.ds(slot * rows, rows), :HEAD_SIZE] = source[1]
    v_win[pl.ds(0, keys), HEAD_SIZE:] = jnp.ones((keys, HEAD_SIZE), jnp.bfloat16)

    first = own * rows
    query_pos = first + lax.broadcasted_iota(jnp.int32, (rows, HEAD_SIZE), 0)
    low = low_ref[...]
    for block in range(keys // HEAD_SIZE):
        key_pos = (
            first + rows - keys + block * HEAD_SIZE
            + lax.broadcasted_iota(jnp.int32, (rows, HEAD_SIZE), 1)
        )
        allowed = (key_pos >= low) & (key_pos <= query_pos)
        bias[:, pl.ds(block * HEAD_SIZE, HEAD_SIZE)] = jnp.where(allowed, 0.0, MASKED)
    dk_acc[:, pl.ds(0, keys)] = jnp.zeros((HEAD_SIZE, keys), jnp.float32)
    dv_acc[:, pl.ds(0, keys)] = jnp.zeros((HEAD_SIZE, keys), jnp.float32)

    def one_head(head, carry):
        column = pl.multiple_of(head * HEAD_SIZE, HEAD_SIZE)
        query = q_ref[:, pl.ds(column, HEAD_SIZE)]
        grad = g_ref[:, pl.ds(column, HEAD_SIZE)].astype(jnp.float32)
        key_block = k_win[pl.ds(0, keys), :]
        value_block = v_win[pl.ds(0, keys), :]
        scores = dot(query, key_block, NT) * (SCORE_SCALE * LOG2E) + bias[:, pl.ds(0, keys)]
        top = jnp.max(scores, axis=1, keepdims=True)
        weights = jnp.exp2(scores - top).astype(jnp.bfloat16)
        summed = dot(weights, value_block)
        inverse = 1.0 / summed[:, HEAD_SIZE:]
        output = (summed[:, :HEAD_SIZE] * inverse).astype(jnp.bfloat16)
        out_ref[:, pl.ds(column, HEAD_SIZE)] = output
        scaled = (grad * inverse).astype(jnp.bfloat16)
        delta = jnp.sum(output.astype(jnp.float32) * scaled.astype(jnp.float32), axis=1, keepdims=True)
        grad_weights = dot(scaled, value_block[:, :HEAD_SIZE], NT)
        grad_scores = (weights.astype(jnp.float32) * (grad_weights - delta)).astype(jnp.bfloat16)
        dq_ref[:, pl.ds(column, HEAD_SIZE)] = (dot(grad_scores, key_block) * SCORE_SCALE).astype(jnp.bfloat16)
        dk_acc[:, pl.ds(0, keys)] += dot(query.T, grad_scores)
        dv_acc[:, pl.ds(0, keys)] += dot(scaled.T, weights)
        return carry

    lax.fori_loop(0, heads, one_head, 0, unroll=2)

    for offset in range(WINDOW):
        target = (odd_ref if offset % 2 else even_ref).at[offset // 2]
        if offset < slots:
            span = pl.ds((slots - 1 - offset) * rows, rows)
            target[0] = (dk_acc[:, span] * SCORE_SCALE).T.astype(jnp.bfloat16)
            target[1] = dv_acc[:, span].T.astype(jnp.bfloat16)
        else:
            target[...] = jnp.zeros(target.shape, jnp.bfloat16)


def group_kernel(heads, unread, info, q_ref, g_ref, own_ref, far_ref, x_ref, c_ref, low_ref, *rest):
    out_ref, dq_ref, even_ref, odd_ref, *scratch = rest[unread:]
    needed = info[1]
    window_refs = [
        own_ref, c_ref.at[0], x_ref.at[0], c_ref.at[1], far_ref, c_ref.at[2], x_ref.at[1], c_ref.at[3]
    ]
    sizes = (2, 4, WINDOW)
    for place, slots in enumerate(sizes):
        least = sizes[place - 1] if place else 0

        @pl.when((needed > least) & (needed <= slots))
        def _(slots=slots):
            attend_window(
                slots, heads, info[0], q_ref, g_ref, window_refs, low_ref,
                out_ref, dq_ref, even_ref, odd_ref, scratch,
            )


def attend_group(group, groups, info, queries, gradient, window, place, low, buffers, before):
    rows, width = queries.shape
    columns = width // groups
    heads = columns // HEAD_SIZE
    keys = WINDOW * rows
    half = WINDOW // 2
    block = pl.BlockSpec((rows, columns), lambda i, info: (0, group))
    shard = pl.BlockSpec((2, rows, HEAD_SIZE), lambda i, info: (0, 0, place))
    several = lambda number, column: pl.BlockSpec(
        (number, 2, rows, HEAD_SIZE), lambda i, info: (0, 0, 0, column)
    )
    grads = jax.ShapeDtypeStruct((half, 2, rows, HEAD_SIZE), jnp.bfloat16)
    unread = len(buffers) + len(before)
    return pl.pallas_call(
        functools.partial(group_kernel, heads, unread),
        grid_spec=pltpu.PrefetchScalarGridSpec(
            num_scalar_prefetch=1,
            grid=(1,),
            in_specs=[block, block, shard, shard, several(half // 2, place), several(half, place)]
            + [pl.BlockSpec(low.shape, lambda i, info: (0, 0))]
            + [pl.BlockSpec(memory_space=pl.ANY)] * unread,
            out_specs=[block, block, several(half, 0), several(half, 0)],
            scratch_shapes=[
                pltpu.VMEM((keys, HEAD_SIZE), jnp.bfloat16),
                pltpu.VMEM((keys, 2 * HEAD_SIZE), jnp.bfloat16),
                pltpu.VMEM((rows, keys), jnp.float32),
                pltpu.VMEM((HEAD_SIZE, keys), jnp.float32),
                pltpu.VMEM((HEAD_SIZE, keys), jnp.float32),
            ],
        ),
        out_shape=[
            jax.ShapeDtypeStruct(queries.shape, jnp.bfloat16),
            jax.ShapeDtypeStruct(queries.shape, jnp.bfloat16),
            grads,
            grads,
        ],
        input_output_aliases={8 + number: number for number in range(len(buffers))},
        compiler_params=pltpu.CompilerParams(vmem_limit_bytes=56 * 1024 * 1024),
        cost_estimate=pl.CostEstimate(
            flops=6 * 2 * heads * rows * keys * HEAD_SIZE,
            bytes_accessed=8 * rows * columns + 8 * keys * HEAD_SIZE,
            transcendentals=heads * rows * keys,
        ),
        name=f"attend_group_{group}",
    )(info, queries, gradient, *window, low, *buffers, *before)


def shifted(value, steps):
    count = lax.axis_size("ctx")
    sources = range(max(0, -steps), min(count, count - steps))
    return lax.ppermute(value, "ctx", [(source, source + steps) for source in sources])


def swapped(value, bit):
    return lax.ppermute(value, "ctx", [(place, place ^ bit) for place in range(lax.axis_size("ctx"))])


def tp_received(block_for):
    count = lax.axis_size("tp")
    own = lax.axis_index("tp")
    received = []
    for step in range(1, count):
        sent = block_for(lax.rem(own + step, count), step)
        received.append(lax.ppermute(sent, "tp", [(place, (place + step) % count) for place in range(count)]))
    return received


def in_tp_order(mine, received):
    count = lax.axis_size("tp")
    own = lax.axis_index("tp")
    parts = [mine, *received]
    ordered = []
    for place in range(count):
        part = parts[0]
        for step in range(1, count):
            part = jnp.where(lax.rem(own - step + count, count) == place, parts[step], part)
        ordered.append(part)
    return ordered


def pack_kernel(count, bounds, own, *refs):
    keys, values = refs[: count - 1], refs[count - 1 : 2 * count - 2]
    outs = iter(refs[2 * count - 2 :])
    for first, last in bounds:
        columns = slice(first * HEAD_SIZE, last * HEAD_SIZE)
        for key, value in zip(keys, values):
            out = next(outs)
            out[0] = key[:, columns]
            out[1] = value[:, columns]


def pack_for_tp(key_vectors, value_vectors, groups, bounds, own):
    count = lax.axis_size("tp")
    local = key_vectors.shape[0]
    blocks = [
        pl.BlockSpec((local, groups * HEAD_SIZE), lambda i, own, step=step: (0, lax.rem(own[0] + step, count)))
        for step in range(1, count)
    ]
    shapes = [(2, local, (last - first) * HEAD_SIZE) for first, last in bounds for _ in range(1, count)]
    packed = pl.pallas_call(
        functools.partial(pack_kernel, count, bounds),
        grid_spec=pltpu.PrefetchScalarGridSpec(
            num_scalar_prefetch=1,
            grid=(1,),
            in_specs=blocks + blocks,
            out_specs=[pl.BlockSpec(shape, lambda i, own: (0, 0, 0)) for shape in shapes],
        ),
        out_shape=[jax.ShapeDtypeStruct(shape, jnp.bfloat16) for shape in shapes],
        name="pack_for_tp",
    )(own, *[key_vectors] * (count - 1), *[value_vectors] * (count - 1))
    return [packed[chunk * (count - 1) : (chunk + 1) * (count - 1)] for chunk in range(len(bounds))]


def join_kernel(count, bound, own, key, value, *refs):
    received, out = refs[:-1], refs[-1]
    local = key.shape[0]
    columns = slice(bound[0] * HEAD_SIZE, bound[1] * HEAD_SIZE)
    here = pl.ds(pl.multiple_of(own[0] * local, local), local)
    out[0, here, :] = key[:, columns]
    out[1, here, :] = value[:, columns]
    for step in range(1, count):
        source = lax.rem(own[0] - step + count, count)
        rows = pl.ds(pl.multiple_of(source * local, local), local)
        out[0, rows, :] = received[step - 1][0]
        out[1, rows, :] = received[step - 1][1]


def join_tokens(key_vectors, value_vectors, received, groups, bound, own):
    count = lax.axis_size("tp")
    local = key_vectors.shape[0]
    block = pl.BlockSpec((local, groups * HEAD_SIZE), lambda i, own: (0, own[0]))
    shape = (2, local * count, (bound[1] - bound[0]) * HEAD_SIZE)
    whole = lambda shape: pl.BlockSpec(shape, lambda i, own: (0, 0, 0))
    return pl.pallas_call(
        functools.partial(join_kernel, count, bound),
        grid_spec=pltpu.PrefetchScalarGridSpec(
            num_scalar_prefetch=1,
            grid=(1,),
            in_specs=[block, block] + [whole(part.shape) for part in received],
            out_specs=whole(shape),
        ),
        out_shape=jax.ShapeDtypeStruct(shape, jnp.bfloat16),
        name=f"join_tokens_{bound[0]}",
    )(own, key_vectors, value_vectors, *received)


def even_window(own_pair, own, direct):
    far = shifted(own_pair, WINDOW // 2)
    beyond = shifted(own_pair, WINDOW) if direct else shifted(far, WINDOW // 2)
    low_x = (own // 2) % 2 == 0
    x_sent = jnp.stack([jnp.where(low_x, own_pair, far), jnp.where(low_x, far, beyond)])
    x_pairs = swapped(x_sent, 2)
    return own_pair, far, beyond, x_pairs, x_sent


def whole_window(evens, low_c):
    own_pair, far, beyond, x_pairs, _ = evens
    evens = [own_pair, x_pairs[0], far, x_pairs[1], beyond]
    c_sent = jnp.stack([jnp.where(low_c, evens[place], evens[place + 1]) for place in range(WINDOW // 2)])
    return own_pair, far, x_pairs, swapped(c_sent, 1)


def wide(part):
    return part.astype(jnp.float32)


def reduce_cores(even, odd, own):
    low_c = own % 2 == 0
    got = wide(swapped(odd, 1))
    even = wide(even)
    nothing = jnp.zeros_like(got[0])
    sums = [even[0] + jnp.where(low_c, got[0], nothing)]
    for place in range(1, WINDOW // 2):
        sums.append(even[place] + jnp.where(low_c, got[place], got[place - 1]))
    sums.append(jnp.where(low_c, nothing, got[WINDOW // 2 - 1]))
    return [part.astype(jnp.bfloat16) for part in sums]


def reduce_rest(sums, x_sent, own):
    low_x = (own // 2) % 2 == 0
    got = wide(swapped(x_sent, 2))
    nothing = jnp.zeros_like(got[0])
    near = wide(sums[0]) + jnp.where(low_x, got[0], nothing)
    far = wide(sums[2]) + jnp.where(low_x, got[1], got[0])
    beyond = wide(sums[4]) + jnp.where(low_x, nothing, got[1])
    far = far + wide(shifted(beyond.astype(jnp.bfloat16), -(WINDOW // 2)))
    near = near + wide(shifted(far.astype(jnp.bfloat16), -(WINDOW // 2)))
    return near.astype(jnp.bfloat16)


def body(queries, key_vectors, value_vectors, output_gradient, doc_lengths):
    own = lax.axis_index("ctx")
    rows = queries.shape[0]
    local = key_vectors.shape[0]
    all_groups = key_vectors.shape[1] // HEAD_SIZE
    tp_count = lax.axis_size("tp")
    groups = all_groups // tp_count
    tp_own = lax.axis_index("tp")
    tp_info = tp_own.reshape(1).astype(jnp.int32)

    doc_starts = jnp.cumsum(doc_lengths, dtype=jnp.int32) - doc_lengths
    query_pos = own * rows + jnp.arange(rows, dtype=jnp.int32)
    low = jnp.max(jnp.where(doc_starts[None, :] <= query_pos[:, None], doc_starts[None, :], 0), axis=1)
    needed = jnp.clip(own - low[0] // rows + 1, 1, WINDOW)
    info = jnp.stack([own, needed]).astype(jnp.int32)
    low = jnp.broadcast_to(low[:, None], (rows, HEAD_SIZE))

    bounds = [(0, 1)] + ([(1, groups)] if groups > 1 else [])
    sent = pack_for_tp(key_vectors, value_vectors, groups, bounds, tp_info)
    evens = []
    for chunk, bound in enumerate(bounds):
        received = tp_received(lambda place, step: sent[chunk][step - 1])
        tokens = join_tokens(key_vectors, value_vectors, received, groups, bound, tp_info)
        evens.append(even_window(tokens, own, chunk == 0))

    low_c = own % 2 == 0
    first_window = whole_window(evens[0], low_c)
    waits = [evens[1][4]] if groups > 1 else []
    results = [attend_group(0, groups, info, queries, output_gradient, first_window, 0, low, (), waits)]
    if groups > 1:
        finite = wide(results[0][2][0, 0, 0, 0]) < jnp.inf
        second_window = whole_window(evens[1], low_c & (finite | (own >= 0)))

    def merged(parts):
        sums = [reduce_cores(results[group][2], results[group][3], own) for group in parts]
        sums = [jnp.stack([sums[place][offset] for place in range(len(parts))]) for offset in range(WINDOW // 2 + 1)]
        return sums, jnp.stack([sums[1], sums[3]])

    last_parts = [[group] for group in range(max(1, groups - 2), groups)]
    parts = [list(range(max(1, groups - 2)))] + last_parts
    totals = []
    for group in range(1, groups):
        waits = []
        if group == groups - 1 and groups > 2:
            early = merged(parts[0])
            waits = [early[1]]
        results.append(
            attend_group(
                group, groups, info, queries, output_gradient, second_window, group - 1, low,
                results[-1][:2], waits,
            )
        )
    for place, part in enumerate(parts):
        sums, x_sent = early if place == 0 and groups > 2 else merged(part)
        totals.append(reduce_rest(sums, x_sent, own))

    ordered = []
    for total in totals:
        def tokens_of(place, step=0, total=total):
            return lax.dynamic_slice_in_dim(total, place * local, local, 2)

        ordered.append(in_tp_order(tokens_of(tp_own), tp_received(tokens_of)))

    def output(which):
        pieces = [
            ordered[place][source][index, which]
            for source in range(tp_count)
            for place, part in enumerate(parts)
            for index in range(len(part))
        ]
        return jnp.concatenate(pieces, axis=1)

    out, dq = results[-1][:2]
    return out, dq, output(0), output(1)


def solution(mesh):
    tokens = P(("ctx", "tp"), None)
    heads = P("ctx", "tp")
    return jax.shard_map(
        body,
        mesh=mesh,
        in_specs=(heads, tokens, tokens, heads, P()),
        out_specs=(heads, heads, tokens, tokens),
        check_vma=False,
    )
```

```python
import functools
import math

import jax
import jax.numpy as jnp
from jax import lax
from jax.experimental import pallas as pl
from jax.experimental.pallas import tpu as pltpu
from jax.sharding import PartitionSpec as P

HEAD_SIZE = 128
WINDOW = 8
SCORE_SCALE = 1.0 / math.sqrt(HEAD_SIZE)
LOG2E = math.log2(math.e)
MASKED = -1e30

NT = (((1,), (1,)), ((), ()))
NN = (((1,), (0,)), ((), ()))


def dot(a, b, dims=NN):
    return lax.dot_general(a, b, dims, preferred_element_type=jnp.float32)


def attend_window(slots, heads, own, q_ref, g_ref, window_refs, low_ref, out_ref, dq_ref, even_ref, odd_ref, scratch):
    k_win, v_win, bias, dk_acc, dv_acc, scores, weights, grads = scratch
    rows = q_ref.shape[0]
    keys = slots * rows
    for slot in range(slots):
        source = window_refs[slots - 1 - slot]
        k_win[pl.ds(slot * rows, rows), :] = source[0]
        v_win[pl.ds(slot * rows, rows), :HEAD_SIZE] = source[1]
    v_win[pl.ds(0, keys), HEAD_SIZE:] = jnp.ones((keys, HEAD_SIZE), jnp.bfloat16)

    first = own * rows
    query_pos = first + lax.broadcasted_iota(jnp.int32, (rows, HEAD_SIZE), 0)
    low = low_ref[...]
    for block in range(keys // HEAD_SIZE):
        key_pos = (
            first + rows - keys + block * HEAD_SIZE
            + lax.broadcasted_iota(jnp.int32, (rows, HEAD_SIZE), 1)
        )
        allowed = (key_pos >= low) & (key_pos <= query_pos)
        bias[:, pl.ds(block * HEAD_SIZE, HEAD_SIZE)] = jnp.where(allowed, 0.0, MASKED)
    dk_acc[:, pl.ds(0, keys)] = jnp.zeros((HEAD_SIZE, keys), jnp.float32)
    dv_acc[:, pl.ds(0, keys)] = jnp.zeros((HEAD_SIZE, keys), jnp.float32)

    blocks = [pl.ds(place * rows, rows) for place in range(slots)]

    def one_pair(step, carry):
        turned_q, turned_g = [], []
        for side in range(2):
            column = pl.multiple_of((step * 2 + side) * HEAD_SIZE, HEAD_SIZE)
            columns = pl.ds(column, HEAD_SIZE)
            here = pl.ds(side * rows, rows)
            query = q_ref[:, columns]
            highest = None
            for block in blocks:
                part = dot(query, k_win[block, :], NT) * (SCORE_SCALE * LOG2E) + bias[:, block]
                scores[here, block] = part
                for lanes in range(0, rows, HEAD_SIZE):
                    piece = part[:, lanes : lanes + HEAD_SIZE]
                    highest = piece if highest is None else jnp.maximum(highest, piece)
            top = jnp.max(highest, axis=1, keepdims=True)
            for block in blocks:
                weights[here, block] = jnp.exp2(scores[here, block] - top).astype(jnp.bfloat16)
            summed = dot(weights[here, pl.ds(0, keys)], v_win[pl.ds(0, keys), :])
            inverse = 1.0 / summed[:, HEAD_SIZE:]
            output = (summed[:, :HEAD_SIZE] * inverse).astype(jnp.bfloat16)
            out_ref[:, columns] = output
            scaled = (g_ref[:, columns].astype(jnp.float32) * inverse).astype(jnp.bfloat16)
            delta = jnp.sum(output.astype(jnp.float32) * scaled.astype(jnp.float32), axis=1, keepdims=True)
            for block in blocks:
                part = dot(scaled, v_win[block, :HEAD_SIZE], NT) - delta
                grads[here, block] = (weights[here, block].astype(jnp.float32) * part).astype(jnp.bfloat16)
            dq = dot(grads[here, pl.ds(0, keys)], k_win[pl.ds(0, keys), :])
            dq_ref[:, columns] = (dq * SCORE_SCALE).astype(jnp.bfloat16)
            turned_q.append(query.T)
            turned_g.append(scaled.T)
        turned_q = jnp.concatenate(turned_q, axis=1)
        turned_g = jnp.concatenate(turned_g, axis=1)
        for block in blocks:
            dk_acc[:, block] += dot(turned_q, grads[:, block])
            dv_acc[:, block] += dot(turned_g, weights[:, block])
        return carry

    lax.fori_loop(0, heads // 2, one_pair, 0)

    for offset in range(WINDOW):
        target = (odd_ref if offset % 2 else even_ref).at[offset // 2]
        if offset < slots:
            span = pl.ds((slots - 1 - offset) * rows, rows)
            target[0] = (dk_acc[:, span] * SCORE_SCALE).T.astype(jnp.bfloat16)
            target[1] = dv_acc[:, span].T.astype(jnp.bfloat16)
        else:
            target[...] = jnp.zeros(target.shape, jnp.bfloat16)


def group_kernel(heads, unread, info, q_ref, g_ref, own_ref, far_ref, x_ref, c_ref, low_ref, *rest):
    out_ref, dq_ref, even_ref, odd_ref, *scratch = rest[unread:]
    needed = info[1]
    window_refs = [
        own_ref, c_ref.at[0], x_ref.at[0], c_ref.at[1], far_ref, c_ref.at[2], x_ref.at[1], c_ref.at[3]
    ]
    sizes = (2, 4, WINDOW)
    for place, slots in enumerate(sizes):
        least = sizes[place - 1] if place else 0

        @pl.when((needed > least) & (needed <= slots))
        def _(slots=slots):
            attend_window(
                slots, heads, info[0], q_ref, g_ref, window_refs, low_ref,
                out_ref, dq_ref, even_ref, odd_ref, scratch,
            )


def attend_group(group, groups, info, queries, gradient, window, place, low, buffers, before):
    rows, width = queries.shape
    columns = width // groups
    heads = columns // HEAD_SIZE
    keys = WINDOW * rows
    half = WINDOW // 2
    block = pl.BlockSpec((rows, columns), lambda i, info: (0, group))
    shard = pl.BlockSpec((2, rows, HEAD_SIZE), lambda i, info: (0, 0, place))
    several = lambda number, column: pl.BlockSpec(
        (number, 2, rows, HEAD_SIZE), lambda i, info: (0, 0, 0, column)
    )
    grads = jax.ShapeDtypeStruct((half, 2, rows, HEAD_SIZE), jnp.bfloat16)
    unread = len(buffers) + len(before)
    return pl.pallas_call(
        functools.partial(group_kernel, heads, unread),
        grid_spec=pltpu.PrefetchScalarGridSpec(
            num_scalar_prefetch=1,
            grid=(1,),
            in_specs=[block, block, shard, shard, several(half // 2, place), several(half, place)]
            + [pl.BlockSpec(low.shape, lambda i, info: (0, 0))]
            + [pl.BlockSpec(memory_space=pl.ANY)] * unread,
            out_specs=[block, block, several(half, 0), several(half, 0)],
            scratch_shapes=[
                pltpu.VMEM((keys, HEAD_SIZE), jnp.bfloat16),
                pltpu.VMEM((keys, 2 * HEAD_SIZE), jnp.bfloat16),
                pltpu.VMEM((rows, keys), jnp.float32),
                pltpu.VMEM((HEAD_SIZE, keys), jnp.float32),
                pltpu.VMEM((HEAD_SIZE, keys), jnp.float32),
                pltpu.VMEM((2 * rows, keys), jnp.float32),
                pltpu.VMEM((2 * rows, keys), jnp.bfloat16),
                pltpu.VMEM((2 * rows, keys), jnp.bfloat16),
            ],
        ),
        out_shape=[
            jax.ShapeDtypeStruct(queries.shape, jnp.bfloat16),
            jax.ShapeDtypeStruct(queries.shape, jnp.bfloat16),
            grads,
            grads,
        ],
        input_output_aliases={8 + number: number for number in range(len(buffers))},
        compiler_params=pltpu.CompilerParams(vmem_limit_bytes=56 * 1024 * 1024),
        cost_estimate=pl.CostEstimate(
            flops=4 * 6 * 2 * heads * rows * keys * HEAD_SIZE,
            bytes_accessed=8 * rows * columns + 8 * keys * HEAD_SIZE,
            transcendentals=heads * rows * keys,
        ),
        name=f"attend_group_{group}",
    )(info, queries, gradient, *window, low, *buffers, *before)


def shifted(value, steps):
    count = lax.axis_size("ctx")
    sources = range(max(0, -steps), min(count, count - steps))
    return lax.ppermute(value, "ctx", [(source, source + steps) for source in sources])


def swapped(value, bit):
    return lax.ppermute(value, "ctx", [(place, place ^ bit) for place in range(lax.axis_size("ctx"))])


def tp_received(block_for):
    count = lax.axis_size("tp")
    own = lax.axis_index("tp")
    received = []
    for step in range(1, count):
        sent = block_for(lax.rem(own + step, count), step)
        received.append(lax.ppermute(sent, "tp", [(place, (place + step) % count) for place in range(count)]))
    return received


def in_tp_order(mine, received):
    count = lax.axis_size("tp")
    own = lax.axis_index("tp")
    parts = [mine, *received]
    ordered = []
    for place in range(count):
        part = parts[0]
        for step in range(1, count):
            part = jnp.where(lax.rem(own - step + count, count) == place, parts[step], part)
        ordered.append(part)
    return ordered


def pack_kernel(count, bound, own, *refs):
    keys, values = refs[: count - 1], refs[count - 1 : 2 * count - 2]
    outs = refs[1 - count :]
    columns = slice(bound[0] * HEAD_SIZE, bound[1] * HEAD_SIZE)
    for key, value, out in zip(keys, values, outs):
        out[0] = key[:, columns]
        out[1] = value[:, columns]


def pack_for_tp(key_vectors, value_vectors, groups, bound, own, before):
    count = lax.axis_size("tp")
    local = key_vectors.shape[0]
    blocks = [
        pl.BlockSpec((local, groups * HEAD_SIZE), lambda i, own, step=step: (0, lax.rem(own[0] + step, count)))
        for step in range(1, count)
    ]
    shape = (2, local, (bound[1] - bound[0]) * HEAD_SIZE)
    return pl.pallas_call(
        functools.partial(pack_kernel, count, bound),
        grid_spec=pltpu.PrefetchScalarGridSpec(
            num_scalar_prefetch=1,
            grid=(1,),
            in_specs=blocks + blocks + [pl.BlockSpec(memory_space=pl.ANY)] * len(before),
            out_specs=[pl.BlockSpec(shape, lambda i, own: (0, 0, 0))] * (count - 1),
        ),
        out_shape=[jax.ShapeDtypeStruct(shape, jnp.bfloat16)] * (count - 1),
        name=f"pack_for_tp_{bound[0]}",
    )(own, *[key_vectors] * (count - 1), *[value_vectors] * (count - 1), *before)


def join_kernel(count, bound, own, key, value, *refs):
    received, out = refs[:-1], refs[-1]
    local = key.shape[0]
    columns = slice(bound[0] * HEAD_SIZE, bound[1] * HEAD_SIZE)
    here = pl.ds(pl.multiple_of(own[0] * local, local), local)
    out[0, here, :] = key[:, columns]
    out[1, here, :] = value[:, columns]
    for step in range(1, count):
        source = lax.rem(own[0] - step + count, count)
        rows = pl.ds(pl.multiple_of(source * local, local), local)
        out[0, rows, :] = received[step - 1][0]
        out[1, rows, :] = received[step - 1][1]


def join_tokens(key_vectors, value_vectors, received, groups, bound, own):
    count = lax.axis_size("tp")
    local = key_vectors.shape[0]
    block = pl.BlockSpec((local, groups * HEAD_SIZE), lambda i, own: (0, own[0]))
    shape = (2, local * count, (bound[1] - bound[0]) * HEAD_SIZE)
    whole = lambda shape: pl.BlockSpec(shape, lambda i, own: (0, 0, 0))
    return pl.pallas_call(
        functools.partial(join_kernel, count, bound),
        grid_spec=pltpu.PrefetchScalarGridSpec(
            num_scalar_prefetch=1,
            grid=(1,),
            in_specs=[block, block] + [whole(part.shape) for part in received],
            out_specs=whole(shape),
        ),
        out_shape=jax.ShapeDtypeStruct(shape, jnp.bfloat16),
        name=f"join_tokens_{bound[0]}",
    )(own, key_vectors, value_vectors, *received)


def even_window(own_pair, own, direct):
    far = shifted(own_pair, WINDOW // 2)
    beyond = shifted(own_pair, WINDOW) if direct else shifted(far, WINDOW // 2)
    low_x = (own // 2) % 2 == 0
    x_sent = jnp.stack([jnp.where(low_x, own_pair, far), jnp.where(low_x, far, beyond)])
    x_pairs = swapped(x_sent, 2)
    return own_pair, far, beyond, x_pairs, x_sent


def whole_window(evens, low_c):
    own_pair, far, beyond, x_pairs, _ = evens
    evens = [own_pair, x_pairs[0], far, x_pairs[1], beyond]
    c_sent = jnp.stack([jnp.where(low_c, evens[place], evens[place + 1]) for place in range(WINDOW // 2)])
    return own_pair, far, x_pairs, swapped(c_sent, 1)


def wide(part):
    return part.astype(jnp.float32)


def done_after(result, own):
    return (wide(result[2][0, 0, 0, 0]) < jnp.inf) | (own >= 0)


def reduce_cores(even, odd, own):
    low_c = own % 2 == 0
    got = wide(swapped(odd, 1))
    even = wide(even)
    nothing = jnp.zeros_like(got[0])
    sums = [even[0] + jnp.where(low_c, got[0], nothing)]
    for place in range(1, WINDOW // 2):
        sums.append(even[place] + jnp.where(low_c, got[place], got[place - 1]))
    sums.append(jnp.where(low_c, nothing, got[WINDOW // 2 - 1]))
    return [part.astype(jnp.bfloat16) for part in sums]


def reduce_rest(sums, x_sent, own):
    low_x = (own // 2) % 2 == 0
    got = wide(swapped(x_sent, 2))
    nothing = jnp.zeros_like(got[0])
    near = wide(sums[0]) + jnp.where(low_x, got[0], nothing)
    far = wide(sums[2]) + jnp.where(low_x, got[1], got[0])
    beyond = wide(sums[4]) + jnp.where(low_x, nothing, got[1])
    near = near + wide(shifted(beyond.astype(jnp.bfloat16), -WINDOW))
    near = near + wide(shifted(far.astype(jnp.bfloat16), -(WINDOW // 2)))
    return near.astype(jnp.bfloat16)


def body(queries, key_vectors, value_vectors, output_gradient, doc_lengths):
    own = lax.axis_index("ctx")
    rows = queries.shape[0]
    local = key_vectors.shape[0]
    all_groups = key_vectors.shape[1] // HEAD_SIZE
    tp_count = lax.axis_size("tp")
    groups = all_groups // tp_count
    tp_own = lax.axis_index("tp")
    tp_info = tp_own.reshape(1).astype(jnp.int32)

    doc_starts = jnp.cumsum(doc_lengths, dtype=jnp.int32) - doc_lengths
    query_pos = own * rows + jnp.arange(rows, dtype=jnp.int32)
    low = jnp.max(jnp.where(doc_starts[None, :] <= query_pos[:, None], doc_starts[None, :], 0), axis=1)
    needed = jnp.clip(own - low[0] // rows + 1, 1, WINDOW)
    info = jnp.stack([own, needed]).astype(jnp.int32)
    low = jnp.broadcast_to(low[:, None], (rows, HEAD_SIZE))

    bounds = [(0, 1)] + ([(1, groups)] if groups > 1 else [])
    evens = []
    received = []
    for chunk, bound in enumerate(bounds):
        sent = pack_for_tp(key_vectors, value_vectors, groups, bound, tp_info, received)
        received = tp_received(lambda place, step: sent[step - 1])
        tokens = join_tokens(key_vectors, value_vectors, received, groups, bound, tp_info)
        evens.append(even_window(tokens, own, chunk == 0))

    low_c = own % 2 == 0
    first_window = whole_window(evens[0], low_c)
    waits = [evens[1][4]] if groups > 1 else []
    results = [attend_group(0, groups, info, queries, output_gradient, first_window, 0, low, (), waits)]
    if groups > 1:
        second_window = whole_window(evens[1], low_c & done_after(results[0], own))

    def merged(parts, after=None):
        sums = [reduce_cores(results[group][2], results[group][3], own) for group in parts]
        if after is not None:
            sums = [[jnp.where(after, part, 0) for part in group_sums] for group_sums in sums]
        sums = [jnp.stack([sums[place][offset] for place in range(len(parts))]) for offset in range(WINDOW // 2 + 1)]
        return sums, jnp.stack([sums[1], sums[3]])

    last_parts = [[group] for group in range(max(1, groups - 2), groups)]
    parts = [list(range(max(1, groups - 2)))] + last_parts
    totals = []
    for group in range(1, groups):
        waits = []
        if group == groups - 1 and groups > 2:
            early = merged(parts[0])
            waits = [early[1]]
        results.append(
            attend_group(
                group, groups, info, queries, output_gradient, second_window, group - 1, low,
                results[-1][:2], waits,
            )
        )
    for place, part in enumerate(parts):
        if place == 0 and groups > 2:
            sums, x_sent = early
        else:
            sums, x_sent = merged(part, done_after(results[-1], own) if part[0] < groups - 1 else None)
        totals.append(reduce_rest(sums, x_sent, own))

    total = jnp.concatenate(totals, axis=0)

    def tokens_of(place, step=0):
        return lax.dynamic_slice_in_dim(total, place * local, local, 2)

    ordered = in_tp_order(tokens_of(tp_own), tp_received(tokens_of))

    def output(which):
        pieces = [ordered[source][group, which] for source in range(tp_count) for group in range(groups)]
        return jnp.concatenate(pieces, axis=1)

    out, dq = results[-1][:2]
    return out, dq, output(0), output(1)


def solution(mesh):
    tokens = P(("ctx", "tp"), None)
    heads = P("ctx", "tp")
    return jax.shard_map(
        body,
        mesh=mesh,
        in_specs=(heads, tokens, tokens, heads, P()),
        out_specs=(heads, heads, tokens, tokens),
        check_vma=False,
    )
```

```python
import functools
import math

import jax
import jax.numpy as jnp
from jax import lax
from jax.experimental import pallas as pl
from jax.experimental.pallas import tpu as pltpu
from jax.sharding import PartitionSpec as P

HEAD_SIZE = 128
WINDOW = 8
SCORE_SCALE = 1.0 / math.sqrt(HEAD_SIZE)
LOG2E = math.log2(math.e)
MASKED = -1e30

NT = (((1,), (1,)), ((), ()))
NN = (((1,), (0,)), ((), ()))


def dot(a, b, dims=NN):
    return lax.dot_general(a, b, dims, preferred_element_type=jnp.float32)


def attend_window(slots, heads, first, doc_lengths, q_ref, g_ref, window_refs, out_ref, dq_ref, even_ref, odd_ref, scratch):
    k_win, v_win, k_turned, v_turned, bias, dk_acc, dv_acc, scores, weights, grads = scratch
    rows = q_ref.shape[0]
    keys = slots * rows
    blocks = [pl.ds(place * rows, rows) for place in range(slots)]
    for slot, block in enumerate(blocks):
        source = window_refs[slots - 1 - slot]
        k_win[block, :] = source[0]
        v_win[block, :HEAD_SIZE] = source[1]
        k_turned[:, block] = source[0].T
        v_turned[:, block] = source[1].T
    v_win[pl.ds(0, keys), HEAD_SIZE:] = jnp.ones((keys, HEAD_SIZE), jnp.bfloat16)

    query_pos = first + lax.broadcasted_iota(jnp.int32, (rows, HEAD_SIZE), 0)
    low = jnp.zeros((rows, HEAD_SIZE), jnp.int32)
    start = 0
    for doc in range(doc_lengths.shape[0]):
        low = jnp.where(query_pos >= start, start, low)
        start = start + doc_lengths[doc]
    for block in range(keys // HEAD_SIZE):
        key_pos = (
            first + rows - keys + block * HEAD_SIZE
            + lax.broadcasted_iota(jnp.int32, (rows, HEAD_SIZE), 1)
        )
        allowed = (key_pos >= low) & (key_pos <= query_pos)
        bias[:, pl.ds(block * HEAD_SIZE, HEAD_SIZE)] = jnp.where(allowed, 0.0, MASKED)
    dk_acc[:, pl.ds(0, keys)] = jnp.zeros((HEAD_SIZE, keys), jnp.float32)
    dv_acc[:, pl.ds(0, keys)] = jnp.zeros((HEAD_SIZE, keys), jnp.float32)
    ones = jnp.ones((2 * HEAD_SIZE, HEAD_SIZE), jnp.bfloat16)

    def one_pair(step, carry):
        turned_q, turned_g = [], []
        for side in range(2):
            column = pl.multiple_of((step * 2 + side) * HEAD_SIZE, HEAD_SIZE)
            columns = pl.ds(column, HEAD_SIZE)
            here = pl.ds(side * rows, rows)
            query = q_ref[:, columns]
            highest = None
            for block in blocks:
                part = dot(query, k_turned[:, block]) * (SCORE_SCALE * LOG2E) + bias[:, block]
                scores[here, block] = part
                for lanes in range(0, rows, HEAD_SIZE):
                    piece = part[:, lanes : lanes + HEAD_SIZE]
                    highest = piece if highest is None else jnp.maximum(highest, piece)
            top = jnp.max(highest, axis=1, keepdims=True)
            for block in blocks:
                weights[here, block] = jnp.exp2(scores[here, block] - top).astype(jnp.bfloat16)
            summed = dot(weights[here, pl.ds(0, keys)], v_win[pl.ds(0, keys), :])
            inverse = 1.0 / summed[:, HEAD_SIZE:]
            output = (summed[:, :HEAD_SIZE] * inverse).astype(jnp.bfloat16)
            out_ref[:, columns] = output
            scaled = (g_ref[:, columns].astype(jnp.float32) * inverse).astype(jnp.bfloat16)
            terms = output.astype(jnp.float32) * scaled.astype(jnp.float32)
            upper = terms.astype(jnp.bfloat16)
            lower = (terms - upper.astype(jnp.float32)).astype(jnp.bfloat16)
            delta = dot(jnp.concatenate([upper, lower], axis=1), ones)
            delta = jnp.concatenate([delta] * (rows // HEAD_SIZE), axis=1)
            for block in blocks:
                part = dot(scaled, v_turned[:, block]) - delta
                grads[here, block] = (weights[here, block].astype(jnp.float32) * part).astype(jnp.bfloat16)
            dq = dot(grads[here, pl.ds(0, keys)], k_win[pl.ds(0, keys), :])
            dq_ref[:, columns] = (dq * SCORE_SCALE).astype(jnp.bfloat16)
            turned_q.append(query.T)
            turned_g.append(scaled.T)
        turned_q = jnp.concatenate(turned_q, axis=1)
        turned_g = jnp.concatenate(turned_g, axis=1)
        for block in blocks:
            dk_acc[:, block] += dot(turned_q, grads[:, block])
            dv_acc[:, block] += dot(turned_g, weights[:, block])
        return carry

    lax.fori_loop(0, heads // 2, one_pair, 0)

    for offset in range(WINDOW):
        target = (odd_ref if offset % 2 else even_ref).at[offset // 2]
        if offset < slots:
            span = blocks[slots - 1 - offset]
            target[0] = (dk_acc[:, span] * SCORE_SCALE).astype(jnp.bfloat16)
            target[1] = dv_acc[:, span].astype(jnp.bfloat16)
        else:
            target[...] = jnp.zeros(target.shape, jnp.bfloat16)


def group_kernel(heads, unread, own, doc_lengths, q_ref, g_ref, own_ref, far_ref, x_ref, c_ref, *rest):
    out_ref, dq_ref, even_ref, odd_ref, *scratch = rest[unread:]
    rows = q_ref.shape[0]
    first = own[0] * rows
    doc_start = 0
    start = 0
    for doc in range(doc_lengths.shape[0]):
        doc_start = jnp.where(first >= start, start, doc_start)
        start = start + doc_lengths[doc]
    needed = jnp.clip(own[0] - doc_start // rows + 1, 1, WINDOW)
    window_refs = [
        own_ref, c_ref.at[0], x_ref.at[0], c_ref.at[1], far_ref, c_ref.at[2], x_ref.at[1], c_ref.at[3]
    ]
    sizes = (2, 4, WINDOW)
    for place, slots in enumerate(sizes):
        least = sizes[place - 1] if place else 0

        @pl.when((needed > least) & (needed <= slots))
        def _(slots=slots):
            attend_window(
                slots, heads, first, doc_lengths, q_ref, g_ref, window_refs,
                out_ref, dq_ref, even_ref, odd_ref, scratch,
            )


def attend_group(group, groups, own, doc_lengths, queries, gradient, window, place, buffers, before):
    rows, width = queries.shape
    columns = width // groups
    heads = columns // HEAD_SIZE
    keys = WINDOW * rows
    half = WINDOW // 2
    block = pl.BlockSpec((rows, columns), lambda i, *_: (0, group))
    shard = pl.BlockSpec((2, rows, HEAD_SIZE), lambda i, *_: (0, 0, place))
    several = lambda number: pl.BlockSpec((number, 2, rows, HEAD_SIZE), lambda i, *_: (0, 0, 0, place))
    grads_block = pl.BlockSpec((half, 2, HEAD_SIZE, rows), lambda i, *_: (0, 0, 0, 0))
    grads = jax.ShapeDtypeStruct((half, 2, HEAD_SIZE, rows), jnp.bfloat16)
    unread = len(buffers) + len(before)
    return pl.pallas_call(
        functools.partial(group_kernel, heads, unread),
        grid_spec=pltpu.PrefetchScalarGridSpec(
            num_scalar_prefetch=2,
            grid=(1,),
            in_specs=[block, block, shard, shard, several(half // 2), several(half)]
            + [pl.BlockSpec(memory_space=pl.ANY)] * unread,
            out_specs=[block, block, grads_block, grads_block],
            scratch_shapes=[
                pltpu.VMEM((keys, HEAD_SIZE), jnp.bfloat16),
                pltpu.VMEM((keys, 2 * HEAD_SIZE), jnp.bfloat16),
                pltpu.VMEM((HEAD_SIZE, keys), jnp.bfloat16),
                pltpu.VMEM((HEAD_SIZE, keys), jnp.bfloat16),
                pltpu.VMEM((rows, keys), jnp.float32),
                pltpu.VMEM((HEAD_SIZE, keys), jnp.float32),
                pltpu.VMEM((HEAD_SIZE, keys), jnp.float32),
                pltpu.VMEM((2 * rows, keys), jnp.float32),
                pltpu.VMEM((2 * rows, keys), jnp.bfloat16),
                pltpu.VMEM((2 * rows, keys), jnp.bfloat16),
            ],
        ),
        out_shape=[
            jax.ShapeDtypeStruct(queries.shape, jnp.bfloat16),
            jax.ShapeDtypeStruct(queries.shape, jnp.bfloat16),
            grads,
            grads,
        ],
        input_output_aliases={8 + number: number for number in range(len(buffers))},
        compiler_params=pltpu.CompilerParams(vmem_limit_bytes=56 * 1024 * 1024),
        cost_estimate=pl.CostEstimate(
            flops=4 * 6 * 2 * heads * rows * keys * HEAD_SIZE,
            bytes_accessed=8 * rows * columns + 8 * keys * HEAD_SIZE,
            transcendentals=heads * rows * keys,
        ),
        name=f"attend_group_{group}",
    )(own, doc_lengths, queries, gradient, *window, *buffers, *before)


def shifted(value, steps):
    count = lax.axis_size("ctx")
    sources = range(max(0, -steps), min(count, count - steps))
    return lax.ppermute(value, "ctx", [(source, source + steps) for source in sources])


def swapped(value, bit):
    return lax.ppermute(value, "ctx", [(place, place ^ bit) for place in range(lax.axis_size("ctx"))])


def tp_received(block_for):
    count = lax.axis_size("tp")
    own = lax.axis_index("tp")
    received = []
    for step in range(1, count):
        sent = block_for(lax.rem(own + step, count), step)
        received.append(lax.ppermute(sent, "tp", [(place, (place + step) % count) for place in range(count)]))
    return received


def in_tp_order(mine, received):
    count = lax.axis_size("tp")
    own = lax.axis_index("tp")
    parts = [mine, *received]
    ordered = []
    for place in range(count):
        part = parts[0]
        for step in range(1, count):
            part = jnp.where(lax.rem(own - step + count, count) == place, parts[step], part)
        ordered.append(part)
    return ordered


def whole_block(shape):
    return pl.BlockSpec(shape, lambda i, *_: (0,) * len(shape))


def small_kernel(kernel, scalars, operands, specs, outs, before, name):
    return pl.pallas_call(
        kernel,
        grid_spec=pltpu.PrefetchScalarGridSpec(
            num_scalar_prefetch=1,
            grid=(1,),
            in_specs=specs + [pl.BlockSpec(memory_space=pl.ANY)] * len(before),
            out_specs=[whole_block(shape) for shape in outs],
        ),
        out_shape=[jax.ShapeDtypeStruct(shape, jnp.bfloat16) for shape in outs],
        compiler_params=pltpu.CompilerParams(vmem_limit_bytes=32 * 1024 * 1024),
        name=name,
    )(scalars, *operands, *before)


def pack_for_tp(key_vectors, value_vectors, groups, tp_own):
    count = lax.axis_size("tp")
    local = key_vectors.shape[0]
    columns = groups * HEAD_SIZE
    blocks = [
        pl.BlockSpec((local, columns), lambda i, own, step=step: (0, lax.rem(own[0] + step, count)))
        for step in range(1, count)
    ]

    def kernel(own, *refs):
        keys, values, outs = refs[: count - 1], refs[count - 1 : 2 * count - 2], refs[1 - count :]
        for key, value, out in zip(keys, values, outs):
            out[0] = key[...]
            out[1] = value[...]

    return small_kernel(
        kernel, tp_own, [key_vectors] * (count - 1) + [value_vectors] * (count - 1), blocks + blocks,
        [(2, local, columns)] * (count - 1), [], "pack_for_tp",
    )


def join_tokens(key_vectors, value_vectors, received, groups, bounds, tp_own):
    count = lax.axis_size("tp")
    local = key_vectors.shape[0]
    block = pl.BlockSpec((local, groups * HEAD_SIZE), lambda i, own: (0, own[0]))

    def kernel(own, key, value, *refs):
        parts, outs = refs[: count - 1], refs[count - 1 :]
        for (first, last), out in zip(bounds, outs):
            columns = slice(first * HEAD_SIZE, last * HEAD_SIZE)
            here = pl.ds(pl.multiple_of(own[0] * local, local), local)
            out[0, here, :] = key[:, columns]
            out[1, here, :] = value[:, columns]
            for step in range(1, count):
                source = lax.rem(own[0] - step + count, count)
                rows = pl.ds(pl.multiple_of(source * local, local), local)
                out[:, rows, :] = parts[step - 1][:, :, columns]

    return small_kernel(
        kernel, tp_own, [key_vectors, value_vectors, *received],
        [block, block] + [whole_block(part.shape) for part in received],
        [(2, local * count, (last - first) * HEAD_SIZE) for first, last in bounds], [], "join_tokens",
    )


def even_window(own_pair, own):
    far = shifted(own_pair, WINDOW // 2)
    beyond = shifted(far, WINDOW // 2)
    low_x = (own // 2) % 2 == 0
    x_sent = jnp.stack([jnp.where(low_x, own_pair, far), jnp.where(low_x, far, beyond)])
    return own_pair, far, beyond, x_sent


def whole_window(evens, own, before, name):
    own_pair, far, beyond, x_sent = evens
    x_pairs = swapped(x_sent, 2)
    half = WINDOW // 2

    def kernel(own, own_ref, far_ref, beyond_ref, x_ref, *refs):
        out = refs[-1]
        evens = [own_ref, x_ref.at[0], far_ref, x_ref.at[1], beyond_ref]
        low_c = lax.rem(own[0], 2)
        for bit in range(2):

            @pl.when(low_c == bit)
            def _(bit=bit):
                for place in range(half):
                    out[place] = evens[place + bit][...]

    operands = [own_pair, far, beyond, x_pairs]
    (c_sent,) = small_kernel(
        kernel, own, operands, [whole_block(part.shape) for part in operands],
        [(half, *own_pair.shape)], before, name,
    )
    return own_pair, far, x_pairs, swapped(c_sent, 1)


def wide(part):
    return part.astype(jnp.float32)


def fold_cores(even, got, own, before, name):
    half = WINDOW // 2

    def kernel(own, even_ref, got_ref, *refs):
        sent, kept = refs[-2:]
        for bit in range(2):

            @pl.when(lax.rem(own[0], 2) == bit)
            def _(bit=bit):
                for place in range(half + 1):
                    out = sent.at[place // 2] if place % 2 else kept.at[place // 2]
                    total = None
                    if place < half:
                        total = wide(even_ref[place])
                    if 0 <= place - bit < half:
                        more = wide(got_ref[place - bit])
                        total = more if total is None else total + more
                    out[...] = jnp.zeros(out.shape, out.dtype) if total is None else total.astype(out.dtype)

    shape = even.shape[1:]
    return small_kernel(
        kernel, own, [even, got], [whole_block(even.shape)] * 2,
        [(half // 2, *shape), (half // 2 + 1, *shape)], before, name,
    )


def fold_x(sent, kept, own, before, name):
    got = swapped(sent, 2)

    def kernel(own, kept_ref, got_ref, *refs):
        near, far, beyond = refs[-3:]
        for bit in range(2):

            @pl.when(lax.rem(own[0] // 2, 2) == bit)
            def _(bit=bit):
                for place, out in enumerate((near, far, beyond)):
                    total = wide(kept_ref[place])
                    if 0 <= place - bit < got_ref.shape[0]:
                        total = total + wide(got_ref[place - bit])
                    out[...] = total.astype(out.dtype)

    return small_kernel(
        kernel, own, [kept, got], [whole_block(kept.shape), whole_block(got.shape)], [kept.shape[1:]] * 3, before, name
    )


def body(queries, key_vectors, value_vectors, output_gradient, doc_lengths):
    own = lax.axis_index("ctx")
    own_info = own.reshape(1).astype(jnp.int32)
    local = key_vectors.shape[0]
    all_groups = key_vectors.shape[1] // HEAD_SIZE
    tp_count = lax.axis_size("tp")
    groups = all_groups // tp_count
    tp_own = lax.axis_index("tp")
    tp_info = tp_own.reshape(1).astype(jnp.int32)

    bounds = [(0, 1)] + ([(1, groups)] if groups > 1 else [])
    packed = pack_for_tp(key_vectors, value_vectors, groups, tp_info)
    received = tp_received(lambda place, step: packed[step - 1])
    chunks = join_tokens(key_vectors, value_vectors, received, groups, bounds, tp_info)
    evens = [even_window(chunk, own) for chunk in chunks]

    windows = [whole_window(evens[0], own_info, [], "core_swap_0")]
    buffers = ()
    results, got, folded, sums = [], [], [], []

    def fold_next_cores(before):
        group = len(folded)
        folded.append(fold_cores(results[group][2], got[group], own_info, before, f"fold_cores_{group}"))

    def fold_next_x(before):
        group = len(sums)
        sums.append(fold_x(*folded[group], own_info, before, f"fold_x_{group}"))

    for group in range(groups):
        waits = [evens[1][3]] if group == 0 and groups > 1 else []
        if group >= 2:
            waits.append(folded[group - 2][0])
        if group >= 3:
            waits.append(sums[group - 3][1])
        chunk = min(group, 1)
        results.append(
            attend_group(
                group, groups, own_info, doc_lengths, queries, output_gradient, windows[chunk], group - chunk,
                buffers, waits,
            )
        )
        *buffers, even, odd = results[-1]
        got.append(swapped(odd, 1))
        if group == 0 and groups > 1:
            windows.append(whole_window(evens[1], own_info, [even], "core_swap_1"))
        if group >= 1:
            fold_next_cores([even])
        if group >= 2 and group < groups - 1:
            fold_next_x([even])
    while len(sums) < groups - 2:
        fold_next_x([got[-1]])
    fold_next_cores([])
    while len(sums) < groups:
        fold_next_x([folded[-1][0]] if len(sums) < groups - 1 else [])

    totals = []
    for near, far, beyond in sums:
        total = wide(near) + wide(shifted(beyond, -WINDOW)) + wide(shifted(far, -(WINDOW // 2)))
        totals.append(jnp.swapaxes(total.astype(jnp.bfloat16), 1, 2))

    def exchanged(total):
        def tokens_of(place, step=0):
            return lax.dynamic_slice_in_dim(total, place * local, local, total.ndim - 2)

        return in_tp_order(tokens_of(tp_own), tp_received(tokens_of))

    if groups > 1:
        early = exchanged(jnp.stack(totals[:-1]))
        late = exchanged(totals[-1])
        ordered = [[*(part[group] for group in range(groups - 1)), last] for part, last in zip(early, late)]
    else:
        ordered = [[part] for part in exchanged(totals[0])]

    def output(which):
        return jnp.concatenate([part[which] for source in ordered for part in source], axis=1)

    out, dq = buffers
    return out, dq, output(0), output(1)


def solution(mesh):
    tokens = P(("ctx", "tp"), None)
    heads = P("ctx", "tp")
    return jax.shard_map(
        body,
        mesh=mesh,
        in_specs=(heads, tokens, tokens, heads, P()),
        out_specs=(heads, heads, tokens, tokens),
        check_vma=False,
    )
```

```python
import functools
import math

import jax
import jax.numpy as jnp
from jax import lax
from jax.experimental import pallas as pl
from jax.experimental.pallas import tpu as pltpu
from jax.sharding import PartitionSpec as P

HEAD_SIZE = 128
WINDOW = 8
HEADS_AT_ONCE = 4
SCORE_SCALE = 1.0 / math.sqrt(HEAD_SIZE)
LOG2E = math.log2(math.e)
MASKED = -1e30


def dot(a, b):
    return jnp.dot(a, b, preferred_element_type=jnp.float32)


def group_kernel(heads, unread, own, doc_lengths, q_ref, g_ref, own_ref, far_ref, x_ref, c_ref, *rest):
    out_ref, dq_ref, even_ref, odd_ref, *scratch = rest[unread:]
    (
        q_all, q_turned, g_all, g_turned, k_win, v_win, k_turned, v_turned,
        bias, scores, weights, grads, highest, summed, delta, dq_acc,
    ) = scratch
    rows = q_ref.shape[0]
    at_once = min(heads, HEADS_AT_ONCE)
    repeats = 2 * rows // HEAD_SIZE
    first = own[0] * rows
    doc_start = 0
    start = 0
    for doc in range(doc_lengths.shape[0]):
        doc_start = jnp.where(first >= start, start, doc_start)
        start = start + doc_lengths[doc]
    needed = jnp.clip(own[0] - doc_start // rows + 1, 1, WINDOW)
    trips = (needed + 1) // 2
    spans = [slice(head * rows, (head + 1) * rows) for head in range(heads)]
    columns = [slice(head * HEAD_SIZE, (head + 1) * HEAD_SIZE) for head in range(heads)]
    batches = [slice(head * rows, (head + at_once) * rows) for head in range(0, heads, at_once)]

    for span, column in zip(spans, columns):
        q_all[span, :] = q_ref[:, column]
        q_turned[:, span] = q_ref[:, column].T
    window_refs = [
        own_ref, c_ref.at[0], x_ref.at[0], c_ref.at[1], far_ref, c_ref.at[2], x_ref.at[1], c_ref.at[3]
    ]
    for offset, source in enumerate(window_refs):
        pair, here = offset // 2, slice(offset % 2 * rows, (offset % 2 + 1) * rows)
        k_win[pair, here, :] = source[0]
        v_win[pair, here, :HEAD_SIZE] = source[1]
        v_win[pair, here, HEAD_SIZE:] = jnp.ones((rows, HEAD_SIZE), jnp.bfloat16)
        k_turned[pair, :, here] = source[0].T
        v_turned[pair, :, here] = source[1].T
    query_pos = first + lax.broadcasted_iota(jnp.int32, (rows, HEAD_SIZE), 0)
    low = jnp.zeros((rows, HEAD_SIZE), jnp.int32)
    start = 0
    for doc in range(doc_lengths.shape[0]):
        low = jnp.where(query_pos >= start, start, low)
        start = start + doc_lengths[doc]
    highest[...] = jnp.full(highest.shape, 2 * MASKED, jnp.float32)
    summed[...] = jnp.zeros_like(summed)
    dq_acc[...] = jnp.zeros_like(dq_acc)

    def score_pair(pair, carry):
        for place in range(repeats):
            offset = 2 * pair + place // (repeats // 2)
            key_pos = (
                first - offset * rows + place % (repeats // 2) * HEAD_SIZE
                + lax.broadcasted_iota(jnp.int32, (rows, HEAD_SIZE), 1)
            )
            allowed = (key_pos >= low) & (key_pos <= query_pos)
            bias[:, place * HEAD_SIZE : (place + 1) * HEAD_SIZE] = jnp.where(allowed, 0.0, MASKED)
        for batch in batches:
            part = dot(q_all[batch, :], k_turned[pair])
            for head in range(at_once):
                here = slice(batch.start + head * rows, batch.start + (head + 1) * rows)
                piece = part[head * rows : (head + 1) * rows] * (SCORE_SCALE * LOG2E) + bias[...]
                scores[pair, here, :] = piece
                most = highest[here, :]
                for place in range(repeats):
                    most = jnp.maximum(most, piece[:, place * HEAD_SIZE : (place + 1) * HEAD_SIZE])
                highest[here, :] = most
        return carry

    lax.fori_loop(0, trips, score_pair, 0)
    for span in spans:
        highest[span, :] = jnp.broadcast_to(jnp.max(highest[span, :], axis=1, keepdims=True), (rows, HEAD_SIZE))

    def sum_pair(pair, carry):
        for batch in batches:
            for head in range(at_once):
                here = slice(batch.start + head * rows, batch.start + (head + 1) * rows)
                top = jnp.concatenate([highest[here, :]] * repeats, axis=1)
                weights[pair, here, :] = jnp.exp2(scores[pair, here, :] - top).astype(jnp.bfloat16)
            summed[batch, :] += dot(weights[pair, batch, :], v_win[pair])
        return carry

    lax.fori_loop(0, trips, sum_pair, 0)
    ones = jnp.ones((2 * HEAD_SIZE, HEAD_SIZE), jnp.bfloat16)
    for span, column in zip(spans, columns):
        inverse = 1.0 / summed[span, HEAD_SIZE:]
        output = (summed[span, :HEAD_SIZE] * inverse).astype(jnp.bfloat16)
        out_ref[:, column] = output
        scaled = (g_ref[:, column].astype(jnp.float32) * inverse).astype(jnp.bfloat16)
        g_all[span, :] = scaled
        g_turned[:, span] = scaled.T
        terms = output.astype(jnp.float32) * scaled.astype(jnp.float32)
        upper = terms.astype(jnp.bfloat16)
        lower = (terms - upper.astype(jnp.float32)).astype(jnp.bfloat16)
        delta[span, :] = dot(jnp.concatenate([upper, lower], axis=1), ones)

    def grad_pair(pair, carry):
        for batch in batches:
            part = dot(g_all[batch, :], v_turned[pair])
            for head in range(at_once):
                here = slice(batch.start + head * rows, batch.start + (head + 1) * rows)
                piece = part[head * rows : (head + 1) * rows] - jnp.concatenate([delta[here, :]] * repeats, axis=1)
                grads[here, :] = (weights[pair, here, :].astype(jnp.float32) * piece).astype(jnp.bfloat16)
            dq_acc[batch, :] += dot(grads[batch, :], k_win[pair])
        dk = (dot(q_turned[...], grads[...]) * SCORE_SCALE).astype(jnp.bfloat16)
        dv = dot(g_turned[...], weights[pair]).astype(jnp.bfloat16)
        even_ref[pair, 0] = dk[:, :rows]
        even_ref[pair, 1] = dv[:, :rows]
        odd_ref[pair, 0] = dk[:, rows:]
        odd_ref[pair, 1] = dv[:, rows:]
        return carry

    lax.fori_loop(0, trips, grad_pair, 0)
    for pair in range(WINDOW // 2):

        @pl.when(pair >= trips)
        def _(pair=pair):
            even_ref[pair] = jnp.zeros(even_ref.shape[1:], jnp.bfloat16)
            odd_ref[pair] = jnp.zeros(odd_ref.shape[1:], jnp.bfloat16)

    for span, column in zip(spans, columns):
        dq_ref[:, column] = (dq_acc[span, :] * SCORE_SCALE).astype(jnp.bfloat16)


def attend_group(group, groups, own, doc_lengths, queries, gradient, window, place, buffers, before):
    rows, width = queries.shape
    columns = width // groups
    heads = columns // HEAD_SIZE
    keys = WINDOW * rows
    stacked = heads * rows
    half = WINDOW // 2
    block = pl.BlockSpec((rows, columns), lambda i, *_: (0, group))
    shard = pl.BlockSpec((2, rows, HEAD_SIZE), lambda i, *_: (0, 0, place))
    several = lambda number: pl.BlockSpec((number, 2, rows, HEAD_SIZE), lambda i, *_: (0, 0, 0, place))
    grads_block = pl.BlockSpec((half, 2, HEAD_SIZE, rows), lambda i, *_: (0, 0, 0, 0))
    grads = jax.ShapeDtypeStruct((half, 2, HEAD_SIZE, rows), jnp.bfloat16)
    unread = len(buffers) + len(before)
    short = lambda *shape: pltpu.VMEM(shape, jnp.bfloat16)
    full = lambda *shape: pltpu.VMEM(shape, jnp.float32)
    return pl.pallas_call(
        functools.partial(group_kernel, heads, unread),
        grid_spec=pltpu.PrefetchScalarGridSpec(
            num_scalar_prefetch=2,
            grid=(1,),
            in_specs=[block, block, shard, shard, several(half // 2), several(half)]
            + [pl.BlockSpec(memory_space=pl.ANY)] * unread,
            out_specs=[block, block, grads_block, grads_block],
            scratch_shapes=[
                short(stacked, HEAD_SIZE),
                short(HEAD_SIZE, stacked),
                short(stacked, HEAD_SIZE),
                short(HEAD_SIZE, stacked),
                short(half, 2 * rows, HEAD_SIZE),
                short(half, 2 * rows, 2 * HEAD_SIZE),
                short(half, HEAD_SIZE, 2 * rows),
                short(half, HEAD_SIZE, 2 * rows),
                full(rows, 2 * rows),
                full(half, stacked, 2 * rows),
                short(half, stacked, 2 * rows),
                short(stacked, 2 * rows),
                full(stacked, HEAD_SIZE),
                full(stacked, 2 * HEAD_SIZE),
                full(stacked, HEAD_SIZE),
                full(stacked, HEAD_SIZE),
            ],
        ),
        out_shape=[
            jax.ShapeDtypeStruct(queries.shape, jnp.bfloat16),
            jax.ShapeDtypeStruct(queries.shape, jnp.bfloat16),
            grads,
            grads,
        ],
        input_output_aliases={8 + number: number for number in range(len(buffers))},
        compiler_params=pltpu.CompilerParams(vmem_limit_bytes=56 * 1024 * 1024),
        cost_estimate=pl.CostEstimate(
            flops=4 * 6 * 2 * heads * rows * keys * HEAD_SIZE,
            bytes_accessed=8 * rows * columns + 8 * keys * HEAD_SIZE,
            transcendentals=heads * rows * keys,
        ),
        name=f"attend_group_{group}",
    )(own, doc_lengths, queries, gradient, *window, *buffers, *before)


def shifted(value, steps):
    count = lax.axis_size("ctx")
    sources = range(max(0, -steps), min(count, count - steps))
    return lax.ppermute(value, "ctx", [(source, source + steps) for source in sources])


def swapped(value, bit):
    return lax.ppermute(value, "ctx", [(place, place ^ bit) for place in range(lax.axis_size("ctx"))])


def tp_received(block_for):
    count = lax.axis_size("tp")
    own = lax.axis_index("tp")
    received = []
    for step in range(1, count):
        sent = block_for(lax.rem(own + step, count), step)
        received.append(lax.ppermute(sent, "tp", [(place, (place + step) % count) for place in range(count)]))
    return received


def in_tp_order(mine, received):
    count = lax.axis_size("tp")
    own = lax.axis_index("tp")
    parts = [mine, *received]
    ordered = []
    for place in range(count):
        part = parts[0]
        for step in range(1, count):
            part = jnp.where(lax.rem(own - step + count, count) == place, parts[step], part)
        ordered.append(part)
    return ordered


def whole_block(shape):
    return pl.BlockSpec(shape, lambda i, *_: (0,) * len(shape))


def small_kernel(kernel, scalars, operands, specs, outs, before, name):
    return pl.pallas_call(
        kernel,
        grid_spec=pltpu.PrefetchScalarGridSpec(
            num_scalar_prefetch=1,
            grid=(1,),
            in_specs=specs + [pl.BlockSpec(memory_space=pl.ANY)] * len(before),
            out_specs=[whole_block(shape) for shape in outs],
        ),
        out_shape=[jax.ShapeDtypeStruct(shape, jnp.bfloat16) for shape in outs],
        compiler_params=pltpu.CompilerParams(vmem_limit_bytes=32 * 1024 * 1024),
        name=name,
    )(scalars, *operands, *before)


def pack_for_tp(key_vectors, value_vectors, groups, tp_own):
    count = lax.axis_size("tp")
    local = key_vectors.shape[0]
    columns = groups * HEAD_SIZE
    blocks = [
        pl.BlockSpec((local, columns), lambda i, own, step=step: (0, lax.rem(own[0] + step, count)))
        for step in range(1, count)
    ]

    def kernel(own, *refs):
        keys, values, outs = refs[: count - 1], refs[count - 1 : 2 * count - 2], refs[1 - count :]
        for key, value, out in zip(keys, values, outs):
            out[0] = key[...]
            out[1] = value[...]

    return small_kernel(
        kernel, tp_own, [key_vectors] * (count - 1) + [value_vectors] * (count - 1), blocks + blocks,
        [(2, local, columns)] * (count - 1), [], "pack_for_tp",
    )


def join_tokens(key_vectors, value_vectors, received, groups, bounds, tp_own):
    count = lax.axis_size("tp")
    local = key_vectors.shape[0]
    block = pl.BlockSpec((local, groups * HEAD_SIZE), lambda i, own: (0, own[0]))

    def kernel(own, key, value, *refs):
        parts, outs = refs[: count - 1], refs[count - 1 :]
        for (first, last), out in zip(bounds, outs):
            columns = slice(first * HEAD_SIZE, last * HEAD_SIZE)
            here = pl.ds(pl.multiple_of(own[0] * local, local), local)
            out[0, here, :] = key[:, columns]
            out[1, here, :] = value[:, columns]
            for step in range(1, count):
                source = lax.rem(own[0] - step + count, count)
                rows = pl.ds(pl.multiple_of(source * local, local), local)
                out[:, rows, :] = parts[step - 1][:, :, columns]

    return small_kernel(
        kernel, tp_own, [key_vectors, value_vectors, *received],
        [block, block] + [whole_block(part.shape) for part in received],
        [(2, local * count, (last - first) * HEAD_SIZE) for first, last in bounds], [], "join_tokens",
    )


def even_window(own_pair, own):
    far = shifted(own_pair, WINDOW // 2)
    beyond = shifted(far, WINDOW // 2)
    low_x = (own // 2) % 2 == 0
    x_sent = jnp.stack([jnp.where(low_x, own_pair, far), jnp.where(low_x, far, beyond)])
    return own_pair, far, beyond, x_sent


def whole_window(evens, own, before, name):
    own_pair, far, beyond, x_sent = evens
    x_pairs = swapped(x_sent, 2)
    half = WINDOW // 2

    def kernel(own, own_ref, far_ref, beyond_ref, x_ref, *refs):
        out = refs[-1]
        evens = [own_ref, x_ref.at[0], far_ref, x_ref.at[1], beyond_ref]
        low_c = lax.rem(own[0], 2)
        for bit in range(2):

            @pl.when(low_c == bit)
            def _(bit=bit):
                for place in range(half):
                    out[place] = evens[place + bit][...]

    operands = [own_pair, far, beyond, x_pairs]
    (c_sent,) = small_kernel(
        kernel, own, operands, [whole_block(part.shape) for part in operands],
        [(half, *own_pair.shape)], before, name,
    )
    return own_pair, far, x_pairs, swapped(c_sent, 1)


def wide(part):
    return part.astype(jnp.float32)


def fold_cores(even, got, own, before, name):
    half = WINDOW // 2

    def kernel(own, even_ref, got_ref, *refs):
        sent, kept = refs[-2:]
        for bit in range(2):

            @pl.when(lax.rem(own[0], 2) == bit)
            def _(bit=bit):
                for place in range(half + 1):
                    out = sent.at[place // 2] if place % 2 else kept.at[place // 2]
                    total = None
                    if place < half:
                        total = wide(even_ref[place])
                    if 0 <= place - bit < half:
                        more = wide(got_ref[place - bit])
                        total = more if total is None else total + more
                    out[...] = jnp.zeros(out.shape, out.dtype) if total is None else total.astype(out.dtype)

    shape = even.shape[1:]
    return small_kernel(
        kernel, own, [even, got], [whole_block(even.shape)] * 2,
        [(half // 2, *shape), (half // 2 + 1, *shape)], before, name,
    )


def fold_x(sent, kept, own, before, name):
    got = swapped(sent, 2)

    def kernel(own, kept_ref, got_ref, *refs):
        near, far, beyond = refs[-3:]
        for bit in range(2):

            @pl.when(lax.rem(own[0] // 2, 2) == bit)
            def _(bit=bit):
                for place, out in enumerate((near, far, beyond)):
                    total = wide(kept_ref[place])
                    if 0 <= place - bit < got_ref.shape[0]:
                        total = total + wide(got_ref[place - bit])
                    out[...] = total.astype(out.dtype)

    return small_kernel(
        kernel, own, [kept, got], [whole_block(kept.shape), whole_block(got.shape)], [kept.shape[1:]] * 3, before, name
    )


def body(queries, key_vectors, value_vectors, output_gradient, doc_lengths):
    own = lax.axis_index("ctx")
    own_info = own.reshape(1).astype(jnp.int32)
    local = key_vectors.shape[0]
    all_groups = key_vectors.shape[1] // HEAD_SIZE
    tp_count = lax.axis_size("tp")
    groups = all_groups // tp_count
    tp_own = lax.axis_index("tp")
    tp_info = tp_own.reshape(1).astype(jnp.int32)

    bounds = [(0, 1)] + ([(1, groups)] if groups > 1 else [])
    packed = pack_for_tp(key_vectors, value_vectors, groups, tp_info)
    received = tp_received(lambda place, step: packed[step - 1])
    chunks = join_tokens(key_vectors, value_vectors, received, groups, bounds, tp_info)
    evens = [even_window(chunk, own) for chunk in chunks]

    windows = [whole_window(evens[0], own_info, [], "core_swap_0")]
    buffers = ()
    results, got, folded, sums = [], [], [], []

    def fold_next_cores(before):
        group = len(folded)
        folded.append(fold_cores(results[group][2], got[group], own_info, before, f"fold_cores_{group}"))

    def fold_next_x(before):
        group = len(sums)
        sums.append(fold_x(*folded[group], own_info, before, f"fold_x_{group}"))

    for group in range(groups):
        waits = [evens[1][3]] if group == 0 and groups > 1 else []
        if group >= 2:
            waits.append(folded[group - 2][0])
        if group >= 3:
            waits.append(sums[group - 3][1])
        chunk = min(group, 1)
        results.append(
            attend_group(
                group, groups, own_info, doc_lengths, queries, output_gradient, windows[chunk], group - chunk,
                buffers, waits,
            )
        )
        *buffers, even, odd = results[-1]
        got.append(swapped(odd, 1))
        if group == 0 and groups > 1:
            windows.append(whole_window(evens[1], own_info, [even], "core_swap_1"))
        if group >= 1:
            fold_next_cores([even])
        if group >= 2 and group < groups - 1:
            fold_next_x([even])
    while len(sums) < groups - 2:
        fold_next_x([got[-1]])
    fold_next_cores([])
    while len(sums) < groups:
        fold_next_x([folded[-1][0]] if len(sums) < groups - 1 else [])

    totals = []
    for near, far, beyond in sums:
        total = wide(near) + wide(shifted(beyond, -WINDOW)) + wide(shifted(far, -(WINDOW // 2)))
        totals.append(jnp.swapaxes(total.astype(jnp.bfloat16), 1, 2))

    def exchanged(total):
        def tokens_of(place, step=0):
            return lax.dynamic_slice_in_dim(total, place * local, local, total.ndim - 2)

        return in_tp_order(tokens_of(tp_own), tp_received(tokens_of))

    if groups > 1:
        early = exchanged(jnp.stack(totals[:-1]))
        late = exchanged(totals[-1])
        ordered = [[*(part[group] for group in range(groups - 1)), last] for part, last in zip(early, late)]
    else:
        ordered = [[part] for part in exchanged(totals[0])]

    def output(which):
        return jnp.concatenate([part[which] for source in ordered for part in source], axis=1)

    out, dq = buffers
    return out, dq, output(0), output(1)


def solution(mesh):
    tokens = P(("ctx", "tp"), None)
    heads = P("ctx", "tp")
    return jax.shard_map(
        body,
        mesh=mesh,
        in_specs=(heads, tokens, tokens, heads, P()),
        out_specs=(heads, heads, tokens, tokens),
        check_vma=False,
    )
```

```python
import functools
import math

import jax
import jax.numpy as jnp
from jax import lax
from jax.experimental import pallas as pl
from jax.experimental.pallas import tpu as pltpu
from jax.sharding import PartitionSpec as P

HEAD_SIZE = 128
WINDOW = 8
HEADS_AT_ONCE = 4
SCORE_SCALE = 1.0 / math.sqrt(HEAD_SIZE)
LOG2E = math.log2(math.e)
MASKED = -1e30


def dot(a, b):
    return jnp.dot(a, b, preferred_element_type=jnp.float32)


def dot_rows(a, b):
    return lax.dot_general(a, b, (((1,), (1,)), ((), ())), preferred_element_type=jnp.float32)


def group_kernel(
    group, heads, unread, own, doc_lengths,
    q_ref, g_hbm, q_turned, g_turned_hbm, own_ref, far_ref, x_ref, c_ref, *rest,
):
    out_hbm, dq_ref, even_ref, odd_ref, *scratch = rest[unread:]
    (
        q_all, g_all, k_win, v_win, g_ref, g_turned, out_ref,
        bias, scores, weights, grads, highest, summed, delta, dq_acc, arrivals,
    ) = scratch
    rows, width = q_ref.shape
    own_columns = pl.ds(group * width, width)
    g_copy = pltpu.make_async_copy(g_hbm.at[:, own_columns], g_ref, arrivals.at[0])
    g_turned_copy = pltpu.make_async_copy(g_turned_hbm.at[group], g_turned, arrivals.at[1])
    out_copy = pltpu.make_async_copy(out_ref, out_hbm.at[:, own_columns], arrivals.at[2])
    g_copy.start()
    g_turned_copy.start()
    at_once = min(heads, HEADS_AT_ONCE)
    repeats = 2 * rows // HEAD_SIZE
    first = own[0] * rows
    doc_start = 0
    start = 0
    for doc in range(doc_lengths.shape[0]):
        doc_start = jnp.where(first >= start, start, doc_start)
        start = start + doc_lengths[doc]
    needed = jnp.clip(own[0] - doc_start // rows + 1, 1, WINDOW)
    trips = (needed + 1) // 2
    spans = [slice(head * rows, (head + 1) * rows) for head in range(heads)]
    columns = [slice(head * HEAD_SIZE, (head + 1) * HEAD_SIZE) for head in range(heads)]
    batches = [slice(head * rows, (head + at_once) * rows) for head in range(0, heads, at_once)]

    for span, column in zip(spans, columns):
        q_all[span, :] = q_ref[:, column]
    window_refs = [
        own_ref, c_ref.at[0], x_ref.at[0], c_ref.at[1], far_ref, c_ref.at[2], x_ref.at[1], c_ref.at[3]
    ]
    for offset, source in enumerate(window_refs):
        pair, here = offset // 2, slice(offset % 2 * rows, (offset % 2 + 1) * rows)
        k_win[pair, here, :] = source[0]
        v_win[pair, here, :HEAD_SIZE] = source[1]
        v_win[pair, here, HEAD_SIZE:] = jnp.ones((rows, HEAD_SIZE), jnp.bfloat16)
    query_pos = first + lax.broadcasted_iota(jnp.int32, (rows, HEAD_SIZE), 0)
    low = jnp.zeros((rows, HEAD_SIZE), jnp.int32)
    start = 0
    for doc in range(doc_lengths.shape[0]):
        low = jnp.where(query_pos >= start, start, low)
        start = start + doc_lengths[doc]
    highest[...] = jnp.full(highest.shape, 2 * MASKED, jnp.float32)
    summed[...] = jnp.zeros_like(summed)
    dq_acc[...] = jnp.zeros_like(dq_acc)

    def score_pair(pair, carry):
        for place in range(repeats):
            offset = 2 * pair + place // (repeats // 2)
            key_pos = (
                first - offset * rows + place % (repeats // 2) * HEAD_SIZE
                + lax.broadcasted_iota(jnp.int32, (rows, HEAD_SIZE), 1)
            )
            allowed = (key_pos >= low) & (key_pos <= query_pos)
            bias[:, place * HEAD_SIZE : (place + 1) * HEAD_SIZE] = jnp.where(allowed, 0.0, MASKED)
        for batch in batches:
            part = dot_rows(q_all[batch, :], k_win[pair])
            for head in range(at_once):
                here = slice(batch.start + head * rows, batch.start + (head + 1) * rows)
                piece = part[head * rows : (head + 1) * rows] * (SCORE_SCALE * LOG2E) + bias[...]
                scores[pair, here, :] = piece
                most = highest[here, :]
                for place in range(repeats):
                    most = jnp.maximum(most, piece[:, place * HEAD_SIZE : (place + 1) * HEAD_SIZE])
                highest[here, :] = most
        return carry

    lax.fori_loop(0, trips, score_pair, 0)
    for span in spans:
        highest[span, :] = jnp.broadcast_to(jnp.max(highest[span, :], axis=1, keepdims=True), (rows, HEAD_SIZE))

    def sum_pair(pair, carry):
        for batch in batches:
            for head in range(at_once):
                here = slice(batch.start + head * rows, batch.start + (head + 1) * rows)
                top = jnp.concatenate([highest[here, :]] * repeats, axis=1)
                weights[pair, here, :] = jnp.exp2(scores[pair, here, :] - top).astype(jnp.bfloat16)
            summed[batch, :] += dot(weights[pair, batch, :], v_win[pair])
        return carry

    lax.fori_loop(0, trips, sum_pair, 0)
    g_copy.wait()
    g_turned_copy.wait()
    lane = lax.broadcasted_iota(jnp.int32, (rows, HEAD_SIZE), 1)
    inverses = jnp.zeros((rows, HEAD_SIZE), jnp.float32)
    for head, (span, column) in enumerate(zip(spans, columns)):
        inverse = 1.0 / summed[span, HEAD_SIZE:]
        inverses = jnp.where(lane == head, inverse, inverses)
        output = (summed[span, :HEAD_SIZE] * inverse).astype(jnp.bfloat16)
        out_ref[:, column] = output
        scaled = (g_ref[:, column].astype(jnp.float32) * inverse).astype(jnp.bfloat16)
        g_all[span, :] = scaled
        terms = output.astype(jnp.float32) * scaled.astype(jnp.float32)
        upper = terms.astype(jnp.bfloat16)
        grads[span, :HEAD_SIZE] = upper
        grads[span, HEAD_SIZE : 2 * HEAD_SIZE] = (terms - upper.astype(jnp.float32)).astype(jnp.bfloat16)
    out_copy.start()
    delta[...] = dot(grads[:, : 2 * HEAD_SIZE], jnp.ones((2 * HEAD_SIZE, HEAD_SIZE), jnp.bfloat16))
    inverses = inverses.T
    for head, span in enumerate(spans):
        turned = g_turned[:, span].astype(jnp.float32) * inverses[head : head + 1, :]
        g_turned[:, span] = turned.astype(jnp.bfloat16)

    def grad_pair(pair, carry):
        for batch in batches:
            part = dot_rows(g_all[batch, :], v_win[pair, :, :HEAD_SIZE])
            for head in range(at_once):
                here = slice(batch.start + head * rows, batch.start + (head + 1) * rows)
                piece = part[head * rows : (head + 1) * rows] - jnp.concatenate([delta[here, :]] * repeats, axis=1)
                grads[here, :] = (weights[pair, here, :].astype(jnp.float32) * piece).astype(jnp.bfloat16)
            dq_acc[batch, :] += dot(grads[batch, :], k_win[pair])
        dk = (dot(q_turned[...], grads[...]) * SCORE_SCALE).astype(jnp.bfloat16)
        dv = dot(g_turned[...], weights[pair]).astype(jnp.bfloat16)
        even_ref[pair, 0] = dk[:, :rows]
        even_ref[pair, 1] = dv[:, :rows]
        odd_ref[pair, 0] = dk[:, rows:]
        odd_ref[pair, 1] = dv[:, rows:]
        return carry

    lax.fori_loop(0, trips, grad_pair, 0)
    for pair in range(WINDOW // 2):

        @pl.when(pair >= trips)
        def _(pair=pair):
            even_ref[pair] = jnp.zeros(even_ref.shape[1:], jnp.bfloat16)
            odd_ref[pair] = jnp.zeros(odd_ref.shape[1:], jnp.bfloat16)

    for span, column in zip(spans, columns):
        dq_ref[:, column] = (dq_acc[span, :] * SCORE_SCALE).astype(jnp.bfloat16)
    out_copy.wait()


def turn_kernel(heads, ref, out):
    rows = ref.shape[0]
    for head in range(heads):
        out[0, :, head * rows : (head + 1) * rows] = ref[:, head * HEAD_SIZE : (head + 1) * HEAD_SIZE].T


def turned_heads(values, groups, name):
    rows, width = values.shape
    columns = width // groups
    heads = columns // HEAD_SIZE
    return pl.pallas_call(
        functools.partial(turn_kernel, heads),
        grid=(groups,),
        in_specs=[pl.BlockSpec((rows, columns), lambda i: (0, i))],
        out_specs=pl.BlockSpec((1, HEAD_SIZE, heads * rows), lambda i: (i, 0, 0)),
        out_shape=jax.ShapeDtypeStruct((groups, HEAD_SIZE, heads * rows), jnp.bfloat16),
        cost_estimate=pl.CostEstimate(flops=0, bytes_accessed=8 * values.size, transcendentals=0),
        name=name,
    )(values)


def attend_group(
    group, groups, own, doc_lengths, queries, gradient, turned_q, turned_g, window, place, buffers, before
):
    rows, width = queries.shape
    columns = width // groups
    heads = columns // HEAD_SIZE
    keys = WINDOW * rows
    stacked = heads * rows
    half = WINDOW // 2
    block = pl.BlockSpec((rows, columns), lambda i, *_: (0, group))
    shard = pl.BlockSpec((2, rows, HEAD_SIZE), lambda i, *_: (0, 0, place))
    several = lambda number: pl.BlockSpec((number, 2, rows, HEAD_SIZE), lambda i, *_: (0, 0, 0, place))
    grads_block = pl.BlockSpec((half, 2, HEAD_SIZE, rows), lambda i, *_: (0, 0, 0, 0))
    grads = jax.ShapeDtypeStruct((half, 2, HEAD_SIZE, rows), jnp.bfloat16)
    unread = len(buffers) + len(before)
    short = lambda *shape: pltpu.VMEM(shape, jnp.bfloat16)
    full = lambda *shape: pltpu.VMEM(shape, jnp.float32)
    return pl.pallas_call(
        functools.partial(group_kernel, group, heads, unread),
        grid_spec=pltpu.PrefetchScalarGridSpec(
            num_scalar_prefetch=2,
            grid=(1,),
            in_specs=[
                block,
                pl.BlockSpec(memory_space=pl.ANY),
                pl.BlockSpec((None, HEAD_SIZE, stacked), lambda i, *_: (group, 0, 0)),
                pl.BlockSpec(memory_space=pl.ANY),
                shard, shard, several(half // 2), several(half),
            ]
            + [pl.BlockSpec(memory_space=pl.ANY)] * unread,
            out_specs=[pl.BlockSpec(memory_space=pl.ANY), block, grads_block, grads_block],
            scratch_shapes=[
                short(stacked, HEAD_SIZE),
                short(stacked, HEAD_SIZE),
                short(half, 2 * rows, HEAD_SIZE),
                short(half, 2 * rows, 2 * HEAD_SIZE),
                short(rows, columns),
                short(HEAD_SIZE, stacked),
                short(rows, columns),
                full(rows, 2 * rows),
                full(half, stacked, 2 * rows),
                short(half, stacked, 2 * rows),
                short(stacked, 2 * rows),
                full(stacked, HEAD_SIZE),
                full(stacked, 2 * HEAD_SIZE),
                full(stacked, HEAD_SIZE),
                full(stacked, HEAD_SIZE),
                pltpu.SemaphoreType.DMA((3,)),
            ],
        ),
        out_shape=[
            jax.ShapeDtypeStruct(queries.shape, jnp.bfloat16),
            jax.ShapeDtypeStruct(queries.shape, jnp.bfloat16),
            grads,
            grads,
        ],
        input_output_aliases={10 + number: number for number in range(len(buffers))},
        compiler_params=pltpu.CompilerParams(vmem_limit_bytes=56 * 1024 * 1024),
        cost_estimate=pl.CostEstimate(
            flops=4 * 6 * 2 * heads * rows * keys * HEAD_SIZE,
            bytes_accessed=8 * rows * columns + 8 * keys * HEAD_SIZE,
            transcendentals=heads * rows * keys,
        ),
        name=f"attend_group_{group}",
    )(own, doc_lengths, queries, gradient, turned_q, turned_g, *window, *buffers, *before)


def shifted(value, steps):
    count = lax.axis_size("ctx")
    sources = range(max(0, -steps), min(count, count - steps))
    return lax.ppermute(value, "ctx", [(source, source + steps) for source in sources])


def swapped(value, bit):
    return lax.ppermute(value, "ctx", [(place, place ^ bit) for place in range(lax.axis_size("ctx"))])


def tp_received(block_for):
    count = lax.axis_size("tp")
    own = lax.axis_index("tp")
    received = []
    for step in range(1, count):
        sent = block_for(lax.rem(own + step, count), step)
        received.append(lax.ppermute(sent, "tp", [(place, (place + step) % count) for place in range(count)]))
    return received


def in_tp_order(mine, received):
    count = lax.axis_size("tp")
    own = lax.axis_index("tp")
    parts = [mine, *received]
    ordered = []
    for place in range(count):
        part = parts[0]
        for step in range(1, count):
            part = jnp.where(lax.rem(own - step + count, count) == place, parts[step], part)
        ordered.append(part)
    return ordered


def whole_block(shape):
    return pl.BlockSpec(shape, lambda i, *_: (0,) * len(shape))


def small_kernel(kernel, scalars, operands, specs, outs, before, name, through=()):
    if through:
        inner, handed = kernel, len(through)
        kernel = lambda *refs: inner(*refs[:-handed])
    first = 1 + len(operands) + len(before)
    return pl.pallas_call(
        kernel,
        grid_spec=pltpu.PrefetchScalarGridSpec(
            num_scalar_prefetch=1,
            grid=(1,),
            in_specs=specs + [pl.BlockSpec(memory_space=pl.ANY)] * (len(before) + len(through)),
            out_specs=[whole_block(shape) for shape in outs] + [pl.BlockSpec(memory_space=pl.ANY)] * len(through),
        ),
        out_shape=[jax.ShapeDtypeStruct(shape, jnp.bfloat16) for shape in outs]
        + [jax.ShapeDtypeStruct(part.shape, part.dtype) for part in through],
        input_output_aliases={first + number: len(outs) + number for number in range(len(through))},
        compiler_params=pltpu.CompilerParams(vmem_limit_bytes=32 * 1024 * 1024),
        name=name,
    )(scalars, *operands, *before, *through)


def pack_for_tp(key_vectors, value_vectors, groups, tp_own):
    count = lax.axis_size("tp")
    local = key_vectors.shape[0]
    columns = groups * HEAD_SIZE
    blocks = [
        pl.BlockSpec((local, columns), lambda i, own, step=step: (0, lax.rem(own[0] + step, count)))
        for step in range(1, count)
    ]

    def kernel(own, *refs):
        keys, values, outs = refs[: count - 1], refs[count - 1 : 2 * count - 2], refs[1 - count :]
        for key, value, out in zip(keys, values, outs):
            out[0] = key[...]
            out[1] = value[...]

    return small_kernel(
        kernel, tp_own, [key_vectors] * (count - 1) + [value_vectors] * (count - 1), blocks + blocks,
        [(2, local, columns)] * (count - 1), [], "pack_for_tp",
    )


def join_tokens(key_vectors, value_vectors, received, groups, bounds, tp_own):
    count = lax.axis_size("tp")
    local = key_vectors.shape[0]
    block = pl.BlockSpec((local, groups * HEAD_SIZE), lambda i, own: (0, own[0]))

    def kernel(own, key, value, *refs):
        parts, outs = refs[: count - 1], refs[count - 1 :]
        for (first, last), out in zip(bounds, outs):
            columns = slice(first * HEAD_SIZE, last * HEAD_SIZE)
            here = pl.ds(pl.multiple_of(own[0] * local, local), local)
            out[0, here, :] = key[:, columns]
            out[1, here, :] = value[:, columns]
            for step in range(1, count):
                source = lax.rem(own[0] - step + count, count)
                rows = pl.ds(pl.multiple_of(source * local, local), local)
                out[:, rows, :] = parts[step - 1][:, :, columns]

    return small_kernel(
        kernel, tp_own, [key_vectors, value_vectors, *received],
        [block, block] + [whole_block(part.shape) for part in received],
        [(2, local * count, (last - first) * HEAD_SIZE) for first, last in bounds], [], "join_tokens",
    )


def even_window(own_pair, own):
    far = shifted(own_pair, WINDOW // 2)
    beyond = shifted(far, WINDOW // 2)
    low_x = (own // 2) % 2 == 0
    x_sent = jnp.stack([jnp.where(low_x, own_pair, far), jnp.where(low_x, far, beyond)])
    return own_pair, far, beyond, x_sent


def whole_window(evens, own, before, name):
    own_pair, far, beyond, x_sent = evens
    x_pairs = swapped(x_sent, 2)
    half = WINDOW // 2

    def kernel(own, own_ref, far_ref, beyond_ref, x_ref, *refs):
        out = refs[-1]
        evens = [own_ref, x_ref.at[0], far_ref, x_ref.at[1], beyond_ref]
        low_c = lax.rem(own[0], 2)
        for bit in range(2):

            @pl.when(low_c == bit)
            def _(bit=bit):
                for place in range(half):
                    out[place] = evens[place + bit][...]

    operands = [own_pair, far, beyond, x_pairs]
    (c_sent,) = small_kernel(
        kernel, own, operands, [whole_block(part.shape) for part in operands],
        [(half, *own_pair.shape)], before, name,
    )
    return own_pair, far, x_pairs, swapped(c_sent, 1)


def wide(part):
    return part.astype(jnp.float32)


def fold_cores(even, got, own, before, name):
    half = WINDOW // 2

    def kernel(own, even_ref, got_ref, *refs):
        sent, kept = refs[-2:]
        for bit in range(2):

            @pl.when(lax.rem(own[0], 2) == bit)
            def _(bit=bit):
                for place in range(half + 1):
                    out = sent.at[place // 2] if place % 2 else kept.at[place // 2]
                    total = None
                    if place < half:
                        total = wide(even_ref[place])
                    if 0 <= place - bit < half:
                        more = wide(got_ref[place - bit])
                        total = more if total is None else total + more
                    out[...] = jnp.zeros(out.shape, out.dtype) if total is None else total.astype(out.dtype)

    shape = even.shape[1:]
    return small_kernel(
        kernel, own, [even, got], [whole_block(even.shape)] * 2,
        [(half // 2, *shape), (half // 2 + 1, *shape)], before, name,
    )


def fold_x(sent, kept, own, before, name, through=()):
    got = swapped(sent, 2)

    def kernel(own, kept_ref, got_ref, *refs):
        near, far, beyond = refs[-3:]
        for bit in range(2):

            @pl.when(lax.rem(own[0] // 2, 2) == bit)
            def _(bit=bit):
                for place, out in enumerate((near, far, beyond)):
                    total = wide(kept_ref[place])
                    if 0 <= place - bit < got_ref.shape[0]:
                        total = total + wide(got_ref[place - bit])
                    out[...] = total.astype(out.dtype)

    return small_kernel(
        kernel, own, [kept, got], [whole_block(kept.shape), whole_block(got.shape)], [kept.shape[1:]] * 3, before, name, through,
    )


def finish(parts, own, before, name):
    count = len(parts)
    operands = [array for part in parts for array in part]
    kinds, depth, rows = operands[0].shape

    def kernel(own, *refs):
        out = refs[-1]
        for index in range(count):
            near, far, beyond = refs[3 * index : 3 * index + 3]
            for kind in range(kinds):
                out[index, kind] = (wide(near[kind]) + wide(far[kind]) + wide(beyond[kind])).T.astype(out.dtype)

    return small_kernel(
        kernel, own, operands, [whole_block(part.shape) for part in operands],
        [(count, kinds, rows, depth)], before, name,
    )[0]


def body(queries, key_vectors, value_vectors, output_gradient, doc_lengths):
    own = lax.axis_index("ctx")
    own_info = own.reshape(1).astype(jnp.int32)
    local = key_vectors.shape[0]
    all_groups = key_vectors.shape[1] // HEAD_SIZE
    tp_count = lax.axis_size("tp")
    groups = all_groups // tp_count
    tp_own = lax.axis_index("tp")
    tp_info = tp_own.reshape(1).astype(jnp.int32)

    bounds = [(0, 1)] + ([(1, groups)] if groups > 1 else [])
    packed = pack_for_tp(key_vectors, value_vectors, groups, tp_info)
    received = tp_received(lambda place, step: packed[step - 1])
    chunks = join_tokens(key_vectors, value_vectors, received, groups, bounds, tp_info)
    evens = [even_window(chunk, own) for chunk in chunks]
    turned_q = turned_heads(queries, groups, "turn_queries")
    turned_g = turned_heads(output_gradient, groups, "turn_gradient")

    windows = [whole_window(evens[0], own_info, [], "core_swap_0")]
    buffers = ()
    results, got, folded, sums, parts = [], [], [], [], []

    def fold_next_cores(before):
        group = len(folded)
        folded.append(fold_cores(results[group][2], got[group], own_info, before, f"fold_cores_{group}"))

    def fold_next_x(before, through=()):
        group = len(sums)
        near, far, beyond, *handed = fold_x(*folded[group], own_info, before, f"fold_x_{group}", through)
        sums.append(near)
        parts.append((near, shifted(far, -(WINDOW // 2)), shifted(beyond, -WINDOW)))
        return handed

    for group in range(groups):
        waits = [evens[1][3]] if group == 0 and groups > 1 else []
        if group >= 2:
            waits.append(folded[group - 2][0])
        if group >= 3:
            waits.append(sums[group - 3])
        chunk = min(group, 1)
        results.append(
            attend_group(
                group, groups, own_info, doc_lengths, queries, output_gradient, turned_q, turned_g,
                windows[chunk], group - chunk, buffers, waits,
            )
        )
        *buffers, even, odd = results[-1]
        if 3 <= groups == group + 1:
            (odd,) = fold_next_x([array for part in parts for array in part[1:]], [odd])
        got.append(swapped(odd, 1))
        if group == 0 and groups > 1:
            windows.append(whole_window(evens[1], own_info, [even], "core_swap_1"))
        if group >= 1:
            fold_next_cores([even])
        if group >= 2 and group < groups - 1:
            fold_next_x([even])
    fold_next_cores([])
    while len(sums) < groups:
        fold_next_x([folded[-1][0]] if len(sums) < groups - 1 else [])

    def exchanged(total):
        def tokens_of(place, step=0):
            return lax.dynamic_slice_in_dim(total, place * local, local, total.ndim - 2)

        return in_tp_order(tokens_of(tp_own), tp_received(tokens_of))

    if groups > 1:
        early = exchanged(finish(parts[:-1], own_info, [sums[-1]], "finish_early"))
        late = exchanged(finish(parts[-1:], own_info, [], "finish_late"))
        ordered = [[*(part[group] for group in range(groups - 1)), last[0]] for part, last in zip(early, late)]
    else:
        ordered = [[part[0]] for part in exchanged(finish(parts, own_info, [], "finish_late"))]

    def output(which):
        return jnp.concatenate([part[which] for source in ordered for part in source], axis=1)

    out, dq = buffers
    return out, dq, output(0), output(1)


def solution(mesh):
    tokens = P(("ctx", "tp"), None)
    heads = P("ctx", "tp")
    return jax.shard_map(
        body,
        mesh=mesh,
        in_specs=(heads, tokens, tokens, heads, P()),
        out_specs=(heads, heads, tokens, tokens),
        check_vma=False,
    )
```

```python
import functools
import math

import jax
import jax.numpy as jnp
from jax import lax
from jax.experimental import pallas as pl
from jax.experimental.pallas import tpu as pltpu
from jax.sharding import PartitionSpec as P

HEAD_SIZE = 128
WINDOW = 8
HEADS_AT_ONCE = 4
SCORE_SCALE = 1.0 / math.sqrt(HEAD_SIZE)
LOG2E = math.log2(math.e)
MASKED = -1e30


def dot(a, b):
    return jnp.dot(a, b, preferred_element_type=jnp.float32)


def dot_rows(a, b):
    return lax.dot_general(a, b, (((1,), (1,)), ((), ())), preferred_element_type=jnp.float32)


def group_kernel(
    group, heads, unread, own, doc_lengths, q_ref, g_hbm, own_ref, far_ref, x_ref, c_ref, *rest
):
    out_hbm, dq_ref, even_ref, odd_ref, *scratch = rest[unread:]
    (
        q_all, q_turned, g_all, g_turned, k_win, v_win, g_ref, out_ref,
        bias, scores, weights, grads, highest, summed, delta, dq_acc, arrivals,
    ) = scratch
    rows, width = q_ref.shape
    own_columns = pl.ds(group * width, width)
    g_copy = pltpu.make_async_copy(g_hbm.at[:, own_columns], g_ref, arrivals.at[0])
    out_copy = pltpu.make_async_copy(out_ref, out_hbm.at[:, own_columns], arrivals.at[1])
    g_copy.start()
    at_once = min(heads, HEADS_AT_ONCE)
    repeats = 2 * rows // HEAD_SIZE
    first = own[0] * rows
    doc_start = 0
    start = 0
    for doc in range(doc_lengths.shape[0]):
        doc_start = jnp.where(first >= start, start, doc_start)
        start = start + doc_lengths[doc]
    needed = jnp.clip(own[0] - doc_start // rows + 1, 1, WINDOW)
    trips = (needed + 1) // 2
    batches = [slice(head * rows, (head + at_once) * rows) for head in range(0, heads, at_once)]

    def each(count, step):
        def body(index, carry):
            step(index)
            return carry

        lax.fori_loop(0, count, body, 0)

    def places_of(head):
        span = pl.ds(pl.multiple_of(head * rows, rows), rows)
        return span, pl.ds(pl.multiple_of(head * HEAD_SIZE, HEAD_SIZE), HEAD_SIZE)

    def load_head(head):
        span, column = places_of(head)
        query = q_ref[:, column]
        q_all[span, :] = query
        q_turned[:, span] = query.T
        highest[span, :] = jnp.full((rows, HEAD_SIZE), 2 * MASKED, jnp.float32)
        summed[span, :] = jnp.zeros((rows, 2 * HEAD_SIZE), jnp.float32)
        dq_acc[span, :] = jnp.zeros((rows, HEAD_SIZE), jnp.float32)

    each(heads, load_head)
    window_refs = [
        own_ref, c_ref.at[0], x_ref.at[0], c_ref.at[1], far_ref, c_ref.at[2], x_ref.at[1], c_ref.at[3]
    ]
    for offset, source in enumerate(window_refs):
        pair, here = offset // 2, slice(offset % 2 * rows, (offset % 2 + 1) * rows)
        k_win[pair, here, :] = source[0]
        v_win[pair, here, :HEAD_SIZE] = source[1]

    def add_ones(pair):
        v_win[pair, :, HEAD_SIZE:] = jnp.ones((2 * rows, HEAD_SIZE), jnp.bfloat16)

    each(trips, add_ones)
    query_pos = first + lax.broadcasted_iota(jnp.int32, (rows, HEAD_SIZE), 0)
    low = jnp.zeros((rows, HEAD_SIZE), jnp.int32)
    start = 0
    for doc in range(doc_lengths.shape[0]):
        low = jnp.where(query_pos >= start, start, low)
        start = start + doc_lengths[doc]

    def score_pair(pair):
        for place in range(repeats):
            offset = 2 * pair + place // (repeats // 2)
            key_pos = (
                first - offset * rows + place % (repeats // 2) * HEAD_SIZE
                + lax.broadcasted_iota(jnp.int32, (rows, HEAD_SIZE), 1)
            )
            allowed = (key_pos >= low) & (key_pos <= query_pos)
            bias[:, place * HEAD_SIZE : (place + 1) * HEAD_SIZE] = jnp.where(allowed, 0.0, MASKED)
        for batch in batches:
            part = dot_rows(q_all[batch, :], k_win[pair])
            for head in range(at_once):
                here = slice(batch.start + head * rows, batch.start + (head + 1) * rows)
                piece = part[head * rows : (head + 1) * rows] * (SCORE_SCALE * LOG2E) + bias[...]
                scores[pair, here, :] = piece
                most = highest[here, :]
                for place in range(repeats):
                    most = jnp.maximum(most, piece[:, place * HEAD_SIZE : (place + 1) * HEAD_SIZE])
                highest[here, :] = most

    each(trips, score_pair)

    def spread_highest(head):
        span, _ = places_of(head)
        top = jnp.max(highest[span, :], axis=1, keepdims=True)
        highest[span, :] = jnp.broadcast_to(top, (rows, HEAD_SIZE))

    each(heads, spread_highest)

    def sum_pair(pair):
        for batch in batches:
            for head in range(at_once):
                here = slice(batch.start + head * rows, batch.start + (head + 1) * rows)
                top = jnp.concatenate([highest[here, :]] * repeats, axis=1)
                weights[pair, here, :] = jnp.exp2(scores[pair, here, :] - top).astype(jnp.bfloat16)
            summed[batch, :] += dot(weights[pair, batch, :], v_win[pair])

    each(trips, sum_pair)
    g_copy.wait()

    def close_head(head):
        span, column = places_of(head)
        inverse = 1.0 / summed[span, HEAD_SIZE:]
        output = (summed[span, :HEAD_SIZE] * inverse).astype(jnp.bfloat16)
        out_ref[:, column] = output
        scaled = (g_ref[:, column].astype(jnp.float32) * inverse).astype(jnp.bfloat16)
        g_all[span, :] = scaled
        g_turned[:, span] = scaled.T
        terms = output.astype(jnp.float32) * scaled.astype(jnp.float32)
        upper = terms.astype(jnp.bfloat16)
        lower = (terms - upper.astype(jnp.float32)).astype(jnp.bfloat16)
        ones = jnp.ones((2 * HEAD_SIZE, HEAD_SIZE), jnp.bfloat16)
        delta[span, :] = dot(jnp.concatenate([upper, lower], axis=1), ones)

    each(heads, close_head)
    out_copy.start()

    def grad_pair(pair):
        for batch in batches:
            part = dot_rows(g_all[batch, :], v_win[pair, :, :HEAD_SIZE])
            for head in range(at_once):
                here = slice(batch.start + head * rows, batch.start + (head + 1) * rows)
                piece = part[head * rows : (head + 1) * rows] - jnp.concatenate([delta[here, :]] * repeats, axis=1)
                grads[here, :] = (weights[pair, here, :].astype(jnp.float32) * piece).astype(jnp.bfloat16)
            dq_acc[batch, :] += dot(grads[batch, :], k_win[pair])
        dk = (dot(q_turned[...], grads[...]) * SCORE_SCALE).astype(jnp.bfloat16)
        dv = dot(g_turned[...], weights[pair]).astype(jnp.bfloat16)
        even_ref[pair, 0] = dk[:, :rows]
        even_ref[pair, 1] = dv[:, :rows]
        odd_ref[pair, 0] = dk[:, rows:]
        odd_ref[pair, 1] = dv[:, rows:]

    each(trips, grad_pair)

    def clear_pair(pair, carry):
        even_ref[pair] = jnp.zeros(even_ref.shape[1:], jnp.bfloat16)
        odd_ref[pair] = jnp.zeros(odd_ref.shape[1:], jnp.bfloat16)
        return carry

    lax.fori_loop(trips, WINDOW // 2, clear_pair, 0)

    def store_dq(head):
        span, column = places_of(head)
        dq_ref[:, column] = (dq_acc[span, :] * SCORE_SCALE).astype(jnp.bfloat16)

    each(heads, store_dq)
    out_copy.wait()


def attend_group(
    group, groups, own, doc_lengths, queries, gradient, window, place, buffers, before
):
    rows, width = queries.shape
    columns = width // groups
    heads = columns // HEAD_SIZE
    keys = WINDOW * rows
    stacked = heads * rows
    half = WINDOW // 2
    block = pl.BlockSpec((rows, columns), lambda i, *_: (0, group))
    shard = pl.BlockSpec((2, rows, HEAD_SIZE), lambda i, *_: (0, 0, place))
    several = lambda number: pl.BlockSpec((number, 2, rows, HEAD_SIZE), lambda i, *_: (0, 0, 0, place))
    grads_block = pl.BlockSpec((half, 2, HEAD_SIZE, rows), lambda i, *_: (0, 0, 0, 0))
    grads = jax.ShapeDtypeStruct((half, 2, HEAD_SIZE, rows), jnp.bfloat16)
    unread = len(buffers) + len(before)
    short = lambda *shape: pltpu.VMEM(shape, jnp.bfloat16)
    full = lambda *shape: pltpu.VMEM(shape, jnp.float32)
    return pl.pallas_call(
        functools.partial(group_kernel, group, heads, unread),
        grid_spec=pltpu.PrefetchScalarGridSpec(
            num_scalar_prefetch=2,
            grid=(1,),
            in_specs=[
                block,
                pl.BlockSpec(memory_space=pl.ANY),
                shard, shard, several(half // 2), several(half),
            ]
            + [pl.BlockSpec(memory_space=pl.ANY)] * unread,
            out_specs=[pl.BlockSpec(memory_space=pl.ANY), block, grads_block, grads_block],
            scratch_shapes=[
                short(stacked, HEAD_SIZE),
                short(HEAD_SIZE, stacked),
                short(stacked, HEAD_SIZE),
                short(HEAD_SIZE, stacked),
                short(half, 2 * rows, HEAD_SIZE),
                short(half, 2 * rows, 2 * HEAD_SIZE),
                short(rows, columns),
                short(rows, columns),
                full(rows, 2 * rows),
                full(half, stacked, 2 * rows),
                short(half, stacked, 2 * rows),
                short(stacked, 2 * rows),
                full(stacked, HEAD_SIZE),
                full(stacked, 2 * HEAD_SIZE),
                full(stacked, HEAD_SIZE),
                full(stacked, HEAD_SIZE),
                pltpu.SemaphoreType.DMA((2,)),
            ],
        ),
        out_shape=[
            jax.ShapeDtypeStruct(queries.shape, jnp.bfloat16),
            jax.ShapeDtypeStruct(queries.shape, jnp.bfloat16),
            grads,
            grads,
        ],
        input_output_aliases={8 + number: number for number in range(len(buffers))},
        compiler_params=pltpu.CompilerParams(vmem_limit_bytes=56 * 1024 * 1024),
        cost_estimate=pl.CostEstimate(
            flops=4 * 6 * 2 * heads * rows * keys * HEAD_SIZE,
            bytes_accessed=8 * rows * columns + 8 * keys * HEAD_SIZE,
            transcendentals=heads * rows * keys,
        ),
        name=f"attend_group_{group}",
    )(own, doc_lengths, queries, gradient, *window, *buffers, *before)


def shifted(value, steps):
    count = lax.axis_size("ctx")
    sources = range(max(0, -steps), min(count, count - steps))
    return lax.ppermute(value, "ctx", [(source, source + steps) for source in sources])


def swapped(value, bit):
    return lax.ppermute(value, "ctx", [(place, place ^ bit) for place in range(lax.axis_size("ctx"))])


def tp_received(block_for):
    count = lax.axis_size("tp")
    own = lax.axis_index("tp")
    received = []
    for step in range(1, count):
        sent = block_for(lax.rem(own + step, count), step)
        received.append(lax.ppermute(sent, "tp", [(place, (place + step) % count) for place in range(count)]))
    return received


def in_tp_order(mine, received):
    count = lax.axis_size("tp")
    own = lax.axis_index("tp")
    parts = [mine, *received]
    ordered = []
    for place in range(count):
        part = parts[0]
        for step in range(1, count):
            part = jnp.where(lax.rem(own - step + count, count) == place, parts[step], part)
        ordered.append(part)
    return ordered


def whole_block(shape):
    return pl.BlockSpec(shape, lambda i, *_: (0,) * len(shape))


def small_kernel(kernel, scalars, operands, specs, outs, before, name, through=()):
    if through:
        inner, handed = kernel, len(through)
        kernel = lambda *refs: inner(*refs[:-handed])
    first = 1 + len(operands) + len(before)
    return pl.pallas_call(
        kernel,
        grid_spec=pltpu.PrefetchScalarGridSpec(
            num_scalar_prefetch=1,
            grid=(1,),
            in_specs=specs + [pl.BlockSpec(memory_space=pl.ANY)] * (len(before) + len(through)),
            out_specs=[whole_block(shape) for shape in outs] + [pl.BlockSpec(memory_space=pl.ANY)] * len(through),
        ),
        out_shape=[jax.ShapeDtypeStruct(shape, jnp.bfloat16) for shape in outs]
        + [jax.ShapeDtypeStruct(part.shape, part.dtype) for part in through],
        input_output_aliases={first + number: len(outs) + number for number in range(len(through))},
        compiler_params=pltpu.CompilerParams(vmem_limit_bytes=32 * 1024 * 1024),
        name=name,
    )(scalars, *operands, *before, *through)


def pack_for_tp(key_vectors, value_vectors, groups, tp_own):
    count = lax.axis_size("tp")
    local = key_vectors.shape[0]
    columns = groups * HEAD_SIZE
    blocks = [
        pl.BlockSpec((local, columns), lambda i, own, step=step: (0, lax.rem(own[0] + step, count)))
        for step in range(1, count)
    ]

    def kernel(own, *refs):
        keys, values, outs = refs[: count - 1], refs[count - 1 : 2 * count - 2], refs[1 - count :]
        for key, value, out in zip(keys, values, outs):
            out[0] = key[...]
            out[1] = value[...]

    return small_kernel(
        kernel, tp_own, [key_vectors] * (count - 1) + [value_vectors] * (count - 1), blocks + blocks,
        [(2, local, columns)] * (count - 1), [], "pack_for_tp",
    )


def join_tokens(key_vectors, value_vectors, received, groups, bounds, tp_own):
    count = lax.axis_size("tp")
    local = key_vectors.shape[0]
    block = pl.BlockSpec((local, groups * HEAD_SIZE), lambda i, own: (0, own[0]))

    def kernel(own, key, value, *refs):
        parts, outs = refs[: count - 1], refs[count - 1 :]
        for (first, last), out in zip(bounds, outs):
            columns = slice(first * HEAD_SIZE, last * HEAD_SIZE)
            here = pl.ds(pl.multiple_of(own[0] * local, local), local)
            out[0, here, :] = key[:, columns]
            out[1, here, :] = value[:, columns]
            for step in range(1, count):
                source = lax.rem(own[0] - step + count, count)
                rows = pl.ds(pl.multiple_of(source * local, local), local)
                out[:, rows, :] = parts[step - 1][:, :, columns]

    return small_kernel(
        kernel, tp_own, [key_vectors, value_vectors, *received],
        [block, block] + [whole_block(part.shape) for part in received],
        [(2, local * count, (last - first) * HEAD_SIZE) for first, last in bounds], [], "join_tokens",
    )


def even_window(own_pair):
    far = shifted(own_pair, WINDOW // 2)
    return own_pair, far, shifted(far, WINDOW // 2)


def for_x_swap(evens, own, before, name):
    def kernel(own, *refs):
        out = refs[-1]
        for bit in range(2):

            @pl.when(lax.rem(own[0] // 2, 2) == bit)
            def _(bit=bit):
                for place in range(2):
                    out[place] = refs[place + bit][...]

    return small_kernel(
        kernel, own, evens, [whole_block(part.shape) for part in evens], [(2, *evens[0].shape)], before, name
    )[0]


def whole_window(evens, x_sent, own, before, name):
    own_pair, far, beyond = evens
    x_pairs = swapped(x_sent, 2)
    half = WINDOW // 2

    def kernel(own, own_ref, far_ref, beyond_ref, x_ref, *refs):
        out = refs[-1]
        evens = [own_ref, x_ref.at[0], far_ref, x_ref.at[1], beyond_ref]
        low_c = lax.rem(own[0], 2)
        for bit in range(2):

            @pl.when(low_c == bit)
            def _(bit=bit):
                for place in range(half):
                    out[place] = evens[place + bit][...]

    operands = [own_pair, far, beyond, x_pairs]
    (c_sent,) = small_kernel(
        kernel, own, operands, [whole_block(part.shape) for part in operands],
        [(half, *own_pair.shape)], before, name,
    )
    return own_pair, far, x_pairs, swapped(c_sent, 1)


def wide(part):
    return part.astype(jnp.float32)


def fold_cores(even, got, own, before, name):
    half = WINDOW // 2

    def kernel(own, even_ref, got_ref, *refs):
        sent, kept = refs[-2:]
        for bit in range(2):

            @pl.when(lax.rem(own[0], 2) == bit)
            def _(bit=bit):
                for place in range(half + 1):
                    out = sent.at[place // 2] if place % 2 else kept.at[place // 2]
                    total = None
                    if place < half:
                        total = wide(even_ref[place])
                    if 0 <= place - bit < half:
                        more = wide(got_ref[place - bit])
                        total = more if total is None else total + more
                    out[...] = jnp.zeros(out.shape, out.dtype) if total is None else total.astype(out.dtype)

    shape = even.shape[1:]
    return small_kernel(
        kernel, own, [even, got], [whole_block(even.shape)] * 2,
        [(half // 2, *shape), (half // 2 + 1, *shape)], before, name,
    )


def fold_x(sent, kept, own, before, name, through=()):
    got = swapped(sent, 2)

    def kernel(own, kept_ref, got_ref, *refs):
        near, far, beyond = refs[-3:]
        for bit in range(2):

            @pl.when(lax.rem(own[0] // 2, 2) == bit)
            def _(bit=bit):
                for place, out in enumerate((near, far, beyond)):
                    total = wide(kept_ref[place])
                    if 0 <= place - bit < got_ref.shape[0]:
                        total = total + wide(got_ref[place - bit])
                    out[...] = total.astype(out.dtype)

    return small_kernel(
        kernel, own, [kept, got], [whole_block(kept.shape), whole_block(got.shape)], [kept.shape[1:]] * 3, before, name, through,
    )


def finish(parts, own, before, name):
    count = len(parts)
    operands = [array for part in parts for array in part]
    kinds, depth, rows = operands[0].shape

    def kernel(own, *refs):
        out = refs[-1]
        for index in range(count):
            near, far, beyond = refs[3 * index : 3 * index + 3]
            for kind in range(kinds):
                out[index, kind] = (wide(near[kind]) + wide(far[kind]) + wide(beyond[kind])).T.astype(out.dtype)

    return small_kernel(
        kernel, own, operands, [whole_block(part.shape) for part in operands],
        [(count, kinds, rows, depth)], before, name,
    )[0]


def body(queries, key_vectors, value_vectors, output_gradient, doc_lengths):
    own = lax.axis_index("ctx")
    own_info = own.reshape(1).astype(jnp.int32)
    local = key_vectors.shape[0]
    all_groups = key_vectors.shape[1] // HEAD_SIZE
    tp_count = lax.axis_size("tp")
    groups = all_groups // tp_count
    tp_own = lax.axis_index("tp")
    tp_info = tp_own.reshape(1).astype(jnp.int32)

    middle = (groups + 1) // 2
    bounds = [(0, middle)] + ([(middle, groups)] if groups > 1 else [])
    packed = pack_for_tp(key_vectors, value_vectors, groups, tp_info)
    received = tp_received(lambda place, step: packed[step - 1])
    chunks = join_tokens(key_vectors, value_vectors, received, groups, bounds, tp_info)
    evens = [even_window(chunk) for chunk in chunks]
    x_sent = [
        for_x_swap(part, own_info, [other[1] for other in evens[1:]] if chunk == 0 else [], f"x_swap_{chunk}")
        for chunk, part in enumerate(evens)
    ]
    windows = [whole_window(evens[0], x_sent[0], own_info, x_sent[1:], "core_swap_0")]
    buffers = ()
    results, got, folded, sums, parts = [], [], [], [], []

    def fold_next_cores(before):
        group = len(folded)
        folded.append(fold_cores(results[group][2], got[group], own_info, before, f"fold_cores_{group}"))

    def fold_next_x(before, through=()):
        group = len(sums)
        near, far, beyond, *handed = fold_x(*folded[group], own_info, before, f"fold_x_{group}", through)
        sums.append(near)
        parts.append((near, shifted(far, -(WINDOW // 2)), shifted(beyond, -WINDOW)))
        return handed

    for group in range(groups):
        waits = []
        if group >= 2:
            waits.append(folded[group - 2][0])
        if group >= 3:
            waits.append(sums[group - 3])
        chunk = 0 if group < middle else 1
        results.append(
            attend_group(
                group, groups, own_info, doc_lengths, queries, output_gradient,
                windows[chunk], group - bounds[chunk][0], buffers, waits,
            )
        )
        *buffers, even, odd = results[-1]
        if 3 <= groups == group + 1:
            (odd,) = fold_next_x([array for part in parts for array in part[1:]], [odd])
        got.append(swapped(odd, 1))
        if group == 0 and groups > 1:
            windows.append(whole_window(evens[1], x_sent[1], own_info, [even], "core_swap_1"))
        if group >= 1:
            fold_next_cores([even])
        if group >= 2 and group < groups - 1:
            fold_next_x([even])
    fold_next_cores([])
    while len(sums) < groups:
        fold_next_x([folded[-1][0]] if len(sums) < groups - 1 else [])

    def exchanged(total):
        def tokens_of(place, step=0):
            return lax.dynamic_slice_in_dim(total, place * local, local, total.ndim - 2)

        return in_tp_order(tokens_of(tp_own), tp_received(tokens_of))

    if groups > 1:
        early = exchanged(finish(parts[:-1], own_info, [sums[-1]], "finish_early"))
        late = exchanged(finish(parts[-1:], own_info, [], "finish_late"))
        ordered = [[*(part[group] for group in range(groups - 1)), last[0]] for part, last in zip(early, late)]
    else:
        ordered = [[part[0]] for part in exchanged(finish(parts, own_info, [], "finish_late"))]

    def output(which):
        return jnp.concatenate([part[which] for source in ordered for part in source], axis=1)

    out, dq = buffers
    return out, dq, output(0), output(1)


def solution(mesh):
    tokens = P(("ctx", "tp"), None)
    heads = P("ctx", "tp")
    return jax.shard_map(
        body,
        mesh=mesh,
        in_specs=(heads, tokens, tokens, heads, P()),
        out_specs=(heads, heads, tokens, tokens),
        check_vma=False,
    )
```

```python
import functools
import math

import jax
import jax.numpy as jnp
from jax import lax
from jax.experimental import pallas as pl
from jax.experimental.pallas import tpu as pltpu
from jax.sharding import PartitionSpec as P

HEAD_SIZE = 128
WINDOW = 8
HEADS_AT_ONCE = 4
KERNEL_VMEM = 44 * 1024 * 1024
SCORE_SCALE = 1.0 / math.sqrt(HEAD_SIZE)
LOG2E = math.log2(math.e)
MASKED = -1e30


def dot(a, b):
    return jnp.dot(a, b, preferred_element_type=jnp.float32)


def dot_rows(a, b):
    return lax.dot_general(a, b, (((1,), (1,)), ((), ())), preferred_element_type=jnp.float32)


def group_kernel(
    group, place, heads, unread, own, doc_lengths, q_hbm, g_hbm, own_hbm, far_hbm, x_hbm, c_hbm, *rest
):
    out_hbm, dq_hbm, even_hbm, odd_hbm, *scratch = rest[unread:]
    (
        q_all, q_turned, g_in, g_all, g_turned, k_win, v_win, outs, even, odd,
        bias, scores, weights, grads, highest, summed, delta, dq_acc,
        q_sems, g_sems, k_sems, v_sems, out_sems, dq_sems, grad_sems,
    ) = scratch
    rows = q_hbm.shape[0]
    at_once = min(heads, HEADS_AT_ONCE)
    repeats = 2 * rows // HEAD_SIZE
    half = WINDOW // 2
    spans = [slice(head * rows, (head + 1) * rows) for head in range(heads)]
    batches = [slice(head * rows, (head + at_once) * rows) for head in range(0, heads, at_once)]

    def columns(head):
        return pl.ds((group * heads + head) * HEAD_SIZE, HEAD_SIZE)

    q_copies = [
        pltpu.make_async_copy(q_hbm.at[:, columns(head)], q_all.at[span], q_sems.at[head])
        for head, span in enumerate(spans)
    ]
    g_copies = [
        pltpu.make_async_copy(g_hbm.at[:, columns(head)], g_in.at[span], g_sems.at[head])
        for head, span in enumerate(spans)
    ]
    out_copies = [
        pltpu.make_async_copy(outs.at[span], out_hbm.at[:, columns(head)], out_sems.at[head])
        for head, span in enumerate(spans)
    ]
    dq_copies = [
        pltpu.make_async_copy(g_in.at[span], dq_hbm.at[:, columns(head)], dq_sems.at[head])
        for head, span in enumerate(spans)
    ]
    window = [
        own_hbm, c_hbm.at[0], x_hbm.at[0], c_hbm.at[1], far_hbm, c_hbm.at[2], x_hbm.at[1], c_hbm.at[3]
    ]

    def window_copy(kind, pair, side, source):
        target, sems = (v_win.at[pair, pl.ds(side * rows, rows), pl.ds(0, HEAD_SIZE)], v_sems) if kind else (
            k_win.at[pair, pl.ds(side * rows, rows)], k_sems
        )
        block = source.at[kind, :, pl.ds(place * HEAD_SIZE, HEAD_SIZE)]
        return pltpu.make_async_copy(block, target, sems.at[2 * pair + side])

    def grad_copies(pair):
        return [
            pltpu.make_async_copy(even.at[pair], even_hbm.at[pair], grad_sems.at[2 * pair]),
            pltpu.make_async_copy(odd.at[pair], odd_hbm.at[pair], grad_sems.at[2 * pair + 1]),
        ]

    first = own[0] * rows
    doc_start = 0
    start = 0
    for doc in range(doc_lengths.shape[0]):
        doc_start = jnp.where(first >= start, start, doc_start)
        start = start + doc_lengths[doc]
    needed = jnp.clip(own[0] - doc_start // rows + 1, 1, WINDOW)
    trips = (needed + 1) // 2
    for copy in q_copies:
        copy.start()
    for kind in range(2):
        for pair in range(half):

            @pl.when(pair < trips)
            def _(kind=kind, pair=pair):
                for side in range(2):
                    window_copy(kind, pair, side, window[2 * pair + side]).start()

    for copy in g_copies:
        copy.start()
    query_pos = first + lax.broadcasted_iota(jnp.int32, (rows, HEAD_SIZE), 0)
    low = jnp.zeros((rows, HEAD_SIZE), jnp.int32)
    start = 0
    for doc in range(doc_lengths.shape[0]):
        low = jnp.where(query_pos >= start, start, low)
        start = start + doc_lengths[doc]
    v_win[:, :, HEAD_SIZE:] = jnp.ones((half, 2 * rows, HEAD_SIZE), jnp.bfloat16)

    def each_pair(step):
        def body(pair, carry):
            step(pair, False)
            return carry

        step(0, True)
        lax.fori_loop(1, trips, body, 0)

    def score_pair(pair, is_first):
        for spot in range(repeats):
            offset = 2 * pair + spot // (repeats // 2)
            key_pos = (
                first - offset * rows + spot % (repeats // 2) * HEAD_SIZE
                + lax.broadcasted_iota(jnp.int32, (rows, HEAD_SIZE), 1)
            )
            allowed = (key_pos >= low) & (key_pos <= query_pos)
            bias[:, spot * HEAD_SIZE : (spot + 1) * HEAD_SIZE] = jnp.where(allowed, 0.0, MASKED)
        for side in range(2):
            window_copy(0, pair, side, own_hbm).wait()
        for batch in batches:
            part = dot_rows(q_all[batch, :], k_win[pair])
            for head in range(at_once):
                here = slice(batch.start + head * rows, batch.start + (head + 1) * rows)
                piece = part[head * rows : (head + 1) * rows] * (SCORE_SCALE * LOG2E) + bias[...]
                scores[pair, here, :] = piece
                pieces = [piece[:, spot * HEAD_SIZE : (spot + 1) * HEAD_SIZE] for spot in range(repeats)]
                most = functools.reduce(jnp.maximum, pieces)
                highest[here, :] = most if is_first else jnp.maximum(highest[here, :], most)

    for head, (copy, span) in enumerate(zip(q_copies, spans)):
        copy.wait()
        q_turned[:, span] = q_all[span, :].T
    each_pair(score_pair)
    for span in spans:
        highest[span, :] = jnp.broadcast_to(jnp.max(highest[span, :], axis=1, keepdims=True), (rows, HEAD_SIZE))

    def sum_pair(pair, is_first):
        for side in range(2):
            window_copy(1, pair, side, own_hbm).wait()
        for batch in batches:
            for head in range(at_once):
                here = slice(batch.start + head * rows, batch.start + (head + 1) * rows)
                top = jnp.concatenate([highest[here, :]] * repeats, axis=1)
                weights[pair, here, :] = jnp.exp2(scores[pair, here, :] - top).astype(jnp.bfloat16)
            part = dot(weights[pair, batch, :], v_win[pair])
            summed[batch, :] = part if is_first else summed[batch, :] + part

    each_pair(sum_pair)
    for head, span in enumerate(spans):
        g_copies[head].wait()
        inverse = 1.0 / summed[span, HEAD_SIZE:]
        output = (summed[span, :HEAD_SIZE] * inverse).astype(jnp.bfloat16)
        outs[span, :] = output
        out_copies[head].start()
        scaled = (g_in[span, :].astype(jnp.float32) * inverse).astype(jnp.bfloat16)
        g_all[span, :] = scaled
        g_turned[:, span] = scaled.T
        terms = output.astype(jnp.float32) * scaled.astype(jnp.float32)
        upper = terms.astype(jnp.bfloat16)
        grads[span, :HEAD_SIZE] = upper
        grads[span, HEAD_SIZE : 2 * HEAD_SIZE] = (terms - upper.astype(jnp.float32)).astype(jnp.bfloat16)
    delta[...] = dot(grads[:, : 2 * HEAD_SIZE], jnp.ones((2 * HEAD_SIZE, HEAD_SIZE), jnp.bfloat16))

    def grad_pair(pair, is_first):
        for batch in batches:
            part = dot_rows(g_all[batch, :], v_win[pair, :, :HEAD_SIZE])
            for head in range(at_once):
                here = slice(batch.start + head * rows, batch.start + (head + 1) * rows)
                piece = part[head * rows : (head + 1) * rows] - jnp.concatenate([delta[here, :]] * repeats, axis=1)
                grads[here, :] = (weights[pair, here, :].astype(jnp.float32) * piece).astype(jnp.bfloat16)
            part = dot(grads[batch, :], k_win[pair])
            dq_acc[batch, :] = part if is_first else dq_acc[batch, :] + part
        dk = (dot(q_turned[...], grads[...]) * SCORE_SCALE).astype(jnp.bfloat16)
        dv = dot(g_turned[...], weights[pair]).astype(jnp.bfloat16)
        even[pair, 0] = dk[:, :rows]
        even[pair, 1] = dv[:, :rows]
        odd[pair, 0] = dk[:, rows:]
        odd[pair, 1] = dv[:, rows:]
        for copy in grad_copies(pair):
            copy.start()

    each_pair(grad_pair)

    def clear_pair(pair, carry):
        even[pair] = jnp.zeros(even.shape[1:], jnp.bfloat16)
        odd[pair] = jnp.zeros(odd.shape[1:], jnp.bfloat16)
        for copy in grad_copies(pair):
            copy.start()
        return carry

    lax.fori_loop(trips, half, clear_pair, 0)
    for head, span in enumerate(spans):
        g_in[span, :] = (dq_acc[span, :] * SCORE_SCALE).astype(jnp.bfloat16)
        dq_copies[head].start()
    for copy in out_copies + [copy for pair in range(half) for copy in grad_copies(pair)] + dq_copies:
        copy.wait()


def attend_group(
    group, groups, own, doc_lengths, queries, gradient, window, place, buffers, before
):
    rows, width = queries.shape
    columns = width // groups
    heads = columns // HEAD_SIZE
    keys = WINDOW * rows
    stacked = heads * rows
    half = WINDOW // 2
    grads = jax.ShapeDtypeStruct((half, 2, HEAD_SIZE, rows), jnp.bfloat16)
    unread = len(buffers) + len(before)
    anywhere = pl.BlockSpec(memory_space=pl.ANY)
    short = lambda *shape: pltpu.VMEM(shape, jnp.bfloat16)
    full = lambda *shape: pltpu.VMEM(shape, jnp.float32)
    sems = lambda count: pltpu.SemaphoreType.DMA((count,))
    return pl.pallas_call(
        functools.partial(group_kernel, group, place, heads, unread),
        grid_spec=pltpu.PrefetchScalarGridSpec(
            num_scalar_prefetch=2,
            grid=(1,),
            in_specs=[anywhere] * (6 + unread),
            out_specs=[anywhere] * 4,
            scratch_shapes=[
                short(stacked, HEAD_SIZE),
                short(HEAD_SIZE, stacked),
                short(stacked, HEAD_SIZE),
                short(stacked, HEAD_SIZE),
                short(HEAD_SIZE, stacked),
                short(half, 2 * rows, HEAD_SIZE),
                short(half, 2 * rows, 2 * HEAD_SIZE),
                short(stacked, HEAD_SIZE),
                short(*grads.shape),
                short(*grads.shape),
                full(rows, 2 * rows),
                full(half, stacked, 2 * rows),
                short(half, stacked, 2 * rows),
                short(stacked, 2 * rows),
                full(stacked, HEAD_SIZE),
                full(stacked, 2 * HEAD_SIZE),
                full(stacked, HEAD_SIZE),
                full(stacked, HEAD_SIZE),
                sems(heads), sems(heads), sems(WINDOW), sems(WINDOW), sems(heads), sems(heads), sems(WINDOW),
            ],
        ),
        out_shape=[
            jax.ShapeDtypeStruct(queries.shape, jnp.bfloat16),
            jax.ShapeDtypeStruct(queries.shape, jnp.bfloat16),
            grads,
            grads,
        ],
        input_output_aliases={8 + number: number for number in range(len(buffers))},
        compiler_params=pltpu.CompilerParams(vmem_limit_bytes=KERNEL_VMEM),
        cost_estimate=pl.CostEstimate(
            flops=4 * 6 * 2 * heads * rows * keys * HEAD_SIZE,
            bytes_accessed=8 * rows * columns + 8 * keys * HEAD_SIZE,
            transcendentals=heads * rows * keys,
        ),
        name=f"attend_group_{group}",
    )(own, doc_lengths, queries, gradient, *window, *buffers, *before)


def shifted(value, steps):
    count = lax.axis_size("ctx")
    sources = range(max(0, -steps), min(count, count - steps))
    return lax.ppermute(value, "ctx", [(source, source + steps) for source in sources])


def swapped(value, bit):
    return lax.ppermute(value, "ctx", [(place, place ^ bit) for place in range(lax.axis_size("ctx"))])


def tp_received(block_for):
    count = lax.axis_size("tp")
    own = lax.axis_index("tp")
    received = []
    for step in range(1, count):
        sent = block_for(lax.rem(own + step, count), step)
        received.append(lax.ppermute(sent, "tp", [(place, (place + step) % count) for place in range(count)]))
    return received


def in_tp_order(mine, received):
    count = lax.axis_size("tp")
    own = lax.axis_index("tp")
    parts = [mine, *received]
    ordered = []
    for place in range(count):
        part = parts[0]
        for step in range(1, count):
            part = jnp.where(lax.rem(own - step + count, count) == place, parts[step], part)
        ordered.append(part)
    return ordered


def whole_block(shape):
    return pl.BlockSpec(shape, lambda i, *_: (0,) * len(shape))


def small_kernel(kernel, scalars, operands, specs, outs, before, name, through=()):
    if through:
        inner, handed = kernel, len(through)
        kernel = lambda *refs: inner(*refs[:-handed])
    first = 1 + len(operands) + len(before)
    return pl.pallas_call(
        kernel,
        grid_spec=pltpu.PrefetchScalarGridSpec(
            num_scalar_prefetch=1,
            grid=(1,),
            in_specs=specs + [pl.BlockSpec(memory_space=pl.ANY)] * (len(before) + len(through)),
            out_specs=[whole_block(shape) for shape in outs] + [pl.BlockSpec(memory_space=pl.ANY)] * len(through),
        ),
        out_shape=[jax.ShapeDtypeStruct(shape, jnp.bfloat16) for shape in outs]
        + [jax.ShapeDtypeStruct(part.shape, part.dtype) for part in through],
        input_output_aliases={first + number: len(outs) + number for number in range(len(through))},
        compiler_params=pltpu.CompilerParams(vmem_limit_bytes=32 * 1024 * 1024),
        name=name,
    )(scalars, *operands, *before, *through)


def pack_for_tp(key_vectors, value_vectors, groups, tp_own):
    count = lax.axis_size("tp")
    local = key_vectors.shape[0]
    columns = groups * HEAD_SIZE

    def kernel(own, key_hbm, value_hbm, *refs):
        outs, sems = refs[:-1], refs[-1]
        copies = []
        for step, out in enumerate(outs, 1):
            block = pl.ds(pl.multiple_of(lax.rem(own[0] + step, count) * columns, HEAD_SIZE), columns)
            for kind, source in enumerate((key_hbm, value_hbm)):
                sem = sems.at[2 * (step - 1) + kind]
                copies.append(pltpu.make_async_copy(source.at[:, block], out.at[kind], sem))
        for copy in copies:
            copy.start()
        for copy in copies:
            copy.wait()

    shape = (2, local, columns)
    return pl.pallas_call(
        kernel,
        grid_spec=pltpu.PrefetchScalarGridSpec(
            num_scalar_prefetch=1,
            grid=(1,),
            in_specs=[pl.BlockSpec(memory_space=pltpu.HBM)] * 2,
            out_specs=[whole_block(shape)] * (count - 1),
            scratch_shapes=[pltpu.SemaphoreType.DMA((2 * (count - 1),))],
        ),
        out_shape=[jax.ShapeDtypeStruct(shape, jnp.bfloat16)] * (count - 1),
        name="pack_for_tp",
    )(tp_own, key_vectors, value_vectors)


def join_tokens(key_vectors, value_vectors, received, groups, bounds, tp_own):
    count = lax.axis_size("tp")
    local = key_vectors.shape[0]
    block = pl.BlockSpec((local, groups * HEAD_SIZE), lambda i, own: (0, own[0]))

    def kernel(own, key, value, *refs):
        parts, outs = refs[: count - 1], refs[count - 1 :]
        for (first, last), out in zip(bounds, outs):
            columns = slice(first * HEAD_SIZE, last * HEAD_SIZE)
            here = pl.ds(pl.multiple_of(own[0] * local, local), local)
            out[0, here, :] = key[:, columns]
            out[1, here, :] = value[:, columns]
            for step in range(1, count):
                source = lax.rem(own[0] - step + count, count)
                rows = pl.ds(pl.multiple_of(source * local, local), local)
                out[:, rows, :] = parts[step - 1][:, :, columns]

    return small_kernel(
        kernel, tp_own, [key_vectors, value_vectors, *received],
        [block, block] + [whole_block(part.shape) for part in received],
        [(2, local * count, (last - first) * HEAD_SIZE) for first, last in bounds], [], "join_tokens",
    )


def even_window(own_pair):
    far = shifted(own_pair, WINDOW // 2)
    return own_pair, far, shifted(far, WINDOW // 2)


def for_x_swap(evens, own, before, name):
    def kernel(own, *refs):
        out = refs[-1]
        for bit in range(2):

            @pl.when(lax.rem(own[0] // 2, 2) == bit)
            def _(bit=bit):
                for place in range(2):
                    out[place] = refs[place + bit][...]

    return small_kernel(
        kernel, own, evens, [whole_block(part.shape) for part in evens], [(2, *evens[0].shape)], before, name
    )[0]


def whole_window(evens, x_sent, own, before, name):
    own_pair, far, beyond = evens
    x_pairs = swapped(x_sent, 2)
    half = WINDOW // 2

    def kernel(own, own_ref, far_ref, beyond_ref, x_ref, *refs):
        out = refs[-1]
        evens = [own_ref, x_ref.at[0], far_ref, x_ref.at[1], beyond_ref]
        low_c = lax.rem(own[0], 2)
        for bit in range(2):

            @pl.when(low_c == bit)
            def _(bit=bit):
                for place in range(half):
                    out[place] = evens[place + bit][...]

    operands = [own_pair, far, beyond, x_pairs]
    (c_sent,) = small_kernel(
        kernel, own, operands, [whole_block(part.shape) for part in operands],
        [(half, *own_pair.shape)], before, name,
    )
    return own_pair, far, x_pairs, swapped(c_sent, 1)


def wide(part):
    return part.astype(jnp.float32)


def fold_cores(even, got, own, before, name):
    half = WINDOW // 2

    def kernel(own, even_ref, got_ref, *refs):
        sent, kept = refs[-2:]
        for bit in range(2):

            @pl.when(lax.rem(own[0], 2) == bit)
            def _(bit=bit):
                for place in range(half + 1):
                    out = sent.at[place // 2] if place % 2 else kept.at[place // 2]
                    total = None
                    if place < half:
                        total = wide(even_ref[place])
                    if 0 <= place - bit < half:
                        more = wide(got_ref[place - bit])
                        total = more if total is None else total + more
                    out[...] = jnp.zeros(out.shape, out.dtype) if total is None else total.astype(out.dtype)

    shape = even.shape[1:]
    return small_kernel(
        kernel, own, [even, got], [whole_block(even.shape)] * 2,
        [(half // 2, *shape), (half // 2 + 1, *shape)], before, name,
    )


def fold_x(sent, kept, own, before, name, through=()):
    got = swapped(sent, 2)

    def kernel(own, kept_ref, got_ref, *refs):
        near, far, beyond = refs[-3:]
        for bit in range(2):

            @pl.when(lax.rem(own[0] // 2, 2) == bit)
            def _(bit=bit):
                for place, out in enumerate((near, far, beyond)):
                    total = wide(kept_ref[place])
                    if 0 <= place - bit < got_ref.shape[0]:
                        total = total + wide(got_ref[place - bit])
                    out[...] = total.astype(out.dtype)

    return small_kernel(
        kernel, own, [kept, got], [whole_block(kept.shape), whole_block(got.shape)], [kept.shape[1:]] * 3, before, name, through,
    )


def finish(parts, own, before, name):
    count = len(parts)
    operands = [array for part in parts for array in part]
    kinds, depth, rows = operands[0].shape

    def kernel(own, *refs):
        out = refs[-1]
        for index in range(count):
            near, far, beyond = refs[3 * index : 3 * index + 3]
            for kind in range(kinds):
                out[index, kind] = (wide(near[kind]) + wide(far[kind]) + wide(beyond[kind])).T.astype(out.dtype)

    return small_kernel(
        kernel, own, operands, [whole_block(part.shape) for part in operands],
        [(count, kinds, rows, depth)], before, name,
    )[0]


def body(queries, key_vectors, value_vectors, output_gradient, doc_lengths):
    own = lax.axis_index("ctx")
    own_info = own.reshape(1).astype(jnp.int32)
    local = key_vectors.shape[0]
    all_groups = key_vectors.shape[1] // HEAD_SIZE
    tp_count = lax.axis_size("tp")
    groups = all_groups // tp_count
    tp_own = lax.axis_index("tp")
    tp_info = tp_own.reshape(1).astype(jnp.int32)

    middle = (groups + 1) // 2
    bounds = [(0, middle)] + ([(middle, groups)] if groups > 1 else [])
    packed = pack_for_tp(key_vectors, value_vectors, groups, tp_info)
    received = tp_received(lambda place, step: packed[step - 1])
    chunks = join_tokens(key_vectors, value_vectors, received, groups, bounds, tp_info)
    evens = [even_window(chunk) for chunk in chunks]
    x_sent = [
        for_x_swap(part, own_info, [other[1] for other in evens[1:]] if chunk == 0 else [], f"x_swap_{chunk}")
        for chunk, part in enumerate(evens)
    ]
    windows = [whole_window(evens[0], x_sent[0], own_info, x_sent[1:], "core_swap_0")]
    buffers = ()
    results, got, folded, sums, parts = [], [], [], [], []

    def fold_next_cores(before):
        group = len(folded)
        folded.append(fold_cores(results[group][2], got[group], own_info, before, f"fold_cores_{group}"))

    def fold_next_x(before, through=()):
        group = len(sums)
        near, far, beyond, *handed = fold_x(*folded[group], own_info, before, f"fold_x_{group}", through)
        sums.append(near)
        parts.append((near, shifted(far, -(WINDOW // 2)), shifted(beyond, -WINDOW)))
        return handed

    for group in range(groups):
        waits = []
        if group >= 2:
            waits.append(folded[group - 2][0])
        if group >= 3:
            waits.append(sums[group - 3])
        chunk = 0 if group < middle else 1
        results.append(
            attend_group(
                group, groups, own_info, doc_lengths, queries, output_gradient,
                windows[chunk], group - bounds[chunk][0], buffers, waits,
            )
        )
        *buffers, even, odd = results[-1]
        if 3 <= groups == group + 1:
            (odd,) = fold_next_x([array for part in parts for array in part[1:]], [odd])
        got.append(swapped(odd, 1))
        if group == 0 and groups > 1:
            windows.append(whole_window(evens[1], x_sent[1], own_info, [even], "core_swap_1"))
        if group >= 1:
            fold_next_cores([even])
        if group >= 2 and group < groups - 1:
            fold_next_x([even])
    fold_next_cores([])
    while len(sums) < groups:
        fold_next_x([folded[-1][0]] if len(sums) < groups - 1 else [])

    def exchanged(total):
        def tokens_of(place, step=0):
            return lax.dynamic_slice_in_dim(total, place * local, local, total.ndim - 2)

        return in_tp_order(tokens_of(tp_own), tp_received(tokens_of))

    if groups > 1:
        early = exchanged(finish(parts[:-1], own_info, [sums[-1]], "finish_early"))
        late = exchanged(finish(parts[-1:], own_info, [], "finish_late"))
        ordered = [[*(part[group] for group in range(groups - 1)), last[0]] for part, last in zip(early, late)]
    else:
        ordered = [[part[0]] for part in exchanged(finish(parts, own_info, [], "finish_late"))]

    def output(which):
        return jnp.concatenate([part[which] for source in ordered for part in source], axis=1)

    out, dq = buffers
    return out, dq, output(0), output(1)


def solution(mesh):
    tokens = P(("ctx", "tp"), None)
    heads = P("ctx", "tp")
    return jax.shard_map(
        body,
        mesh=mesh,
        in_specs=(heads, tokens, tokens, heads, P()),
        out_specs=(heads, heads, tokens, tokens),
        check_vma=False,
    )
```

```python
import functools
import math

import jax
import jax.numpy as jnp
from jax import lax
from jax.experimental import pallas as pl
from jax.experimental.pallas import tpu as pltpu
from jax.sharding import PartitionSpec as P

HEAD_SIZE = 128
WINDOW = 8
HEADS_AT_ONCE = 4
KERNEL_VMEM = 44 * 1024 * 1024
SCORE_SCALE = 1.0 / math.sqrt(HEAD_SIZE)
LOG2E = math.log2(math.e)
MASKED = -1e30


def dot(a, b):
    return jnp.dot(a, b, preferred_element_type=jnp.float32)


def dot_rows(a, b):
    return lax.dot_general(a, b, (((1,), (1,)), ((), ())), preferred_element_type=jnp.float32)


def group_kernel(
    group, place, heads, unread, own, doc_lengths, q_hbm, g_hbm, own_hbm, far_hbm, x_hbm, c_hbm, *rest
):
    out_hbm, dq_hbm, even_hbm, odd_hbm, *scratch = rest[unread:]
    (
        q_all, q_turned, g_in, g_all, g_turned, k_win, v_win, outs, even, odd,
        bias, scores, weights, grads, highest, summed, delta, dq_acc,
        q_sems, g_sems, k_sems, v_sems, out_sems, dq_sems, grad_sems,
    ) = scratch
    rows = q_hbm.shape[0]
    at_once = min(heads, HEADS_AT_ONCE)
    repeats = 2 * rows // HEAD_SIZE
    half = WINDOW // 2
    spans = [slice(head * rows, (head + 1) * rows) for head in range(heads)]
    batches = [slice(head * rows, (head + at_once) * rows) for head in range(0, heads, at_once)]

    def columns(head):
        return pl.ds((group * heads + head) * HEAD_SIZE, HEAD_SIZE)

    q_copies = [
        pltpu.make_async_copy(q_hbm.at[:, columns(head)], q_all.at[span], q_sems.at[head])
        for head, span in enumerate(spans)
    ]
    g_copies = [
        pltpu.make_async_copy(g_hbm.at[:, columns(head)], g_in.at[span], g_sems.at[head])
        for head, span in enumerate(spans)
    ]
    out_copies = [
        pltpu.make_async_copy(outs.at[span], out_hbm.at[:, columns(head)], out_sems.at[head])
        for head, span in enumerate(spans)
    ]
    dq_copies = [
        pltpu.make_async_copy(g_in.at[span], dq_hbm.at[:, columns(head)], dq_sems.at[head])
        for head, span in enumerate(spans)
    ]
    window = [
        own_hbm, c_hbm.at[0], x_hbm.at[0], c_hbm.at[1], far_hbm, c_hbm.at[2], x_hbm.at[1], c_hbm.at[3]
    ]

    def window_copy(kind, pair, side, source):
        target, sems = (v_win.at[pair, pl.ds(side * rows, rows), pl.ds(0, HEAD_SIZE)], v_sems) if kind else (
            k_win.at[pair, pl.ds(side * rows, rows)], k_sems
        )
        block = source.at[kind, :, pl.ds(place * HEAD_SIZE, HEAD_SIZE)]
        return pltpu.make_async_copy(block, target, sems.at[2 * pair + side])

    def grad_copies(pair):
        return [
            pltpu.make_async_copy(even.at[pair], even_hbm.at[pair], grad_sems.at[2 * pair]),
            pltpu.make_async_copy(odd.at[pair], odd_hbm.at[pair], grad_sems.at[2 * pair + 1]),
        ]

    first = own[0] * rows
    doc_start = 0
    start = 0
    for doc in range(doc_lengths.shape[0]):
        doc_start = jnp.where(first >= start, start, doc_start)
        start = start + doc_lengths[doc]
    needed = jnp.clip(own[0] - doc_start // rows + 1, 1, WINDOW)
    trips = (needed + 1) // 2
    for copy in q_copies:
        copy.start()
    for kind in range(2):
        for pair in range(half):

            @pl.when(pair < trips)
            def _(kind=kind, pair=pair):
                for side in range(2):
                    window_copy(kind, pair, side, window[2 * pair + side]).start()

    for copy in g_copies:
        copy.start()
    query_pos = first + lax.broadcasted_iota(jnp.int32, (rows, HEAD_SIZE), 0)
    low = jnp.zeros((rows, HEAD_SIZE), jnp.int32)
    start = 0
    for doc in range(doc_lengths.shape[0]):
        low = jnp.where(query_pos >= start, start, low)
        start = start + doc_lengths[doc]
    v_win[:, :, HEAD_SIZE:] = jnp.ones((half, 2 * rows, HEAD_SIZE), jnp.bfloat16)

    def each_pair(step):
        def body(pair, carry):
            step(pair, False)
            return carry

        step(0, True)
        lax.fori_loop(1, trips, body, 0)

    def score_pair(pair, is_first):
        for spot in range(repeats):
            offset = 2 * pair + spot // (repeats // 2)
            key_pos = (
                first - offset * rows + spot % (repeats // 2) * HEAD_SIZE
                + lax.broadcasted_iota(jnp.int32, (rows, HEAD_SIZE), 1)
            )
            allowed = (key_pos >= low) & (key_pos <= query_pos)
            bias[:, spot * HEAD_SIZE : (spot + 1) * HEAD_SIZE] = jnp.where(allowed, 0.0, MASKED)
        for side in range(2):
            window_copy(0, pair, side, own_hbm).wait()
        for batch in batches:
            part = dot_rows(q_all[batch, :], k_win[pair])
            for head in range(at_once):
                here = slice(batch.start + head * rows, batch.start + (head + 1) * rows)
                if is_first:
                    q_turned[:, here] = q_all[here, :].T
                piece = part[head * rows : (head + 1) * rows] * (SCORE_SCALE * LOG2E) + bias[...]
                scores[pair, here, :] = piece
                pieces = [piece[:, spot * HEAD_SIZE : (spot + 1) * HEAD_SIZE] for spot in range(repeats)]
                most = functools.reduce(jnp.maximum, pieces)
                highest[here, :] = most if is_first else jnp.maximum(highest[here, :], most)

    for copy in q_copies:
        copy.wait()
    each_pair(score_pair)

    def sum_pair(pair, is_first):
        for side in range(2):
            window_copy(1, pair, side, own_hbm).wait()
        for batch in batches:
            for head in range(at_once):
                here = slice(batch.start + head * rows, batch.start + (head + 1) * rows)
                top = highest[here, :]
                if is_first:
                    top = jnp.broadcast_to(jnp.max(top, axis=1, keepdims=True), (rows, HEAD_SIZE))
                    highest[here, :] = top
                top = jnp.concatenate([top] * repeats, axis=1)
                weights[pair, here, :] = jnp.exp2(scores[pair, here, :] - top).astype(jnp.bfloat16)
            part = dot(weights[pair, batch, :], v_win[pair])
            summed[batch, :] = part if is_first else summed[batch, :] + part

    each_pair(sum_pair)

    def close_head(head):
        span = spans[head]
        inverse = 1.0 / summed[span, HEAD_SIZE:]
        output = (summed[span, :HEAD_SIZE] * inverse).astype(jnp.bfloat16)
        outs[span, :] = output
        scaled = (g_in[span, :].astype(jnp.float32) * inverse).astype(jnp.bfloat16)
        g_all[span, :] = scaled
        g_turned[:, span] = scaled.T
        terms = output.astype(jnp.float32) * scaled.astype(jnp.float32)
        upper = terms.astype(jnp.bfloat16)
        grads[span, :HEAD_SIZE] = upper
        grads[span, HEAD_SIZE : 2 * HEAD_SIZE] = (terms - upper.astype(jnp.float32)).astype(jnp.bfloat16)

    for copy in g_copies:
        copy.wait()
    ones = jnp.ones((2 * HEAD_SIZE, HEAD_SIZE), jnp.bfloat16)

    def grad_pair(pair, is_first):
        for number, batch in enumerate(batches):
            if is_first:
                for head in range(number * at_once, (number + 1) * at_once):
                    close_head(head)
                delta[batch, :] = dot(grads[batch, : 2 * HEAD_SIZE], ones)
            part = dot_rows(g_all[batch, :], v_win[pair, :, :HEAD_SIZE])
            for head in range(at_once):
                here = slice(batch.start + head * rows, batch.start + (head + 1) * rows)
                piece = part[head * rows : (head + 1) * rows] - jnp.concatenate([delta[here, :]] * repeats, axis=1)
                grads[here, :] = (weights[pair, here, :].astype(jnp.float32) * piece).astype(jnp.bfloat16)
            part = dot(grads[batch, :], k_win[pair])
            dq_acc[batch, :] = part if is_first else dq_acc[batch, :] + part
        dk = (dot(q_turned[...], grads[...]) * SCORE_SCALE).astype(jnp.bfloat16)
        dv = dot(g_turned[...], weights[pair]).astype(jnp.bfloat16)
        even[pair, 0] = dk[:, :rows]
        even[pair, 1] = dv[:, :rows]
        odd[pair, 0] = dk[:, rows:]
        odd[pair, 1] = dv[:, rows:]
        for copy in grad_copies(pair) + (out_copies if is_first else []):
            copy.start()

    each_pair(grad_pair)

    def clear_pair(pair, carry):
        even[pair] = jnp.zeros(even.shape[1:], jnp.bfloat16)
        odd[pair] = jnp.zeros(odd.shape[1:], jnp.bfloat16)
        for copy in grad_copies(pair):
            copy.start()
        return carry

    lax.fori_loop(trips, half, clear_pair, 0)
    for head, span in enumerate(spans):
        g_in[span, :] = (dq_acc[span, :] * SCORE_SCALE).astype(jnp.bfloat16)
        dq_copies[head].start()
    for copy in out_copies + [copy for pair in range(half) for copy in grad_copies(pair)] + dq_copies:
        copy.wait()


def attend_group(
    group, groups, own, doc_lengths, queries, gradient, window, place, buffers, before
):
    rows, width = queries.shape
    columns = width // groups
    heads = columns // HEAD_SIZE
    keys = WINDOW * rows
    stacked = heads * rows
    half = WINDOW // 2
    grads = jax.ShapeDtypeStruct((half, 2, HEAD_SIZE, rows), jnp.bfloat16)
    unread = len(buffers) + len(before)
    anywhere = pl.BlockSpec(memory_space=pl.ANY)
    short = lambda *shape: pltpu.VMEM(shape, jnp.bfloat16)
    full = lambda *shape: pltpu.VMEM(shape, jnp.float32)
    sems = lambda count: pltpu.SemaphoreType.DMA((count,))
    return pl.pallas_call(
        functools.partial(group_kernel, group, place, heads, unread),
        grid_spec=pltpu.PrefetchScalarGridSpec(
            num_scalar_prefetch=2,
            grid=(1,),
            in_specs=[anywhere] * (6 + unread),
            out_specs=[anywhere] * 4,
            scratch_shapes=[
                short(stacked, HEAD_SIZE),
                short(HEAD_SIZE, stacked),
                short(stacked, HEAD_SIZE),
                short(stacked, HEAD_SIZE),
                short(HEAD_SIZE, stacked),
                short(half, 2 * rows, HEAD_SIZE),
                short(half, 2 * rows, 2 * HEAD_SIZE),
                short(stacked, HEAD_SIZE),
                short(*grads.shape),
                short(*grads.shape),
                full(rows, 2 * rows),
                full(half, stacked, 2 * rows),
                short(half, stacked, 2 * rows),
                short(stacked, 2 * rows),
                full(stacked, HEAD_SIZE),
                full(stacked, 2 * HEAD_SIZE),
                full(stacked, HEAD_SIZE),
                full(stacked, HEAD_SIZE),
                sems(heads), sems(heads), sems(WINDOW), sems(WINDOW), sems(heads), sems(heads), sems(WINDOW),
            ],
        ),
        out_shape=[
            jax.ShapeDtypeStruct(queries.shape, jnp.bfloat16),
            jax.ShapeDtypeStruct(queries.shape, jnp.bfloat16),
            grads,
            grads,
        ],
        input_output_aliases={8 + number: number for number in range(len(buffers))},
        compiler_params=pltpu.CompilerParams(vmem_limit_bytes=KERNEL_VMEM),
        cost_estimate=pl.CostEstimate(
            flops=4 * 6 * 2 * heads * rows * keys * HEAD_SIZE,
            bytes_accessed=8 * rows * columns + 8 * keys * HEAD_SIZE,
            transcendentals=heads * rows * keys,
        ),
        name=f"attend_group_{group}",
    )(own, doc_lengths, queries, gradient, *window, *buffers, *before)


def shifted(value, steps):
    count = lax.axis_size("ctx")
    sources = range(max(0, -steps), min(count, count - steps))
    return lax.ppermute(value, "ctx", [(source, source + steps) for source in sources])


def swapped(value, bit):
    return lax.ppermute(value, "ctx", [(place, place ^ bit) for place in range(lax.axis_size("ctx"))])


def tp_received(block_for):
    count = lax.axis_size("tp")
    own = lax.axis_index("tp")
    received = []
    for step in range(1, count):
        sent = block_for(lax.rem(own + step, count), step)
        received.append(lax.ppermute(sent, "tp", [(place, (place + step) % count) for place in range(count)]))
    return received


def in_tp_order(mine, received):
    count = lax.axis_size("tp")
    own = lax.axis_index("tp")
    parts = [mine, *received]
    ordered = []
    for place in range(count):
        part = parts[0]
        for step in range(1, count):
            part = jnp.where(lax.rem(own - step + count, count) == place, parts[step], part)
        ordered.append(part)
    return ordered


def whole_block(shape):
    return pl.BlockSpec(shape, lambda i, *_: (0,) * len(shape))


def small_kernel(kernel, scalars, operands, specs, outs, before, name, through=()):
    if through:
        inner, handed = kernel, len(through)
        kernel = lambda *refs: inner(*refs[:-handed])
    first = 1 + len(operands) + len(before)
    return pl.pallas_call(
        kernel,
        grid_spec=pltpu.PrefetchScalarGridSpec(
            num_scalar_prefetch=1,
            grid=(1,),
            in_specs=specs + [pl.BlockSpec(memory_space=pl.ANY)] * (len(before) + len(through)),
            out_specs=[whole_block(shape) for shape in outs] + [pl.BlockSpec(memory_space=pl.ANY)] * len(through),
        ),
        out_shape=[jax.ShapeDtypeStruct(shape, jnp.bfloat16) for shape in outs]
        + [jax.ShapeDtypeStruct(part.shape, part.dtype) for part in through],
        input_output_aliases={first + number: len(outs) + number for number in range(len(through))},
        compiler_params=pltpu.CompilerParams(vmem_limit_bytes=32 * 1024 * 1024),
        name=name,
    )(scalars, *operands, *before, *through)


def pack_for_tp(key_vectors, value_vectors, groups, tp_own):
    count = lax.axis_size("tp")
    local = key_vectors.shape[0]
    columns = groups * HEAD_SIZE

    def kernel(own, key_hbm, value_hbm, *refs):
        outs, sems = refs[:-1], refs[-1]
        copies = []
        for step, out in enumerate(outs):
            block = pl.ds(pl.multiple_of(lax.rem(own[0] + step, count) * columns, HEAD_SIZE), columns)
            for kind, source in enumerate((key_hbm, value_hbm)):
                copies.append(pltpu.make_async_copy(source.at[:, block], out.at[kind], sems.at[2 * step + kind]))
        for copy in copies:
            copy.start()
        for copy in copies:
            copy.wait()

    shape = (2, local, columns)
    return pl.pallas_call(
        kernel,
        grid_spec=pltpu.PrefetchScalarGridSpec(
            num_scalar_prefetch=1,
            grid=(1,),
            in_specs=[pl.BlockSpec(memory_space=pltpu.HBM)] * 2,
            out_specs=[whole_block(shape)] * count,
            scratch_shapes=[pltpu.SemaphoreType.DMA((2 * count,))],
        ),
        out_shape=[jax.ShapeDtypeStruct(shape, jnp.bfloat16)] * count,
        name="pack_for_tp",
    )(tp_own, key_vectors, value_vectors)


def join_tokens(parts, bounds, tp_own):
    count = len(parts)
    local = parts[0].shape[1]

    def kernel(own, *refs):
        parts, outs = refs[:count], refs[count:]
        for (first, last), out in zip(bounds, outs):
            columns = slice(first * HEAD_SIZE, last * HEAD_SIZE)
            for step in range(count):
                source = lax.rem(own[0] - step + count, count)
                rows = pl.ds(pl.multiple_of(source * local, local), local)
                out[:, rows, :] = parts[step][:, :, columns]

    return small_kernel(
        kernel, tp_own, parts, [whole_block(part.shape) for part in parts],
        [(2, local * count, (last - first) * HEAD_SIZE) for first, last in bounds], [], "join_tokens",
    )


def even_window(own_pair):
    far = shifted(own_pair, WINDOW // 2)
    return own_pair, far, shifted(far, WINDOW // 2)


def for_x_swap(evens, own, before, name):
    def kernel(own, *refs):
        out = refs[-1]
        for bit in range(2):

            @pl.when(lax.rem(own[0] // 2, 2) == bit)
            def _(bit=bit):
                for place in range(2):
                    out[place] = refs[place + bit][...]

    return small_kernel(
        kernel, own, evens, [whole_block(part.shape) for part in evens], [(2, *evens[0].shape)], before, name
    )[0]


def whole_window(evens, x_sent, own, before, name):
    own_pair, far, beyond = evens
    x_pairs = swapped(x_sent, 2)
    half = WINDOW // 2

    def kernel(own, own_ref, far_ref, beyond_ref, x_ref, *refs):
        out = refs[-1]
        evens = [own_ref, x_ref.at[0], far_ref, x_ref.at[1], beyond_ref]
        low_c = lax.rem(own[0], 2)
        for bit in range(2):

            @pl.when(low_c == bit)
            def _(bit=bit):
                for place in range(half):
                    out[place] = evens[place + bit][...]

    operands = [own_pair, far, beyond, x_pairs]
    (c_sent,) = small_kernel(
        kernel, own, operands, [whole_block(part.shape) for part in operands],
        [(half, *own_pair.shape)], before, name,
    )
    return own_pair, far, x_pairs, swapped(c_sent, 1)


def wide(part):
    return part.astype(jnp.float32)


def fold_cores(even, got, own, before, name):
    half = WINDOW // 2

    def kernel(own, even_ref, got_ref, *refs):
        sent, kept = refs[-2:]
        for bit in range(2):

            @pl.when(lax.rem(own[0], 2) == bit)
            def _(bit=bit):
                for place in range(half + 1):
                    out = sent.at[place // 2] if place % 2 else kept.at[place // 2]
                    total = None
                    if place < half:
                        total = wide(even_ref[place])
                    if 0 <= place - bit < half:
                        more = wide(got_ref[place - bit])
                        total = more if total is None else total + more
                    out[...] = jnp.zeros(out.shape, out.dtype) if total is None else total.astype(out.dtype)

    shape = even.shape[1:]
    return small_kernel(
        kernel, own, [even, got], [whole_block(even.shape)] * 2,
        [(half // 2, *shape), (half // 2 + 1, *shape)], before, name,
    )


def fold_x(sent, kept, own, before, name, through=()):
    got = swapped(sent, 2)

    def kernel(own, kept_ref, got_ref, *refs):
        near, far, beyond = refs[-3:]
        for bit in range(2):

            @pl.when(lax.rem(own[0] // 2, 2) == bit)
            def _(bit=bit):
                for place, out in enumerate((near, far, beyond)):
                    total = wide(kept_ref[place])
                    if 0 <= place - bit < got_ref.shape[0]:
                        total = total + wide(got_ref[place - bit])
                    out[...] = total.astype(out.dtype)

    return small_kernel(
        kernel, own, [kept, got], [whole_block(kept.shape), whole_block(got.shape)], [kept.shape[1:]] * 3, before, name, through,
    )


def fold_z(parts, own, before, name):
    count = len(parts)
    operands = [array for part in parts for array in part]
    shape = operands[0].shape

    def kernel(own, *refs):
        out = refs[-1]
        for index in range(count):
            out[index] = (wide(refs[2 * index][...]) + wide(refs[2 * index + 1][...])).astype(out.dtype)

    return small_kernel(
        kernel, own, operands, [whole_block(shape)] * len(operands), [(count, *shape)], before, name
    )[0]


def finish(nears, received, own, before, name):
    count = len(nears)
    kinds, depth, rows = nears[0].shape
    sizes = [part.shape[0] for part in received]

    def kernel(own, *refs):
        out = refs[-1]
        others = [ref.at[index] for ref, size in zip(refs[count:], sizes) for index in range(size)]
        for index in range(count):
            for kind in range(kinds):
                out[index, kind] = (wide(refs[index][kind]) + wide(others[index][kind])).T.astype(out.dtype)

    operands = [*nears, *received]
    return small_kernel(
        kernel, own, operands, [whole_block(part.shape) for part in operands],
        [(count, kinds, rows, depth)], before, name,
    )[0]


def body(queries, key_vectors, value_vectors, output_gradient, doc_lengths):
    own = lax.axis_index("ctx")
    own_info = own.reshape(1).astype(jnp.int32)
    local = key_vectors.shape[0]
    all_groups = key_vectors.shape[1] // HEAD_SIZE
    tp_count = lax.axis_size("tp")
    groups = all_groups // tp_count
    tp_own = lax.axis_index("tp")
    tp_info = tp_own.reshape(1).astype(jnp.int32)

    middle = (groups + 1) // 2
    bounds = [(0, middle)] + ([(middle, groups)] if groups > 1 else [])
    packed = pack_for_tp(key_vectors, value_vectors, groups, tp_info)
    received = tp_received(lambda place, step: packed[step])
    chunks = join_tokens([packed[0], *received], bounds, tp_info)
    evens = [even_window(chunk) for chunk in chunks]
    x_sent = [
        for_x_swap(part, own_info, [other[1] for other in evens[1:]] if chunk == 0 else [], f"x_swap_{chunk}")
        for chunk, part in enumerate(evens)
    ]
    windows = [whole_window(evens[0], x_sent[0], own_info, x_sent[1:], "core_swap_0")]
    buffers = ()
    results, got, folded, sums, passing = [], [], [], [], []

    def fold_next_cores(before):
        group = len(folded)
        folded.append(fold_cores(results[group][2], got[group], own_info, before, f"fold_cores_{group}"))

    def fold_next_x(before, through=()):
        group = len(sums)
        near, far, beyond, *handed = fold_x(*folded[group], own_info, before, f"fold_x_{group}", through)
        sums.append(near)
        passing.append((far, shifted(beyond, -(WINDOW // 2))))
        return handed

    for group in range(groups):
        waits = []
        if group >= 2:
            waits.append(folded[group - 2][0])
        if group >= 3:
            waits.append(sums[group - 3])
        chunk = 0 if group < middle else 1
        results.append(
            attend_group(
                group, groups, own_info, doc_lengths, queries, output_gradient,
                windows[chunk], group - bounds[chunk][0], buffers, waits,
            )
        )
        *buffers, even, odd = results[-1]
        if 3 <= groups == group + 1:
            (odd,) = fold_next_x([part[1] for part in passing], [odd])
        got.append(swapped(odd, 1))
        if group == 0 and groups > 1:
            windows.append(whole_window(evens[1], x_sent[1], own_info, [even], "core_swap_1"))
        if group >= 1:
            fold_next_cores([even])
        if group >= 2 and group < groups - 1:
            fold_next_x([even])
    fold_next_cores([])
    while len(sums) < groups:
        fold_next_x([folded[-1][0]] if len(sums) < groups - 1 else [])

    def exchanged(total):
        def tokens_of(place, step=0):
            return lax.dynamic_slice_in_dim(total, place * local, local, total.ndim - 2)

        return in_tp_order(tokens_of(tp_own), tp_received(tokens_of))

    joint = [list(range(max(1, groups - 2)))] + [[group] for group in range(max(1, groups - 2), groups)]
    sent = []
    for number, members in enumerate(joint):
        later = [sums[members[-1] + 1]] if members[-1] + 1 < groups else []
        sent.append(fold_z([passing[group] for group in members], own_info, later, f"fold_z_{number}"))
    came = [shifted(part, -(WINDOW // 2)) for part in sent]
    if groups > 1:
        early = exchanged(finish(sums[:-1], came[:-1], own_info, sent[-1:], "finish_early"))
        late = exchanged(finish(sums[-1:], came[-1:], own_info, [], "finish_late"))
        ordered = [[*(part[group] for group in range(groups - 1)), last[0]] for part, last in zip(early, late)]
    else:
        ordered = [[part[0]] for part in exchanged(finish(sums, came, own_info, [], "finish_late"))]

    def output(which):
        return jnp.concatenate([part[which] for source in ordered for part in source], axis=1)

    out, dq = buffers
    return out, dq, output(0), output(1)


def solution(mesh):
    tokens = P(("ctx", "tp"), None)
    heads = P("ctx", "tp")
    return jax.shard_map(
        body,
        mesh=mesh,
        in_specs=(heads, tokens, tokens, heads, P()),
        out_specs=(heads, heads, tokens, tokens),
        check_vma=False,
    )
```

```python
import functools
import math

import jax
import jax.numpy as jnp
from jax import lax
from jax.experimental import pallas as pl
from jax.experimental.pallas import tpu as pltpu
from jax.sharding import PartitionSpec as P

HEAD_SIZE = 128
WINDOW = 8
HEADS_AT_ONCE = 4
KERNEL_VMEM = 44 * 1024 * 1024
SCORE_SCALE = 1.0 / math.sqrt(HEAD_SIZE)
LOG2E = math.log2(math.e)
MASKED = -1e30


def dot(a, b):
    return jnp.dot(a, b, preferred_element_type=jnp.float32)


def dot_rows(a, b):
    return lax.dot_general(a, b, (((1,), (1,)), ((), ())), preferred_element_type=jnp.float32)


def group_kernel(
    group, place, heads, unread, own, doc_lengths, q_hbm, g_hbm, own_hbm, far_hbm, x_hbm, c_hbm, *rest
):
    out_hbm, dq_hbm, even_hbm, odd_hbm, *scratch = rest[unread:]
    (
        q_all, q_turned, g_in, g_all, g_turned, k_win, v_win, outs, even, odd,
        bias, scores, weights, grads, highest, summed, delta, dq_acc,
        q_sems, g_sems, k_sems, v_sems, out_sems, dq_sems, grad_sems,
    ) = scratch
    rows = q_hbm.shape[0]
    at_once = min(heads, HEADS_AT_ONCE)
    repeats = 2 * rows // HEAD_SIZE
    half = WINDOW // 2
    spans = [slice(head * rows, (head + 1) * rows) for head in range(heads)]
    batches = [slice(head * rows, (head + at_once) * rows) for head in range(0, heads, at_once)]

    def columns(head):
        return pl.ds((group * heads + head) * HEAD_SIZE, HEAD_SIZE)

    q_copies = [
        pltpu.make_async_copy(q_hbm.at[:, columns(head)], q_all.at[span], q_sems.at[head])
        for head, span in enumerate(spans)
    ]
    g_copies = [
        pltpu.make_async_copy(g_hbm.at[:, columns(head)], g_in.at[span], g_sems.at[head])
        for head, span in enumerate(spans)
    ]
    out_copies = [
        pltpu.make_async_copy(outs.at[span], out_hbm.at[:, columns(head)], out_sems.at[head])
        for head, span in enumerate(spans)
    ]
    dq_copies = [
        pltpu.make_async_copy(g_in.at[span], dq_hbm.at[:, columns(head)], dq_sems.at[head])
        for head, span in enumerate(spans)
    ]
    window = [
        own_hbm, c_hbm.at[0], x_hbm.at[0], c_hbm.at[1], far_hbm, c_hbm.at[2], x_hbm.at[1], c_hbm.at[3]
    ]

    def window_copy(kind, pair, side, source):
        target, sems = (v_win.at[pair, pl.ds(side * rows, rows), pl.ds(0, HEAD_SIZE)], v_sems) if kind else (
            k_win.at[pair, pl.ds(side * rows, rows)], k_sems
        )
        block = source.at[kind, :, pl.ds(place * HEAD_SIZE, HEAD_SIZE)]
        return pltpu.make_async_copy(block, target, sems.at[2 * pair + side])

    def grad_copies(pair):
        return [
            pltpu.make_async_copy(even.at[pair], even_hbm.at[pair], grad_sems.at[2 * pair]),
            pltpu.make_async_copy(odd.at[pair], odd_hbm.at[pair], grad_sems.at[2 * pair + 1]),
        ]

    first = own[0] * rows
    doc_start = 0
    start = 0
    for doc in range(doc_lengths.shape[0]):
        doc_start = jnp.where(first >= start, start, doc_start)
        start = start + doc_lengths[doc]
    needed = jnp.clip(own[0] - doc_start // rows + 1, 1, WINDOW)
    trips = (needed + 1) // 2
    for copy in q_copies:
        copy.start()
    for kind in range(2):
        for pair in range(half):

            @pl.when(pair < trips)
            def _(kind=kind, pair=pair):
                for side in range(2):
                    window_copy(kind, pair, side, window[2 * pair + side]).start()

    for copy in g_copies:
        copy.start()
    query_pos = first + lax.broadcasted_iota(jnp.int32, (rows, HEAD_SIZE), 0)
    low = jnp.zeros((rows, HEAD_SIZE), jnp.int32)
    start = 0
    for doc in range(doc_lengths.shape[0]):
        low = jnp.where(query_pos >= start, start, low)
        start = start + doc_lengths[doc]
    v_win[:, :, HEAD_SIZE:] = jnp.ones((half, 2 * rows, HEAD_SIZE), jnp.bfloat16)

    def each_pair(step):
        def body(pair, carry):
            step(pair, False)
            return carry

        step(0, True)
        lax.fori_loop(1, trips, body, 0)

    def score_pair(pair, is_first):
        for spot in range(repeats):
            offset = 2 * pair + spot // (repeats // 2)
            key_pos = (
                first - offset * rows + spot % (repeats // 2) * HEAD_SIZE
                + lax.broadcasted_iota(jnp.int32, (rows, HEAD_SIZE), 1)
            )
            allowed = (key_pos >= low) & (key_pos <= query_pos)
            bias[:, spot * HEAD_SIZE : (spot + 1) * HEAD_SIZE] = jnp.where(allowed, 0.0, MASKED)
        for side in range(2):
            window_copy(0, pair, side, own_hbm).wait()
        for batch in batches:
            part = dot_rows(q_all[batch, :], k_win[pair])
            for head in range(at_once):
                here = slice(batch.start + head * rows, batch.start + (head + 1) * rows)
                if is_first:
                    q_turned[:, here] = q_all[here, :].T
                piece = part[head * rows : (head + 1) * rows] * (SCORE_SCALE * LOG2E) + bias[...]
                scores[pair, here, :] = piece
                pieces = [piece[:, spot * HEAD_SIZE : (spot + 1) * HEAD_SIZE] for spot in range(repeats)]
                most = functools.reduce(jnp.maximum, pieces)
                highest[here, :] = most if is_first else jnp.maximum(highest[here, :], most)

    for copy in q_copies:
        copy.wait()
    each_pair(score_pair)

    def sum_pair(pair, is_first):
        for side in range(2):
            window_copy(1, pair, side, own_hbm).wait()
        for batch in batches:
            for head in range(at_once):
                here = slice(batch.start + head * rows, batch.start + (head + 1) * rows)
                top = highest[here, :]
                if is_first:
                    top = jnp.broadcast_to(jnp.max(top, axis=1, keepdims=True), (rows, HEAD_SIZE))
                    highest[here, :] = top
                top = jnp.concatenate([top] * repeats, axis=1)
                weights[pair, here, :] = jnp.exp2(scores[pair, here, :] - top).astype(jnp.bfloat16)
            part = dot(weights[pair, batch, :], v_win[pair])
            summed[batch, :] = part if is_first else summed[batch, :] + part

    each_pair(sum_pair)

    def close_head(head):
        span = spans[head]
        inverse = 1.0 / summed[span, HEAD_SIZE:]
        output = (summed[span, :HEAD_SIZE] * inverse).astype(jnp.bfloat16)
        outs[span, :] = output
        scaled = (g_in[span, :].astype(jnp.float32) * inverse).astype(jnp.bfloat16)
        g_all[span, :] = scaled
        g_turned[:, span] = scaled.T
        terms = output.astype(jnp.float32) * scaled.astype(jnp.float32)
        upper = terms.astype(jnp.bfloat16)
        grads[span, :HEAD_SIZE] = upper
        grads[span, HEAD_SIZE : 2 * HEAD_SIZE] = (terms - upper.astype(jnp.float32)).astype(jnp.bfloat16)

    for copy in g_copies:
        copy.wait()
    ones = jnp.ones((2 * HEAD_SIZE, HEAD_SIZE), jnp.bfloat16)

    def grad_pair(pair, is_first):
        for number, batch in enumerate(batches):
            if is_first:
                for head in range(number * at_once, (number + 1) * at_once):
                    close_head(head)
                delta[batch, :] = dot(grads[batch, : 2 * HEAD_SIZE], ones)
            part = dot_rows(g_all[batch, :], v_win[pair, :, :HEAD_SIZE])
            for head in range(at_once):
                here = slice(batch.start + head * rows, batch.start + (head + 1) * rows)
                piece = part[head * rows : (head + 1) * rows] - jnp.concatenate([delta[here, :]] * repeats, axis=1)
                grads[here, :] = (weights[pair, here, :].astype(jnp.float32) * piece).astype(jnp.bfloat16)
            part = dot(grads[batch, :], k_win[pair])
            dq_acc[batch, :] = part if is_first else dq_acc[batch, :] + part
        dk = (dot(q_turned[...], grads[...]) * SCORE_SCALE).astype(jnp.bfloat16)
        dv = dot(g_turned[...], weights[pair]).astype(jnp.bfloat16)
        even[pair, 0] = dk[:, :rows]
        even[pair, 1] = dv[:, :rows]
        odd[pair, 0] = dk[:, rows:]
        odd[pair, 1] = dv[:, rows:]
        for copy in grad_copies(pair) + (out_copies if is_first else []):
            copy.start()

    each_pair(grad_pair)

    def clear_pair(pair, carry):
        even[pair] = jnp.zeros(even.shape[1:], jnp.bfloat16)
        odd[pair] = jnp.zeros(odd.shape[1:], jnp.bfloat16)
        for copy in grad_copies(pair):
            copy.start()
        return carry

    lax.fori_loop(trips, half, clear_pair, 0)
    for head, span in enumerate(spans):
        g_in[span, :] = (dq_acc[span, :] * SCORE_SCALE).astype(jnp.bfloat16)
        dq_copies[head].start()
    for copy in out_copies + [copy for pair in range(half) for copy in grad_copies(pair)] + dq_copies:
        copy.wait()


def attend_group(
    group, groups, own, doc_lengths, queries, gradient, window, place, buffers, before
):
    rows, width = queries.shape
    columns = width // groups
    heads = columns // HEAD_SIZE
    keys = WINDOW * rows
    stacked = heads * rows
    half = WINDOW // 2
    grads = jax.ShapeDtypeStruct((half, 2, HEAD_SIZE, rows), jnp.bfloat16)
    unread = len(buffers) + len(before)
    anywhere = pl.BlockSpec(memory_space=pl.ANY)
    short = lambda *shape: pltpu.VMEM(shape, jnp.bfloat16)
    full = lambda *shape: pltpu.VMEM(shape, jnp.float32)
    sems = lambda count: pltpu.SemaphoreType.DMA((count,))
    return pl.pallas_call(
        functools.partial(group_kernel, group, place, heads, unread),
        grid_spec=pltpu.PrefetchScalarGridSpec(
            num_scalar_prefetch=2,
            grid=(1,),
            in_specs=[anywhere] * (6 + unread),
            out_specs=[anywhere] * 4,
            scratch_shapes=[
                short(stacked, HEAD_SIZE),
                short(HEAD_SIZE, stacked),
                short(stacked, HEAD_SIZE),
                short(stacked, HEAD_SIZE),
                short(HEAD_SIZE, stacked),
                short(half, 2 * rows, HEAD_SIZE),
                short(half, 2 * rows, 2 * HEAD_SIZE),
                short(stacked, HEAD_SIZE),
                short(*grads.shape),
                short(*grads.shape),
                full(rows, 2 * rows),
                full(half, stacked, 2 * rows),
                short(half, stacked, 2 * rows),
                short(stacked, 2 * rows),
                full(stacked, HEAD_SIZE),
                full(stacked, 2 * HEAD_SIZE),
                full(stacked, HEAD_SIZE),
                full(stacked, HEAD_SIZE),
                sems(heads), sems(heads), sems(WINDOW), sems(WINDOW), sems(heads), sems(heads), sems(WINDOW),
            ],
        ),
        out_shape=[
            jax.ShapeDtypeStruct(queries.shape, jnp.bfloat16),
            jax.ShapeDtypeStruct(queries.shape, jnp.bfloat16),
            grads,
            grads,
        ],
        input_output_aliases={8 + number: number for number in range(len(buffers))},
        compiler_params=pltpu.CompilerParams(vmem_limit_bytes=KERNEL_VMEM),
        cost_estimate=pl.CostEstimate(
            flops=4 * 6 * 2 * heads * rows * keys * HEAD_SIZE,
            bytes_accessed=8 * rows * columns + 8 * keys * HEAD_SIZE,
            transcendentals=heads * rows * keys,
        ),
        name=f"attend_group_{group}",
    )(own, doc_lengths, queries, gradient, *window, *buffers, *before)


def shifted(value, steps):
    count = lax.axis_size("ctx")
    sources = range(max(0, -steps), min(count, count - steps))
    return lax.ppermute(value, "ctx", [(source, source + steps) for source in sources])


def swapped(value, bit):
    return lax.ppermute(value, "ctx", [(place, place ^ bit) for place in range(lax.axis_size("ctx"))])


def tp_received(block_for):
    count = lax.axis_size("tp")
    own = lax.axis_index("tp")
    received = []
    for step in range(1, count):
        sent = block_for(lax.rem(own + step, count), step)
        received.append(lax.ppermute(sent, "tp", [(place, (place + step) % count) for place in range(count)]))
    return received


def in_tp_order(mine, received):
    count = lax.axis_size("tp")
    own = lax.axis_index("tp")
    parts = [mine, *received]
    ordered = []
    for place in range(count):
        part = parts[0]
        for step in range(1, count):
            part = jnp.where(lax.rem(own - step + count, count) == place, parts[step], part)
        ordered.append(part)
    return ordered


def whole_block(shape):
    return pl.BlockSpec(shape, lambda i, *_: (0,) * len(shape))


def small_kernel(kernel, scalars, operands, specs, outs, before, name, through=()):
    if through:
        inner, handed = kernel, len(through)
        kernel = lambda *refs: inner(*refs[:-handed])
    first = 1 + len(operands) + len(before)
    return pl.pallas_call(
        kernel,
        grid_spec=pltpu.PrefetchScalarGridSpec(
            num_scalar_prefetch=1,
            grid=(1,),
            in_specs=specs + [pl.BlockSpec(memory_space=pl.ANY)] * (len(before) + len(through)),
            out_specs=[whole_block(shape) for shape in outs] + [pl.BlockSpec(memory_space=pl.ANY)] * len(through),
        ),
        out_shape=[jax.ShapeDtypeStruct(shape, jnp.bfloat16) for shape in outs]
        + [jax.ShapeDtypeStruct(part.shape, part.dtype) for part in through],
        input_output_aliases={first + number: len(outs) + number for number in range(len(through))},
        compiler_params=pltpu.CompilerParams(vmem_limit_bytes=32 * 1024 * 1024),
        name=name,
    )(scalars, *operands, *before, *through)


def pack_for_tp(key_vectors, value_vectors, groups, tp_own):
    count = lax.axis_size("tp")
    local = key_vectors.shape[0]
    columns = groups * HEAD_SIZE

    def kernel(own, key_hbm, value_hbm, *refs):
        outs, sems = refs[:-1], refs[-1]
        copies = []
        for step, out in enumerate(outs):
            block = pl.ds(pl.multiple_of(lax.rem(own[0] + step, count) * columns, HEAD_SIZE), columns)
            for kind, source in enumerate((key_hbm, value_hbm)):
                copies.append(pltpu.make_async_copy(source.at[:, block], out.at[kind], sems.at[2 * step + kind]))
        for copy in copies:
            copy.start()
        for copy in copies:
            copy.wait()

    shape = (2, local, columns)
    return pl.pallas_call(
        kernel,
        grid_spec=pltpu.PrefetchScalarGridSpec(
            num_scalar_prefetch=1,
            grid=(1,),
            in_specs=[pl.BlockSpec(memory_space=pltpu.HBM)] * 2,
            out_specs=[whole_block(shape)] * count,
            scratch_shapes=[pltpu.SemaphoreType.DMA((2 * count,))],
        ),
        out_shape=[jax.ShapeDtypeStruct(shape, jnp.bfloat16)] * count,
        name="pack_for_tp",
    )(tp_own, key_vectors, value_vectors)


def join_tokens(parts, bounds, tp_own):
    count = len(parts)
    local = parts[0].shape[1]

    def kernel(own, *refs):
        parts, outs = refs[:count], refs[count:]
        for (first, last), out in zip(bounds, outs):
            columns = slice(first * HEAD_SIZE, last * HEAD_SIZE)
            for step in range(count):
                source = lax.rem(own[0] - step + count, count)
                rows = pl.ds(pl.multiple_of(source * local, local), local)
                out[:, rows, :] = parts[step][:, :, columns]

    return small_kernel(
        kernel, tp_own, parts, [whole_block(part.shape) for part in parts],
        [(2, local * count, (last - first) * HEAD_SIZE) for first, last in bounds], [], "join_tokens",
    )


def even_window(own_pair):
    far = shifted(own_pair, WINDOW // 2)
    return own_pair, far, shifted(far, WINDOW // 2)


def for_x_swap(evens, own, before, name):
    def kernel(own, *refs):
        out = refs[-1]
        for bit in range(2):

            @pl.when(lax.rem(own[0] // 2, 2) == bit)
            def _(bit=bit):
                for place in range(2):
                    out[place] = refs[place + bit][...]

    return small_kernel(
        kernel, own, evens, [whole_block(part.shape) for part in evens], [(2, *evens[0].shape)], before, name
    )[0]


def whole_window(evens, x_sent, own, before, name):
    own_pair, far, beyond = evens
    x_pairs = swapped(x_sent, 2)
    half = WINDOW // 2

    def kernel(own, own_ref, far_ref, beyond_ref, x_ref, *refs):
        out = refs[-1]
        evens = [own_ref, x_ref.at[0], far_ref, x_ref.at[1], beyond_ref]
        low_c = lax.rem(own[0], 2)
        for bit in range(2):

            @pl.when(low_c == bit)
            def _(bit=bit):
                for place in range(half):
                    out[place] = evens[place + bit][...]

    operands = [own_pair, far, beyond, x_pairs]
    (c_sent,) = small_kernel(
        kernel, own, operands, [whole_block(part.shape) for part in operands],
        [(half, *own_pair.shape)], before, name,
    )
    return own_pair, far, x_pairs, swapped(c_sent, 1)


def wide(part):
    return part.astype(jnp.float32)


def fold_cores(even, got, own, before, name):
    half = WINDOW // 2

    def kernel(own, even_ref, got_ref, *refs):
        sent, kept = refs[-2:]
        for bit in range(2):

            @pl.when(lax.rem(own[0], 2) == bit)
            def _(bit=bit):
                for place in range(half + 1):
                    out = sent.at[place // 2] if place % 2 else kept.at[place // 2]
                    total = None
                    if place < half:
                        total = wide(even_ref[place])
                    if 0 <= place - bit < half:
                        more = wide(got_ref[place - bit])
                        total = more if total is None else total + more
                    out[...] = jnp.zeros(out.shape, out.dtype) if total is None else total.astype(out.dtype)

    shape = even.shape[1:]
    return small_kernel(
        kernel, own, [even, got], [whole_block(even.shape)] * 2,
        [(half // 2, *shape), (half // 2 + 1, *shape)], before, name,
    )


def fold_x(parts, own, before, name, through=()):
    count = len(parts)
    operands = [array for sent, kept in parts for array in (kept, swapped(sent, 2))]
    shape = operands[0].shape[1:]

    def kernel(own, *refs):
        outs = refs[-3:]
        for bit in range(2):

            @pl.when(lax.rem(own[0] // 2, 2) == bit)
            def _(bit=bit):
                for index in range(count):
                    kept, got = refs[2 * index : 2 * index + 2]
                    for place, out in enumerate(outs):
                        total = wide(kept[place])
                        if 0 <= place - bit < got.shape[0]:
                            total = total + wide(got[place - bit])
                        out[index] = total.astype(out.dtype)

    return small_kernel(
        kernel, own, operands, [whole_block(part.shape) for part in operands], [(count, *shape)] * 3,
        before, name, through,
    )


def groups_of(refs, sizes):
    return [ref.at[index] for ref, size in zip(refs, sizes) for index in range(size)]


def fold_z(parts, own, before, name):
    sizes = [part[0].shape[0] for part in parts]
    operands = [part[0] for part in parts] + [part[1] for part in parts]

    def kernel(own, *refs):
        out = refs[-1]
        shares, others = groups_of(refs, sizes), groups_of(refs[len(sizes) :], sizes)
        for index, (share, other) in enumerate(zip(shares, others)):
            out[index] = (wide(share[...]) + wide(other[...])).astype(out.dtype)

    return small_kernel(
        kernel, own, operands, [whole_block(part.shape) for part in operands],
        [(sum(sizes), *operands[0].shape[1:])], before, name,
    )[0]


def finish(nears, received, own, before, name):
    sizes = [part.shape[0] for part in nears]
    kinds, depth, rows = nears[0].shape[1:]

    def kernel(own, *refs):
        out = refs[-1]
        shares, others = groups_of(refs, sizes), groups_of(refs[len(sizes) :], [sum(sizes)])
        for index, (share, other) in enumerate(zip(shares, others)):
            for kind in range(kinds):
                out[index, kind] = (wide(share[kind]) + wide(other[kind])).T.astype(out.dtype)

    operands = [*nears, received]
    return small_kernel(
        kernel, own, operands, [whole_block(part.shape) for part in operands],
        [(sum(sizes), kinds, rows, depth)], before, name,
    )[0]


def body(queries, key_vectors, value_vectors, output_gradient, doc_lengths):
    own = lax.axis_index("ctx")
    own_info = own.reshape(1).astype(jnp.int32)
    local = key_vectors.shape[0]
    all_groups = key_vectors.shape[1] // HEAD_SIZE
    tp_count = lax.axis_size("tp")
    groups = all_groups // tp_count
    tp_own = lax.axis_index("tp")
    tp_info = tp_own.reshape(1).astype(jnp.int32)

    middle = (groups + 1) // 2
    bounds = [(0, middle)] + ([(middle, groups)] if groups > 1 else [])
    packed = pack_for_tp(key_vectors, value_vectors, groups, tp_info)
    received = tp_received(lambda place, step: packed[step])
    chunks = join_tokens([packed[0], *received], bounds, tp_info)
    evens = [even_window(chunk) for chunk in chunks]
    x_sent = [
        for_x_swap(part, own_info, [other[1] for other in evens[1:]] if chunk == 0 else [], f"x_swap_{chunk}")
        for chunk, part in enumerate(evens)
    ]
    windows = [whole_window(evens[0], x_sent[0], own_info, x_sent[1:], "core_swap_0")]
    buffers = ()
    results, got, folded, nears, passing = [], [], [], [], []

    def fold_next_cores(before):
        group = len(folded)
        folded.append(fold_cores(results[group][2], got[group], own_info, before, f"fold_cores_{group}"))

    def fold_next_x(last, before, through=()):
        first = sum(part.shape[0] for part in nears)
        near, far, beyond, *handed = fold_x(folded[first : last + 1], own_info, before, f"fold_x_{first}", through)
        nears.append(near)
        passing.append((far, shifted(beyond, -(WINDOW // 2))))
        return handed

    for group in range(groups):
        waits = []
        if group >= 2:
            waits.append(folded[group - 2][0])
        if group >= 2 and group == groups - 1:
            waits.append(folded[group - 1][0])
        if group >= 3:
            waits.append(nears[-1])
        chunk = 0 if group < middle else 1
        results.append(
            attend_group(
                group, groups, own_info, doc_lengths, queries, output_gradient,
                windows[chunk], group - bounds[chunk][0], buffers, waits,
            )
        )
        *buffers, even, odd = results[-1]
        if 3 <= groups == group + 1:
            (odd,) = fold_next_x(group - 1, [part[1] for part in passing], [odd])
        elif group >= 2:
            (odd,) = fold_next_x(group - 2, [], [odd])
        got.append(swapped(odd, 1))
        if group == 0 and groups > 1:
            windows.append(whole_window(evens[1], x_sent[1], own_info, [even], "core_swap_1"))
        if group >= 1 and len(folded) < group:
            fold_next_cores([even])
        if 2 <= group == groups - 2:
            fold_next_cores([])
    while len(folded) < groups:
        fold_next_cores([])
    while sum(part.shape[0] for part in nears) < groups:
        fold_next_x(sum(part.shape[0] for part in nears), [])

    def exchanged(total):
        def tokens_of(place, step=0):
            return lax.dynamic_slice_in_dim(total, place * local, local, total.ndim - 2)

        return in_tp_order(tokens_of(tp_own), tp_received(tokens_of))

    split = len(passing) - 1
    sent = [fold_z(passing[:split], own_info, folded[-1][:1], "fold_z_early")] if split else []
    sent.append(fold_z(passing[split:], own_info, [], "fold_z_late"))
    came = [shifted(part, -(WINDOW // 2)) for part in sent]
    totals = [exchanged(finish(nears[:split], came[0], own_info, sent[-1:], "finish_early"))] if split else []
    totals.append(exchanged(finish(nears[split:], came[-1], own_info, [], "finish_late")))
    ordered = [
        [part[source][group] for part in totals for group in range(part[source].shape[0])]
        for source in range(tp_count)
    ]

    def output(which):
        return jnp.concatenate([part[which] for source in ordered for part in source], axis=1)

    out, dq = buffers
    return out, dq, output(0), output(1)


def solution(mesh):
    tokens = P(("ctx", "tp"), None)
    heads = P("ctx", "tp")
    return jax.shard_map(
        body,
        mesh=mesh,
        in_specs=(heads, tokens, tokens, heads, P()),
        out_specs=(heads, heads, tokens, tokens),
        check_vma=False,
    )
```

```python
import functools
import math

import jax
import jax.numpy as jnp
from jax import lax
from jax.experimental import pallas as pl
from jax.experimental.pallas import tpu as pltpu
from jax.sharding import PartitionSpec as P

HEAD_SIZE = 128
WINDOW = 8
HEADS_AT_ONCE = 4
KERNEL_VMEM = 44 * 1024 * 1024
SCORE_SCALE = 1.0 / math.sqrt(HEAD_SIZE)
LOG2E = math.log2(math.e)
MASKED = -1e30


def dot(a, b):
    return jnp.dot(a, b, preferred_element_type=jnp.float32)


def dot_rows(a, b):
    return lax.dot_general(a, b, (((1,), (1,)), ((), ())), preferred_element_type=jnp.float32)


def group_kernel(
    group, place, heads, unread, own, doc_lengths, q_hbm, g_hbm, own_hbm, far_hbm, x_hbm, c_hbm, *rest
):
    out_hbm, dq_hbm, even_hbm, odd_hbm, *scratch = rest[unread:]
    (
        q_all, q_turned, g_in, g_all, g_turned, k_win, v_win, outs, even, odd,
        bias, scores, weights, grads, highest, summed, delta, dq_acc,
        q_sems, g_sems, k_sems, v_sems, out_sems, dq_sems, grad_sems,
    ) = scratch
    rows = q_hbm.shape[0]
    at_once = min(heads, HEADS_AT_ONCE)
    repeats = 2 * rows // HEAD_SIZE
    half = WINDOW // 2
    spans = [slice(head * rows, (head + 1) * rows) for head in range(heads)]
    batches = [slice(head * rows, (head + at_once) * rows) for head in range(0, heads, at_once)]

    def columns(head):
        return pl.ds((group * heads + head) * HEAD_SIZE, HEAD_SIZE)

    q_copies = [
        pltpu.make_async_copy(q_hbm.at[:, columns(head)], q_all.at[span], q_sems.at[head])
        for head, span in enumerate(spans)
    ]
    g_copies = [
        pltpu.make_async_copy(g_hbm.at[:, columns(head)], g_in.at[span], g_sems.at[head])
        for head, span in enumerate(spans)
    ]
    out_copies = [
        pltpu.make_async_copy(outs.at[span], out_hbm.at[:, columns(head)], out_sems.at[head])
        for head, span in enumerate(spans)
    ]
    dq_copies = [
        pltpu.make_async_copy(g_in.at[span], dq_hbm.at[:, columns(head)], dq_sems.at[head])
        for head, span in enumerate(spans)
    ]
    window = [
        own_hbm, c_hbm.at[0], x_hbm.at[0], c_hbm.at[1], far_hbm, c_hbm.at[2], x_hbm.at[1], c_hbm.at[3]
    ]

    def window_copy(kind, pair, side, source):
        target, sems = (v_win.at[pair, pl.ds(side * rows, rows), pl.ds(0, HEAD_SIZE)], v_sems) if kind else (
            k_win.at[pair, pl.ds(side * rows, rows)], k_sems
        )
        block = source.at[kind, :, pl.ds(place * HEAD_SIZE, HEAD_SIZE)]
        return pltpu.make_async_copy(block, target, sems.at[2 * pair + side])

    def grad_copies(pair):
        return [
            pltpu.make_async_copy(even.at[pair], even_hbm.at[pair], grad_sems.at[2 * pair]),
            pltpu.make_async_copy(odd.at[pair], odd_hbm.at[pair], grad_sems.at[2 * pair + 1]),
        ]

    first = own[0] * rows
    doc_start = 0
    start = 0
    for doc in range(doc_lengths.shape[0]):
        doc_start = jnp.where(first >= start, start, doc_start)
        start = start + doc_lengths[doc]
    needed = jnp.clip(own[0] - doc_start // rows + 1, 1, WINDOW)
    trips = (needed + 1) // 2
    for copy in q_copies:
        copy.start()
    for kind in range(2):
        for pair in range(half):

            @pl.when(pair < trips)
            def _(kind=kind, pair=pair):
                for side in range(2):
                    window_copy(kind, pair, side, window[2 * pair + side]).start()

    for copy in g_copies:
        copy.start()
    query_pos = first + lax.broadcasted_iota(jnp.int32, (rows, HEAD_SIZE), 0)
    low = jnp.zeros((rows, HEAD_SIZE), jnp.int32)
    start = 0
    for doc in range(doc_lengths.shape[0]):
        low = jnp.where(query_pos >= start, start, low)
        start = start + doc_lengths[doc]
    v_win[:, :, HEAD_SIZE:] = jnp.ones((half, 2 * rows, HEAD_SIZE), jnp.bfloat16)

    def each_pair(step):
        def body(pair, carry):
            step(pair, False)
            return carry

        step(0, True)
        lax.fori_loop(1, trips, body, 0)

    def score_pair(pair, is_first):
        for spot in range(repeats):
            offset = 2 * pair + spot // (repeats // 2)
            key_pos = (
                first - offset * rows + spot % (repeats // 2) * HEAD_SIZE
                + lax.broadcasted_iota(jnp.int32, (rows, HEAD_SIZE), 1)
            )
            allowed = (key_pos >= low) & (key_pos <= query_pos)
            bias[:, spot * HEAD_SIZE : (spot + 1) * HEAD_SIZE] = jnp.where(allowed, 0.0, MASKED)
        for side in range(2):
            window_copy(0, pair, side, own_hbm).wait()
        for batch in batches:
            part = dot_rows(q_all[batch, :], k_win[pair])
            for head in range(at_once):
                here = slice(batch.start + head * rows, batch.start + (head + 1) * rows)
                if is_first:
                    q_turned[:, here] = q_all[here, :].T
                piece = part[head * rows : (head + 1) * rows] * (SCORE_SCALE * LOG2E) + bias[...]
                scores[pair, here, :] = piece
                pieces = [piece[:, spot * HEAD_SIZE : (spot + 1) * HEAD_SIZE] for spot in range(repeats)]
                most = functools.reduce(jnp.maximum, pieces)
                highest[here, :] = most if is_first else jnp.maximum(highest[here, :], most)

    for copy in q_copies:
        copy.wait()
    each_pair(score_pair)

    def sum_pair(pair, is_first):
        for side in range(2):
            window_copy(1, pair, side, own_hbm).wait()
        for batch in batches:
            for head in range(at_once):
                here = slice(batch.start + head * rows, batch.start + (head + 1) * rows)
                top = highest[here, :]
                if is_first:
                    top = jnp.broadcast_to(jnp.max(top, axis=1, keepdims=True), (rows, HEAD_SIZE))
                    highest[here, :] = top
                top = jnp.concatenate([top] * repeats, axis=1)
                weights[pair, here, :] = jnp.exp2(scores[pair, here, :] - top).astype(jnp.bfloat16)
            part = dot(weights[pair, batch, :], v_win[pair])
            summed[batch, :] = part if is_first else summed[batch, :] + part

    each_pair(sum_pair)

    def close_head(head):
        span = spans[head]
        inverse = 1.0 / summed[span, HEAD_SIZE:]
        output = (summed[span, :HEAD_SIZE] * inverse).astype(jnp.bfloat16)
        outs[span, :] = output
        scaled = (g_in[span, :].astype(jnp.float32) * inverse).astype(jnp.bfloat16)
        g_all[span, :] = scaled
        g_turned[:, span] = scaled.T
        terms = output.astype(jnp.float32) * scaled.astype(jnp.float32)
        upper = terms.astype(jnp.bfloat16)
        grads[span, :HEAD_SIZE] = upper
        grads[span, HEAD_SIZE : 2 * HEAD_SIZE] = (terms - upper.astype(jnp.float32)).astype(jnp.bfloat16)

    for copy in g_copies:
        copy.wait()
    ones = jnp.ones((2 * HEAD_SIZE, HEAD_SIZE), jnp.bfloat16)

    def grad_pair(pair, is_first):
        for number, batch in enumerate(batches):
            if is_first:
                for head in range(number * at_once, (number + 1) * at_once):
                    close_head(head)
                delta[batch, :] = dot(grads[batch, : 2 * HEAD_SIZE], ones)
            part = dot_rows(g_all[batch, :], v_win[pair, :, :HEAD_SIZE])
            for head in range(at_once):
                here = slice(batch.start + head * rows, batch.start + (head + 1) * rows)
                piece = part[head * rows : (head + 1) * rows] - jnp.concatenate([delta[here, :]] * repeats, axis=1)
                grads[here, :] = (weights[pair, here, :].astype(jnp.float32) * piece).astype(jnp.bfloat16)
            part = dot(grads[batch, :], k_win[pair])
            dq_acc[batch, :] = part if is_first else dq_acc[batch, :] + part
        dk = (dot(q_turned[...], grads[...]) * SCORE_SCALE).astype(jnp.bfloat16)
        dv = dot(g_turned[...], weights[pair]).astype(jnp.bfloat16)
        even[pair, 0] = dk[:, :rows]
        even[pair, 1] = dv[:, :rows]
        odd[pair, 0] = dk[:, rows:]
        odd[pair, 1] = dv[:, rows:]
        for copy in grad_copies(pair) + (out_copies if is_first else []):
            copy.start()

    each_pair(grad_pair)

    def clear_pair(pair, carry):
        even[pair] = jnp.zeros(even.shape[1:], jnp.bfloat16)
        odd[pair] = jnp.zeros(odd.shape[1:], jnp.bfloat16)
        for copy in grad_copies(pair):
            copy.start()
        return carry

    lax.fori_loop(trips, half, clear_pair, 0)
    for head, span in enumerate(spans):
        g_in[span, :] = (dq_acc[span, :] * SCORE_SCALE).astype(jnp.bfloat16)
        dq_copies[head].start()
    for copy in out_copies + [copy for pair in range(half) for copy in grad_copies(pair)] + dq_copies:
        copy.wait()


def attend_group(
    group, groups, own, doc_lengths, queries, gradient, window, place, buffers, before
):
    rows, width = queries.shape
    columns = width // groups
    heads = columns // HEAD_SIZE
    keys = WINDOW * rows
    stacked = heads * rows
    half = WINDOW // 2
    grads = jax.ShapeDtypeStruct((half, 2, HEAD_SIZE, rows), jnp.bfloat16)
    unread = len(buffers) + len(before)
    anywhere = pl.BlockSpec(memory_space=pl.ANY)
    short = lambda *shape: pltpu.VMEM(shape, jnp.bfloat16)
    full = lambda *shape: pltpu.VMEM(shape, jnp.float32)
    sems = lambda count: pltpu.SemaphoreType.DMA((count,))
    return pl.pallas_call(
        functools.partial(group_kernel, group, place, heads, unread),
        grid_spec=pltpu.PrefetchScalarGridSpec(
            num_scalar_prefetch=2,
            grid=(1,),
            in_specs=[anywhere] * (6 + unread),
            out_specs=[anywhere] * 4,
            scratch_shapes=[
                short(stacked, HEAD_SIZE),
                short(HEAD_SIZE, stacked),
                short(stacked, HEAD_SIZE),
                short(stacked, HEAD_SIZE),
                short(HEAD_SIZE, stacked),
                short(half, 2 * rows, HEAD_SIZE),
                short(half, 2 * rows, 2 * HEAD_SIZE),
                short(stacked, HEAD_SIZE),
                short(*grads.shape),
                short(*grads.shape),
                full(rows, 2 * rows),
                full(half, stacked, 2 * rows),
                short(half, stacked, 2 * rows),
                short(stacked, 2 * rows),
                full(stacked, HEAD_SIZE),
                full(stacked, 2 * HEAD_SIZE),
                full(stacked, HEAD_SIZE),
                full(stacked, HEAD_SIZE),
                sems(heads), sems(heads), sems(WINDOW), sems(WINDOW), sems(heads), sems(heads), sems(WINDOW),
            ],
        ),
        out_shape=[
            jax.ShapeDtypeStruct(queries.shape, jnp.bfloat16),
            jax.ShapeDtypeStruct(queries.shape, jnp.bfloat16),
            grads,
            grads,
        ],
        input_output_aliases={8 + number: number for number in range(len(buffers))},
        compiler_params=pltpu.CompilerParams(vmem_limit_bytes=KERNEL_VMEM),
        cost_estimate=pl.CostEstimate(
            flops=4 * 6 * 2 * heads * rows * keys * HEAD_SIZE,
            bytes_accessed=8 * rows * columns + 8 * keys * HEAD_SIZE,
            transcendentals=heads * rows * keys,
        ),
        name=f"attend_group_{group}",
    )(own, doc_lengths, queries, gradient, *window, *buffers, *before)


def shifted(value, steps):
    count = lax.axis_size("ctx")
    sources = range(max(0, -steps), min(count, count - steps))
    return lax.ppermute(value, "ctx", [(source, source + steps) for source in sources])


def swapped(value, bit):
    return lax.ppermute(value, "ctx", [(place, place ^ bit) for place in range(lax.axis_size("ctx"))])


def tp_received(block_for):
    count = lax.axis_size("tp")
    own = lax.axis_index("tp")
    received = []
    for step in range(1, count):
        sent = block_for(lax.rem(own + step, count), step)
        received.append(lax.ppermute(sent, "tp", [(place, (place + step) % count) for place in range(count)]))
    return received


def in_tp_order(mine, received):
    count = lax.axis_size("tp")
    own = lax.axis_index("tp")
    parts = [mine, *received]
    ordered = []
    for place in range(count):
        part = parts[0]
        for step in range(1, count):
            part = jnp.where(lax.rem(own - step + count, count) == place, parts[step], part)
        ordered.append(part)
    return ordered


def whole_block(shape):
    return pl.BlockSpec(shape, lambda i, *_: (0,) * len(shape))


def small_kernel(kernel, scalars, operands, specs, outs, before, name, through=(), cost=1):
    if through:
        inner, handed = kernel, len(through)
        kernel = lambda *refs: inner(*refs[:-handed])
    first = 1 + len(operands) + len(before)
    return pl.pallas_call(
        kernel,
        grid_spec=pltpu.PrefetchScalarGridSpec(
            num_scalar_prefetch=1,
            grid=(1,),
            in_specs=specs + [pl.BlockSpec(memory_space=pl.ANY)] * (len(before) + len(through)),
            out_specs=[whole_block(shape) for shape in outs] + [pl.BlockSpec(memory_space=pl.ANY)] * len(through),
        ),
        out_shape=[jax.ShapeDtypeStruct(shape, jnp.bfloat16) for shape in outs]
        + [jax.ShapeDtypeStruct(part.shape, part.dtype) for part in through],
        input_output_aliases={first + number: len(outs) + number for number in range(len(through))},
        compiler_params=pltpu.CompilerParams(vmem_limit_bytes=32 * 1024 * 1024),
        cost_estimate=pl.CostEstimate(flops=cost, bytes_accessed=1, transcendentals=0),
        name=name,
    )(scalars, *operands, *before, *through)


def pack_for_tp(key_vectors, value_vectors, groups, tp_own):
    count = lax.axis_size("tp")
    local = key_vectors.shape[0]
    columns = groups * HEAD_SIZE

    def kernel(own, key_hbm, value_hbm, *refs):
        outs, sems = refs[:-1], refs[-1]
        copies = []
        for step, out in enumerate(outs):
            block = pl.ds(pl.multiple_of(lax.rem(own[0] + step, count) * columns, HEAD_SIZE), columns)
            for kind, source in enumerate((key_hbm, value_hbm)):
                copies.append(pltpu.make_async_copy(source.at[:, block], out.at[kind], sems.at[2 * step + kind]))
        for copy in copies:
            copy.start()
        for copy in copies:
            copy.wait()

    shape = (2, local, columns)
    return pl.pallas_call(
        kernel,
        grid_spec=pltpu.PrefetchScalarGridSpec(
            num_scalar_prefetch=1,
            grid=(1,),
            in_specs=[pl.BlockSpec(memory_space=pltpu.HBM)] * 2,
            out_specs=[whole_block(shape)] * count,
            scratch_shapes=[pltpu.SemaphoreType.DMA((2 * count,))],
        ),
        out_shape=[jax.ShapeDtypeStruct(shape, jnp.bfloat16)] * count,
        name="pack_for_tp",
    )(tp_own, key_vectors, value_vectors)


def join_tokens(parts, bounds, tp_own):
    count = len(parts)
    local = parts[0].shape[1]

    def kernel(own, *refs):
        parts, outs = refs[:count], refs[count:]
        for (first, last), out in zip(bounds, outs):
            columns = slice(first * HEAD_SIZE, last * HEAD_SIZE)
            for step in range(count):
                source = lax.rem(own[0] - step + count, count)
                rows = pl.ds(pl.multiple_of(source * local, local), local)
                out[:, rows, :] = parts[step][:, :, columns]

    return small_kernel(
        kernel, tp_own, parts, [whole_block(part.shape) for part in parts],
        [(2, local * count, (last - first) * HEAD_SIZE) for first, last in bounds], [], "join_tokens",
    )


def even_window(own_pair):
    far = shifted(own_pair, WINDOW // 2)
    return own_pair, far, shifted(far, WINDOW // 2)


def for_x_swap(evens, own, before, name):
    def kernel(own, *refs):
        out = refs[-1]
        for bit in range(2):

            @pl.when(lax.rem(own[0] // 2, 2) == bit)
            def _(bit=bit):
                for place in range(2):
                    out[place] = refs[place + bit][...]

    return small_kernel(
        kernel, own, evens, [whole_block(part.shape) for part in evens], [(2, *evens[0].shape)], before, name
    )[0]


def whole_window(evens, x_sent, own, before, name):
    own_pair, far, beyond = evens
    x_pairs = swapped(x_sent, 2)
    half = WINDOW // 2

    def kernel(own, own_ref, far_ref, beyond_ref, x_ref, *refs):
        out = refs[-1]
        evens = [own_ref, x_ref.at[0], far_ref, x_ref.at[1], beyond_ref]
        low_c = lax.rem(own[0], 2)
        for bit in range(2):

            @pl.when(low_c == bit)
            def _(bit=bit):
                for place in range(half):
                    out[place] = evens[place + bit][...]

    operands = [own_pair, far, beyond, x_pairs]
    (c_sent,) = small_kernel(
        kernel, own, operands, [whole_block(part.shape) for part in operands],
        [(half, *own_pair.shape)], before, name,
    )
    return own_pair, far, x_pairs, swapped(c_sent, 1)


def wide(part):
    return part.astype(jnp.float32)


def fold_cores(even, got, own, before, name):
    half = WINDOW // 2

    def kernel(own, even_ref, got_ref, *refs):
        sent, kept = refs[-2:]
        for bit in range(2):

            @pl.when(lax.rem(own[0], 2) == bit)
            def _(bit=bit):
                for place in range(half + 1):
                    out = sent.at[place // 2] if place % 2 else kept.at[place // 2]
                    total = None
                    if place < half:
                        total = wide(even_ref[place])
                    if 0 <= place - bit < half:
                        more = wide(got_ref[place - bit])
                        total = more if total is None else total + more
                    out[...] = jnp.zeros(out.shape, out.dtype) if total is None else total.astype(out.dtype)

    shape = even.shape[1:]
    return small_kernel(
        kernel, own, [even, got], [whole_block(even.shape)] * 2,
        [(half // 2, *shape), (half // 2 + 1, *shape)], before, name,
    )


def fold_x(parts, own, before, name, through=()):
    count = len(parts)
    operands = [array for sent, kept in parts for array in (kept, swapped(sent, 2))]
    shape = operands[0].shape[1:]

    def kernel(own, *refs):
        outs = refs[-3:]
        for bit in range(2):

            @pl.when(lax.rem(own[0] // 2, 2) == bit)
            def _(bit=bit):
                for index in range(count):
                    kept, got = refs[2 * index : 2 * index + 2]
                    for place, out in enumerate(outs):
                        total = wide(kept[place])
                        if 0 <= place - bit < got.shape[0]:
                            total = total + wide(got[place - bit])
                        out[index] = total.astype(out.dtype)

    return small_kernel(
        kernel, own, operands, [whole_block(part.shape) for part in operands], [(count, *shape)] * 3,
        before, name, through,
    )


def groups_of(refs, sizes):
    return [ref.at[index] for ref, size in zip(refs, sizes) for index in range(size)]


def fold_z(parts, own, before, name, cost):
    sizes = [part[0].shape[0] for part in parts]
    operands = [part[0] for part in parts] + [part[1] for part in parts]

    def kernel(own, *refs):
        out = refs[-1]
        shares, others = groups_of(refs, sizes), groups_of(refs[len(sizes) :], sizes)
        for index, (share, other) in enumerate(zip(shares, others)):
            out[index] = (wide(share[...]) + wide(other[...])).astype(out.dtype)

    return small_kernel(
        kernel, own, operands, [whole_block(part.shape) for part in operands],
        [(sum(sizes), *operands[0].shape[1:])], before, name, cost=cost,
    )[0]


def finish(terms, count, own, before, name):
    operands = [array for array, _ in terms]
    kinds, depth, rows = operands[0].shape[1:]

    def kernel(own, *refs):
        out = refs[-1]
        for index in range(count):
            parts = [
                ref.at[index - first]
                for ref, (array, first) in zip(refs, terms)
                if 0 <= index - first < array.shape[0]
            ]
            for kind in range(kinds):
                total = functools.reduce(jnp.add, [wide(part[kind]) for part in parts])
                out[index, kind] = total.T.astype(out.dtype)

    return small_kernel(
        kernel, own, operands, [whole_block(part.shape) for part in operands],
        [(count, kinds, rows, depth)], before, name,
    )[0]


def body(queries, key_vectors, value_vectors, output_gradient, doc_lengths):
    own = lax.axis_index("ctx")
    own_info = own.reshape(1).astype(jnp.int32)
    local = key_vectors.shape[0]
    all_groups = key_vectors.shape[1] // HEAD_SIZE
    tp_count = lax.axis_size("tp")
    groups = all_groups // tp_count
    tp_own = lax.axis_index("tp")
    tp_info = tp_own.reshape(1).astype(jnp.int32)

    middle = (groups + 1) // 2
    bounds = [(0, middle)] + ([(middle, groups)] if groups > 1 else [])
    packed = pack_for_tp(key_vectors, value_vectors, groups, tp_info)
    received = tp_received(lambda place, step: packed[step])
    chunks = join_tokens([packed[0], *received], bounds, tp_info)
    evens = [even_window(chunk) for chunk in chunks]
    x_sent = [
        for_x_swap(part, own_info, [other[1] for other in evens[1:]] if chunk == 0 else [], f"x_swap_{chunk}")
        for chunk, part in enumerate(evens)
    ]
    windows = [whole_window(evens[0], x_sent[0], own_info, x_sent[1:], "core_swap_0")]
    buffers = ()
    results, got, folded, nears, passing = [], [], [], [], []

    def fold_next_cores(before):
        group = len(folded)
        folded.append(fold_cores(results[group][2], got[group], own_info, before, f"fold_cores_{group}"))

    def fold_next_x(last, before, through=()):
        first = sum(part.shape[0] for part in nears)
        near, far, beyond, *handed = fold_x(folded[first : last + 1], own_info, before, f"fold_x_{first}", through)
        nears.append(near)
        if first == 0 and groups > 2:
            passing.append((shifted(far, -(WINDOW // 2)), shifted(beyond, -WINDOW)))
        else:
            passing.append((far, shifted(beyond, -(WINDOW // 2))))
        return handed

    for group in range(groups):
        waits = []
        if group >= 2:
            waits.append(folded[group - 2][0])
        if group >= 2 and group == groups - 1:
            waits.append(folded[group - 1][0])
        if group >= 3:
            waits.append(nears[-1])
        chunk = 0 if group < middle else 1
        results.append(
            attend_group(
                group, groups, own_info, doc_lengths, queries, output_gradient,
                windows[chunk], group - bounds[chunk][0], buffers, waits,
            )
        )
        *buffers, even, odd = results[-1]
        if 3 <= groups == group + 1:
            (odd,) = fold_next_x(group - 1, [part for pair in passing for part in pair], [odd])
        elif group >= 2:
            (odd,) = fold_next_x(group - 2, [], [odd])
        got.append(swapped(odd, 1))
        if group == 0 and groups > 1:
            windows.append(whole_window(evens[1], x_sent[1], own_info, [even], "core_swap_1"))
        if group >= 1 and len(folded) < group:
            fold_next_cores([even])
        if 2 <= group == groups - 2:
            fold_next_cores([])
    while len(folded) < groups:
        fold_next_cores([])
    while sum(part.shape[0] for part in nears) < groups:
        fold_next_x(sum(part.shape[0] for part in nears), [])

    def exchanged(total):
        def tokens_of(place, step=0):
            return lax.dynamic_slice_in_dim(total, place * local, local, total.ndim - 2)

        return in_tp_order(tokens_of(tp_own), tp_received(tokens_of))

    direct = 1 if groups > 2 else 0
    terms = [(part, 0) for part in (nears[0], *passing[0])] if direct else []
    split = len(passing) - 1
    early = groups - nears[-1].shape[0]
    late = fold_z(passing[split:], own_info, [], "fold_z_late", 1)
    if split > direct:
        joint = fold_z(passing[direct:split], own_info, nears[-1:], "fold_z_early", 1 << 34)
        terms += [(part, direct) for part in (nears[direct], shifted(joint, -(WINDOW // 2)))]
    finished = [finish(terms, early, own_info, [late], "finish_early")] if early else []
    terms = [(nears[-1], 0), (shifted(late, -(WINDOW // 2)), 0)]
    finished.append(finish(terms, groups - early, own_info, finished, "finish_late"))
    totals = [exchanged(part) for part in finished]
    ordered = [
        [part[source][group] for part in totals for group in range(part[source].shape[0])]
        for source in range(tp_count)
    ]

    def output(which):
        return jnp.concatenate([part[which] for source in ordered for part in source], axis=1)

    out, dq = buffers
    return out, dq, output(0), output(1)


def solution(mesh):
    tokens = P(("ctx", "tp"), None)
    heads = P("ctx", "tp")
    return jax.shard_map(
        body,
        mesh=mesh,
        in_specs=(heads, tokens, tokens, heads, P()),
        out_specs=(heads, heads, tokens, tokens),
        check_vma=False,
    )
```

```python
import functools
import math

import jax
import jax.numpy as jnp
from jax import lax
from jax.experimental import pallas as pl
from jax.experimental.pallas import tpu as pltpu
from jax.sharding import PartitionSpec as P

HEAD_SIZE = 128
WINDOW = 8
HEADS_AT_ONCE = 2
KERNEL_VMEM = 44 * 1024 * 1024
SCORE_SCALE = 1.0 / math.sqrt(HEAD_SIZE)
LOG2E = math.log2(math.e)
MASKED = -1e30


def dot(a, b):
    return jnp.dot(a, b, preferred_element_type=jnp.float32)


def dot_rows(a, b):
    return lax.dot_general(a, b, (((1,), (1,)), ((), ())), preferred_element_type=jnp.float32)


def group_kernel(
    group, place, heads, unread, own, doc_lengths, q_hbm, g_hbm, own_hbm, far_hbm, x_hbm, c_hbm, *rest
):
    out_hbm, dq_hbm, even_hbm, odd_hbm, *scratch = rest[unread:]
    (
        q_in, q_all, q_turned, g_in, g_all, g_turned, k_win, v_win, outs, even, odd,
        bias, scores, weights, grads, highest, summed, delta, dq_acc,
        sems, k_sems, v_sems, grad_sems,
    ) = scratch
    rows = q_hbm.shape[0]
    at_once = min(heads, HEADS_AT_ONCE)
    repeats = 2 * rows // HEAD_SIZE
    half = WINDOW // 2
    spans = [slice(head * rows, (head + 1) * rows) for head in range(heads)]
    batches = [slice(head * rows, (head + at_once) * rows) for head in range(0, heads, at_once)]

    width = heads * HEAD_SIZE
    own_columns = pl.ds(group * width, width)
    columns = [slice(head * HEAD_SIZE, (head + 1) * HEAD_SIZE) for head in range(heads)]
    q_copy = pltpu.make_async_copy(q_hbm.at[:, own_columns], q_in, sems.at[0])
    g_copy = pltpu.make_async_copy(g_hbm.at[:, own_columns], g_in, sems.at[1])
    out_copy = pltpu.make_async_copy(outs, out_hbm.at[:, own_columns], sems.at[2])
    dq_copy = pltpu.make_async_copy(q_in, dq_hbm.at[:, own_columns], sems.at[3])
    window = [
        own_hbm, c_hbm.at[0], x_hbm.at[0], c_hbm.at[1], far_hbm, c_hbm.at[2], x_hbm.at[1], c_hbm.at[3]
    ]

    def window_copy(kind, pair, side, source):
        target, sems = (v_win.at[pair, pl.ds(side * rows, rows), pl.ds(0, HEAD_SIZE)], v_sems) if kind else (
            k_win.at[pair, pl.ds(side * rows, rows)], k_sems
        )
        block = source.at[kind, :, pl.ds(place * HEAD_SIZE, HEAD_SIZE)]
        return pltpu.make_async_copy(block, target, sems.at[2 * pair + side])

    def grad_copies(pair):
        return [
            pltpu.make_async_copy(even.at[pair], even_hbm.at[pair], grad_sems.at[2 * pair]),
            pltpu.make_async_copy(odd.at[pair], odd_hbm.at[pair], grad_sems.at[2 * pair + 1]),
        ]

    first = own[0] * rows
    doc_start = 0
    start = 0
    for doc in range(doc_lengths.shape[0]):
        doc_start = jnp.where(first >= start, start, doc_start)
        start = start + doc_lengths[doc]
    needed = jnp.clip(own[0] - doc_start // rows + 1, 1, WINDOW)
    trips = (needed + 1) // 2
    q_copy.start()
    for kind in range(2):
        for pair in range(half):

            @pl.when(pair < trips)
            def _(kind=kind, pair=pair):
                for side in range(2):
                    window_copy(kind, pair, side, window[2 * pair + side]).start()

    g_copy.start()
    query_pos = first + lax.broadcasted_iota(jnp.int32, (rows, HEAD_SIZE), 0)
    low = jnp.zeros((rows, HEAD_SIZE), jnp.int32)
    start = 0
    for doc in range(doc_lengths.shape[0]):
        low = jnp.where(query_pos >= start, start, low)
        start = start + doc_lengths[doc]
    v_win[:, :, HEAD_SIZE:] = jnp.ones((half, 2 * rows, HEAD_SIZE), jnp.bfloat16)

    def each_pair(step):
        def body(pair, carry):
            step(pair, False)
            return carry

        step(0, True)
        lax.fori_loop(1, trips, body, 0)

    def score_pair(pair, is_first):
        for spot in range(repeats):
            offset = 2 * pair + spot // (repeats // 2)
            key_pos = (
                first - offset * rows + spot % (repeats // 2) * HEAD_SIZE
                + lax.broadcasted_iota(jnp.int32, (rows, HEAD_SIZE), 1)
            )
            allowed = (key_pos >= low) & (key_pos <= query_pos)
            bias[:, spot * HEAD_SIZE : (spot + 1) * HEAD_SIZE] = jnp.where(allowed, 0.0, MASKED)
        for side in range(2):
            window_copy(0, pair, side, own_hbm).wait()
        for batch in batches:
            part = dot_rows(q_all[batch, :], k_win[pair])
            for head in range(at_once):
                here = slice(batch.start + head * rows, batch.start + (head + 1) * rows)
                if is_first:
                    q_turned[:, here] = q_all[here, :].T
                piece = part[head * rows : (head + 1) * rows] * (SCORE_SCALE * LOG2E) + bias[...]
                scores[pair, here, :] = piece
                pieces = [piece[:, spot * HEAD_SIZE : (spot + 1) * HEAD_SIZE] for spot in range(repeats)]
                most = functools.reduce(jnp.maximum, pieces)
                highest[here, :] = most if is_first else jnp.maximum(highest[here, :], most)

    q_copy.wait()
    for span, column in zip(spans, columns):
        q_all[span, :] = q_in[:, column]
    each_pair(score_pair)

    def sum_pair(pair, is_first):
        for side in range(2):
            window_copy(1, pair, side, own_hbm).wait()
        for batch in batches:
            for head in range(at_once):
                here = slice(batch.start + head * rows, batch.start + (head + 1) * rows)
                top = highest[here, :]
                if is_first:
                    top = jnp.broadcast_to(jnp.max(top, axis=1, keepdims=True), (rows, HEAD_SIZE))
                    highest[here, :] = top
                top = jnp.concatenate([top] * repeats, axis=1)
                weights[pair, here, :] = jnp.exp2(scores[pair, here, :] - top).astype(jnp.bfloat16)
            part = dot(weights[pair, batch, :], v_win[pair])
            summed[batch, :] = part if is_first else summed[batch, :] + part

    each_pair(sum_pair)

    def close_head(head):
        span, column = spans[head], columns[head]
        inverse = 1.0 / summed[span, HEAD_SIZE:]
        output = (summed[span, :HEAD_SIZE] * inverse).astype(jnp.bfloat16)
        outs[:, column] = output
        scaled = (g_in[:, column].astype(jnp.float32) * inverse).astype(jnp.bfloat16)
        g_all[span, :] = scaled
        g_turned[:, span] = scaled.T
        terms = output.astype(jnp.float32) * scaled.astype(jnp.float32)
        upper = terms.astype(jnp.bfloat16)
        grads[span, :HEAD_SIZE] = upper
        grads[span, HEAD_SIZE : 2 * HEAD_SIZE] = (terms - upper.astype(jnp.float32)).astype(jnp.bfloat16)

    g_copy.wait()
    ones = jnp.ones((2 * HEAD_SIZE, HEAD_SIZE), jnp.bfloat16)

    def grad_pair(pair, is_first):
        for number, batch in enumerate(batches):
            if is_first:
                for head in range(number * at_once, (number + 1) * at_once):
                    close_head(head)
                delta[batch, :] = dot(grads[batch, : 2 * HEAD_SIZE], ones)
            part = dot_rows(g_all[batch, :], v_win[pair, :, :HEAD_SIZE])
            for head in range(at_once):
                here = slice(batch.start + head * rows, batch.start + (head + 1) * rows)
                piece = part[head * rows : (head + 1) * rows] - jnp.concatenate([delta[here, :]] * repeats, axis=1)
                grads[here, :] = (weights[pair, here, :].astype(jnp.float32) * piece).astype(jnp.bfloat16)
            part = dot(grads[batch, :], k_win[pair])
            dq_acc[batch, :] = part if is_first else dq_acc[batch, :] + part
        dk = (dot(q_turned[...], grads[...]) * SCORE_SCALE).astype(jnp.bfloat16)
        dv = dot(g_turned[...], weights[pair]).astype(jnp.bfloat16)
        even[pair, 0] = dk[:, :rows]
        even[pair, 1] = dv[:, :rows]
        odd[pair, 0] = dk[:, rows:]
        odd[pair, 1] = dv[:, rows:]
        for copy in grad_copies(pair) + ([out_copy] if is_first else []):
            copy.start()

    each_pair(grad_pair)

    def clear_pair(pair, carry):
        even[pair] = jnp.zeros(even.shape[1:], jnp.bfloat16)
        odd[pair] = jnp.zeros(odd.shape[1:], jnp.bfloat16)
        for copy in grad_copies(pair):
            copy.start()
        return carry

    lax.fori_loop(trips, half, clear_pair, 0)
    for span, column in zip(spans, columns):
        q_in[:, column] = (dq_acc[span, :] * SCORE_SCALE).astype(jnp.bfloat16)
    dq_copy.start()
    for copy in [out_copy] + [copy for pair in range(half) for copy in grad_copies(pair)] + [dq_copy]:
        copy.wait()


def attend_group(
    group, groups, own, doc_lengths, queries, gradient, window, place, buffers, before
):
    rows, width = queries.shape
    columns = width // groups
    heads = columns // HEAD_SIZE
    keys = WINDOW * rows
    stacked = heads * rows
    half = WINDOW // 2
    grads = jax.ShapeDtypeStruct((half, 2, HEAD_SIZE, rows), jnp.bfloat16)
    unread = len(buffers) + len(before)
    anywhere = pl.BlockSpec(memory_space=pl.ANY)
    short = lambda *shape: pltpu.VMEM(shape, jnp.bfloat16)
    full = lambda *shape: pltpu.VMEM(shape, jnp.float32)
    sems = lambda count: pltpu.SemaphoreType.DMA((count,))
    return pl.pallas_call(
        functools.partial(group_kernel, group, place, heads, unread),
        grid_spec=pltpu.PrefetchScalarGridSpec(
            num_scalar_prefetch=2,
            grid=(1,),
            in_specs=[anywhere] * (6 + unread),
            out_specs=[anywhere] * 4,
            scratch_shapes=[
                short(rows, columns),
                short(stacked, HEAD_SIZE),
                short(HEAD_SIZE, stacked),
                short(rows, columns),
                short(stacked, HEAD_SIZE),
                short(HEAD_SIZE, stacked),
                short(half, 2 * rows, HEAD_SIZE),
                short(half, 2 * rows, 2 * HEAD_SIZE),
                short(rows, columns),
                short(*grads.shape),
                short(*grads.shape),
                full(rows, 2 * rows),
                full(half, stacked, 2 * rows),
                short(half, stacked, 2 * rows),
                short(stacked, 2 * rows),
                full(stacked, HEAD_SIZE),
                full(stacked, 2 * HEAD_SIZE),
                full(stacked, HEAD_SIZE),
                full(stacked, HEAD_SIZE),
                sems(4), sems(WINDOW), sems(WINDOW), sems(WINDOW),
            ],
        ),
        out_shape=[
            jax.ShapeDtypeStruct(queries.shape, jnp.bfloat16),
            jax.ShapeDtypeStruct(queries.shape, jnp.bfloat16),
            grads,
            grads,
        ],
        input_output_aliases={8 + number: number for number in range(len(buffers))},
        compiler_params=pltpu.CompilerParams(vmem_limit_bytes=KERNEL_VMEM),
        cost_estimate=pl.CostEstimate(
            flops=4 * 6 * 2 * heads * rows * keys * HEAD_SIZE,
            bytes_accessed=8 * rows * columns + 8 * keys * HEAD_SIZE,
            transcendentals=heads * rows * keys,
        ),
        name=f"attend_group_{group}",
    )(own, doc_lengths, queries, gradient, *window, *buffers, *before)


def shifted(value, steps):
    count = lax.axis_size("ctx")
    sources = range(max(0, -steps), min(count, count - steps))
    return lax.ppermute(value, "ctx", [(source, source + steps) for source in sources])


def swapped(value, bit):
    return lax.ppermute(value, "ctx", [(place, place ^ bit) for place in range(lax.axis_size("ctx"))])


def tp_received(block_for):
    count = lax.axis_size("tp")
    own = lax.axis_index("tp")
    received = []
    for step in range(1, count):
        sent = block_for(lax.rem(own + step, count), step)
        received.append(lax.ppermute(sent, "tp", [(place, (place + step) % count) for place in range(count)]))
    return received


def in_tp_order(mine, received):
    count = lax.axis_size("tp")
    own = lax.axis_index("tp")
    parts = [mine, *received]
    ordered = []
    for place in range(count):
        part = parts[0]
        for step in range(1, count):
            part = jnp.where(lax.rem(own - step + count, count) == place, parts[step], part)
        ordered.append(part)
    return ordered


def whole_block(shape):
    return pl.BlockSpec(shape, lambda i, *_: (0,) * len(shape))


def small_kernel(kernel, scalars, operands, specs, outs, before, name, through=(), cost=1):
    if through:
        inner, handed = kernel, len(through)
        kernel = lambda *refs: inner(*refs[:-handed])
    first = 1 + len(operands) + len(before)
    return pl.pallas_call(
        kernel,
        grid_spec=pltpu.PrefetchScalarGridSpec(
            num_scalar_prefetch=1,
            grid=(1,),
            in_specs=specs + [pl.BlockSpec(memory_space=pl.ANY)] * (len(before) + len(through)),
            out_specs=[whole_block(shape) for shape in outs] + [pl.BlockSpec(memory_space=pl.ANY)] * len(through),
        ),
        out_shape=[jax.ShapeDtypeStruct(shape, jnp.bfloat16) for shape in outs]
        + [jax.ShapeDtypeStruct(part.shape, part.dtype) for part in through],
        input_output_aliases={first + number: len(outs) + number for number in range(len(through))},
        compiler_params=pltpu.CompilerParams(vmem_limit_bytes=32 * 1024 * 1024),
        cost_estimate=pl.CostEstimate(flops=cost, bytes_accessed=1, transcendentals=0),
        name=name,
    )(scalars, *operands, *before, *through)


def pack_for_tp(key_vectors, value_vectors, groups, tp_own):
    count = lax.axis_size("tp")
    local = key_vectors.shape[0]
    columns = groups * HEAD_SIZE

    def kernel(own, key_hbm, value_hbm, *refs):
        outs, sems = refs[:-1], refs[-1]
        copies = []
        for step, out in enumerate(outs):
            block = pl.ds(pl.multiple_of(lax.rem(own[0] + step, count) * columns, HEAD_SIZE), columns)
            for kind, source in enumerate((key_hbm, value_hbm)):
                copies.append(pltpu.make_async_copy(source.at[:, block], out.at[kind], sems.at[2 * step + kind]))
        for copy in copies:
            copy.start()
        for copy in copies:
            copy.wait()

    shape = (2, local, columns)
    return pl.pallas_call(
        kernel,
        grid_spec=pltpu.PrefetchScalarGridSpec(
            num_scalar_prefetch=1,
            grid=(1,),
            in_specs=[pl.BlockSpec(memory_space=pltpu.HBM)] * 2,
            out_specs=[whole_block(shape)] * count,
            scratch_shapes=[pltpu.SemaphoreType.DMA((2 * count,))],
        ),
        out_shape=[jax.ShapeDtypeStruct(shape, jnp.bfloat16)] * count,
        name="pack_for_tp",
    )(tp_own, key_vectors, value_vectors)


def join_tokens(parts, bounds, tp_own):
    count = len(parts)
    local = parts[0].shape[1]

    def kernel(own, *refs):
        parts, outs = refs[:count], refs[count:]
        for (first, last), out in zip(bounds, outs):
            columns = slice(first * HEAD_SIZE, last * HEAD_SIZE)
            for step in range(count):
                source = lax.rem(own[0] - step + count, count)
                rows = pl.ds(pl.multiple_of(source * local, local), local)
                out[:, rows, :] = parts[step][:, :, columns]

    return small_kernel(
        kernel, tp_own, parts, [whole_block(part.shape) for part in parts],
        [(2, local * count, (last - first) * HEAD_SIZE) for first, last in bounds], [], "join_tokens",
    )


def even_window(own_pair):
    far = shifted(own_pair, WINDOW // 2)
    return own_pair, far, shifted(far, WINDOW // 2)


def for_x_swap(evens, own, before, name):
    def kernel(own, *refs):
        out = refs[-1]
        for bit in range(2):

            @pl.when(lax.rem(own[0] // 2, 2) == bit)
            def _(bit=bit):
                for place in range(2):
                    out[place] = refs[place + bit][...]

    return small_kernel(
        kernel, own, evens, [whole_block(part.shape) for part in evens], [(2, *evens[0].shape)], before, name
    )[0]


def whole_window(evens, x_sent, own, before, name):
    own_pair, far, beyond = evens
    x_pairs = swapped(x_sent, 2)
    half = WINDOW // 2

    def kernel(own, own_ref, far_ref, beyond_ref, x_ref, *refs):
        out = refs[-1]
        evens = [own_ref, x_ref.at[0], far_ref, x_ref.at[1], beyond_ref]
        low_c = lax.rem(own[0], 2)
        for bit in range(2):

            @pl.when(low_c == bit)
            def _(bit=bit):
                for place in range(half):
                    out[place] = evens[place + bit][...]

    operands = [own_pair, far, beyond, x_pairs]
    (c_sent,) = small_kernel(
        kernel, own, operands, [whole_block(part.shape) for part in operands],
        [(half, *own_pair.shape)], before, name,
    )
    return own_pair, far, x_pairs, swapped(c_sent, 1)


def wide(part):
    return part.astype(jnp.float32)


def fold_cores(even, got, own, before, name):
    half = WINDOW // 2

    def kernel(own, even_ref, got_ref, *refs):
        sent, kept = refs[-2:]
        for bit in range(2):

            @pl.when(lax.rem(own[0], 2) == bit)
            def _(bit=bit):
                for place in range(half + 1):
                    out = sent.at[place // 2] if place % 2 else kept.at[place // 2]
                    total = None
                    if place < half:
                        total = wide(even_ref[place])
                    if 0 <= place - bit < half:
                        more = wide(got_ref[place - bit])
                        total = more if total is None else total + more
                    out[...] = jnp.zeros(out.shape, out.dtype) if total is None else total.astype(out.dtype)

    shape = even.shape[1:]
    return small_kernel(
        kernel, own, [even, got], [whole_block(even.shape)] * 2,
        [(half // 2, *shape), (half // 2 + 1, *shape)], before, name,
    )


def fold_x(parts, own, before, name, through=()):
    count = len(parts)
    operands = [array for sent, kept in parts for array in (kept, swapped(sent, 2))]
    shape = operands[0].shape[1:]

    def kernel(own, *refs):
        outs = refs[-3:]
        for bit in range(2):

            @pl.when(lax.rem(own[0] // 2, 2) == bit)
            def _(bit=bit):
                for index in range(count):
                    kept, got = refs[2 * index : 2 * index + 2]
                    for place, out in enumerate(outs):
                        total = wide(kept[place])
                        if 0 <= place - bit < got.shape[0]:
                            total = total + wide(got[place - bit])
                        out[index] = total.astype(out.dtype)

    return small_kernel(
        kernel, own, operands, [whole_block(part.shape) for part in operands], [(count, *shape)] * 3,
        before, name, through,
    )


def groups_of(refs, sizes):
    return [ref.at[index] for ref, size in zip(refs, sizes) for index in range(size)]


def fold_z(parts, own, before, name, cost):
    sizes = [part[0].shape[0] for part in parts]
    operands = [part[0] for part in parts] + [part[1] for part in parts]

    def kernel(own, *refs):
        out = refs[-1]
        shares, others = groups_of(refs, sizes), groups_of(refs[len(sizes) :], sizes)
        for index, (share, other) in enumerate(zip(shares, others)):
            out[index] = (wide(share[...]) + wide(other[...])).astype(out.dtype)

    return small_kernel(
        kernel, own, operands, [whole_block(part.shape) for part in operands],
        [(sum(sizes), *operands[0].shape[1:])], before, name, cost=cost,
    )[0]


def finish(terms, count, own, before, name):
    operands = [array for array, _ in terms]
    kinds, depth, rows = operands[0].shape[1:]

    def kernel(own, *refs):
        out = refs[-1]
        for index in range(count):
            parts = [
                ref.at[index - first]
                for ref, (array, first) in zip(refs, terms)
                if 0 <= index - first < array.shape[0]
            ]
            for kind in range(kinds):
                total = functools.reduce(jnp.add, [wide(part[kind]) for part in parts])
                out[index, kind] = total.T.astype(out.dtype)

    return small_kernel(
        kernel, own, operands, [whole_block(part.shape) for part in operands],
        [(count, kinds, rows, depth)], before, name,
    )[0]


def body(queries, key_vectors, value_vectors, output_gradient, doc_lengths):
    own = lax.axis_index("ctx")
    own_info = own.reshape(1).astype(jnp.int32)
    local = key_vectors.shape[0]
    all_groups = key_vectors.shape[1] // HEAD_SIZE
    tp_count = lax.axis_size("tp")
    groups = all_groups // tp_count
    tp_own = lax.axis_index("tp")
    tp_info = tp_own.reshape(1).astype(jnp.int32)

    middle = (groups + 1) // 2
    bounds = [(0, middle)] + ([(middle, groups)] if groups > 1 else [])
    packed = pack_for_tp(key_vectors, value_vectors, groups, tp_info)
    received = tp_received(lambda place, step: packed[step])
    chunks = join_tokens([packed[0], *received], bounds, tp_info)
    evens = [even_window(chunk) for chunk in chunks]
    x_sent = [
        for_x_swap(part, own_info, [other[1] for other in evens[1:]] if chunk == 0 else [], f"x_swap_{chunk}")
        for chunk, part in enumerate(evens)
    ]
    windows = [whole_window(evens[0], x_sent[0], own_info, x_sent[1:], "core_swap_0")]
    buffers = ()
    results, got, folded, nears, passing = [], [], [], [], []

    def fold_next_cores(before):
        group = len(folded)
        folded.append(fold_cores(results[group][2], got[group], own_info, before, f"fold_cores_{group}"))

    def fold_next_x(last, before, through=()):
        first = sum(part.shape[0] for part in nears)
        near, far, beyond, *handed = fold_x(folded[first : last + 1], own_info, before, f"fold_x_{first}", through)
        nears.append(near)
        if first == 0 and groups > 2:
            passing.append((shifted(far, -(WINDOW // 2)), shifted(beyond, -WINDOW)))
        else:
            passing.append((far, shifted(beyond, -(WINDOW // 2))))
        return handed

    for group in range(groups):
        waits = []
        if group >= 2:
            waits.append(folded[group - 2][0])
        if group >= 2 and group == groups - 1:
            waits.append(folded[group - 1][0])
        if group >= 3:
            waits.append(nears[-1])
        chunk = 0 if group < middle else 1
        results.append(
            attend_group(
                group, groups, own_info, doc_lengths, queries, output_gradient,
                windows[chunk], group - bounds[chunk][0], buffers, waits,
            )
        )
        *buffers, even, odd = results[-1]
        if 3 <= groups == group + 1:
            (odd,) = fold_next_x(group - 1, [part for pair in passing for part in pair], [odd])
        elif group >= 2:
            (odd,) = fold_next_x(group - 2, [], [odd])
        got.append(swapped(odd, 1))
        if group == 0 and groups > 1:
            windows.append(whole_window(evens[1], x_sent[1], own_info, [even], "core_swap_1"))
        if group >= 1 and len(folded) < group:
            fold_next_cores([even])
        if 2 <= group == groups - 2:
            fold_next_cores([])
    while len(folded) < groups:
        fold_next_cores([])
    while sum(part.shape[0] for part in nears) < groups:
        fold_next_x(sum(part.shape[0] for part in nears), [])

    def exchanged(total):
        def tokens_of(place, step=0):
            return lax.dynamic_slice_in_dim(total, place * local, local, total.ndim - 2)

        return in_tp_order(tokens_of(tp_own), tp_received(tokens_of))

    direct = 1 if groups > 2 else 0
    terms = [(part, 0) for part in (nears[0], *passing[0])] if direct else []
    split = len(passing) - 1
    early = groups - nears[-1].shape[0]
    late = fold_z(passing[split:], own_info, [], "fold_z_late", 1)
    if split > direct:
        joint = fold_z(passing[direct:split], own_info, nears[-1:], "fold_z_early", 1 << 34)
        terms += [(part, direct) for part in (nears[direct], shifted(joint, -(WINDOW // 2)))]
    finished = [finish(terms, early, own_info, [late], "finish_early")] if early else []
    terms = [(nears[-1], 0), (shifted(late, -(WINDOW // 2)), 0)]
    finished.append(finish(terms, groups - early, own_info, finished, "finish_late"))
    totals = [exchanged(part) for part in finished]
    ordered = [
        [part[source][group] for part in totals for group in range(part[source].shape[0])]
        for source in range(tp_count)
    ]

    def output(which):
        return jnp.concatenate([part[which] for source in ordered for part in source], axis=1)

    out, dq = buffers
    return out, dq, output(0), output(1)


def solution(mesh):
    tokens = P(("ctx", "tp"), None)
    heads = P("ctx", "tp")
    return jax.shard_map(
        body,
        mesh=mesh,
        in_specs=(heads, tokens, tokens, heads, P()),
        out_specs=(heads, heads, tokens, tokens),
        check_vma=False,
    )
```

```python
import functools
import math

import jax
import jax.numpy as jnp
from jax import lax
from jax.experimental import pallas as pl
from jax.experimental.pallas import tpu as pltpu
from jax.sharding import PartitionSpec as P

HEAD_SIZE = 128
WINDOW = 8
HEADS_AT_ONCE = 2
KERNEL_VMEM = 44 * 1024 * 1024
SCORE_SCALE = 1.0 / math.sqrt(HEAD_SIZE)
LOG2E = math.log2(math.e)
MASKED = -1e30


def dot(a, b):
    return jnp.dot(a, b, preferred_element_type=jnp.float32)


def dot_rows(a, b):
    return lax.dot_general(a, b, (((1,), (1,)), ((), ())), preferred_element_type=jnp.float32)


def group_kernel(
    group, place, heads, unread, own, doc_lengths, q_hbm, g_hbm, own_hbm, far_hbm, x_hbm, c_hbm, *rest
):
    out_hbm, dq_hbm, even_hbm, odd_hbm, *scratch = rest[unread:]
    (
        q_in, q_all, q_turned, g_in, g_all, g_turned, k_win, v_win, outs, even, odd,
        bias, scores, weights, grads, highest, summed, delta, dq_acc,
        sems, k_sems, v_sems, grad_sems,
    ) = scratch
    rows = q_hbm.shape[0]
    at_once = min(heads, HEADS_AT_ONCE)
    repeats = 2 * rows // HEAD_SIZE
    half = WINDOW // 2
    spans = [slice(head * rows, (head + 1) * rows) for head in range(heads)]
    batches = [slice(head * rows, (head + at_once) * rows) for head in range(0, heads, at_once)]

    width = heads * HEAD_SIZE
    own_columns = pl.ds(group * width, width)
    columns = [slice(head * HEAD_SIZE, (head + 1) * HEAD_SIZE) for head in range(heads)]
    q_copy = pltpu.make_async_copy(q_hbm.at[:, own_columns], q_in, sems.at[0])
    g_copy = pltpu.make_async_copy(g_hbm.at[:, own_columns], g_in, sems.at[1])
    out_copy = pltpu.make_async_copy(outs, out_hbm.at[:, own_columns], sems.at[2])
    dq_copy = pltpu.make_async_copy(q_in, dq_hbm.at[:, own_columns], sems.at[3])
    window = [
        own_hbm, c_hbm.at[0], x_hbm.at[0], c_hbm.at[1], far_hbm, c_hbm.at[2], x_hbm.at[1], c_hbm.at[3]
    ]

    def window_copy(kind, pair, side, source):
        target, sems = (v_win.at[pair, pl.ds(side * rows, rows), pl.ds(0, HEAD_SIZE)], v_sems) if kind else (
            k_win.at[pair, pl.ds(side * rows, rows)], k_sems
        )
        block = source.at[kind, :, pl.ds(place * HEAD_SIZE, HEAD_SIZE)]
        return pltpu.make_async_copy(block, target, sems.at[2 * pair + side])

    def grad_copies(pair):
        return [
            pltpu.make_async_copy(even.at[pair], even_hbm.at[pair], grad_sems.at[2 * pair]),
            pltpu.make_async_copy(odd.at[pair], odd_hbm.at[pair], grad_sems.at[2 * pair + 1]),
        ]

    first = own[0] * rows
    doc_start = 0
    start = 0
    for doc in range(doc_lengths.shape[0]):
        doc_start = jnp.where(first >= start, start, doc_start)
        start = start + doc_lengths[doc]
    needed = jnp.clip(own[0] - doc_start // rows + 1, 1, WINDOW)
    trips = (needed + 1) // 2
    q_copy.start()
    for kind in range(2):
        for pair in range(half):

            @pl.when(pair < trips)
            def _(kind=kind, pair=pair):
                for side in range(2):
                    window_copy(kind, pair, side, window[2 * pair + side]).start()

    g_copy.start()
    query_pos = first + lax.broadcasted_iota(jnp.int32, (rows, HEAD_SIZE), 0)
    low = jnp.zeros((rows, HEAD_SIZE), jnp.int32)
    start = 0
    for doc in range(doc_lengths.shape[0]):
        low = jnp.where(query_pos >= start, start, low)
        start = start + doc_lengths[doc]
    v_win[:, :, HEAD_SIZE:] = jnp.ones((half, 2 * rows, HEAD_SIZE), jnp.bfloat16)

    def each_pair(step):
        def body(pair, carry):
            step(pair, False)
            return carry

        step(0, True)
        lax.fori_loop(1, trips, body, 0)

    def score_pair(pair, is_first):
        for spot in range(repeats):
            offset = 2 * pair + spot // (repeats // 2)
            key_pos = (
                first - offset * rows + spot % (repeats // 2) * HEAD_SIZE
                + lax.broadcasted_iota(jnp.int32, (rows, HEAD_SIZE), 1)
            )
            allowed = (key_pos >= low) & (key_pos <= query_pos)
            bias[:, spot * HEAD_SIZE : (spot + 1) * HEAD_SIZE] = jnp.where(allowed, 0.0, MASKED)
        for side in range(2):
            window_copy(0, pair, side, own_hbm).wait()
        for batch in batches:
            part = dot_rows(q_all[batch, :], k_win[pair])
            for head in range(at_once):
                here = slice(batch.start + head * rows, batch.start + (head + 1) * rows)
                if is_first:
                    q_turned[:, here] = q_all[here, :].T
                piece = part[head * rows : (head + 1) * rows] * (SCORE_SCALE * LOG2E) + bias[...]
                scores[pair, here, :] = piece
                pieces = [piece[:, spot * HEAD_SIZE : (spot + 1) * HEAD_SIZE] for spot in range(repeats)]
                most = functools.reduce(jnp.maximum, pieces)
                highest[here, :] = most if is_first else jnp.maximum(highest[here, :], most)

    q_copy.wait()
    for span, column in zip(spans, columns):
        q_all[span, :] = q_in[:, column]
    each_pair(score_pair)

    def sum_pair(pair, is_first):
        for side in range(2):
            window_copy(1, pair, side, own_hbm).wait()
        for batch in batches:
            for head in range(at_once):
                here = slice(batch.start + head * rows, batch.start + (head + 1) * rows)
                top = highest[here, :]
                if is_first:
                    top = jnp.broadcast_to(jnp.max(top, axis=1, keepdims=True), (rows, HEAD_SIZE))
                    highest[here, :] = top
                top = jnp.concatenate([top] * repeats, axis=1)
                weights[pair, here, :] = jnp.exp2(scores[pair, here, :] - top).astype(jnp.bfloat16)
            part = dot(weights[pair, batch, :], v_win[pair])
            summed[batch, :] = part if is_first else summed[batch, :] + part

    each_pair(sum_pair)

    def close_head(head):
        span, column = spans[head], columns[head]
        inverse = 1.0 / summed[span, HEAD_SIZE:]
        output = (summed[span, :HEAD_SIZE] * inverse).astype(jnp.bfloat16)
        outs[:, column] = output
        scaled = (g_in[:, column].astype(jnp.float32) * inverse).astype(jnp.bfloat16)
        g_all[span, :] = scaled
        g_turned[:, span] = scaled.T
        terms = output.astype(jnp.float32) * scaled.astype(jnp.float32)
        upper = terms.astype(jnp.bfloat16)
        grads[span, :HEAD_SIZE] = upper
        grads[span, HEAD_SIZE : 2 * HEAD_SIZE] = (terms - upper.astype(jnp.float32)).astype(jnp.bfloat16)

    g_copy.wait()
    ones = jnp.ones((2 * HEAD_SIZE, HEAD_SIZE), jnp.bfloat16)

    def grad_pair(pair, is_first):
        for number, batch in enumerate(batches):
            if is_first:
                for head in range(number * at_once, (number + 1) * at_once):
                    close_head(head)
                delta[batch, :] = dot(grads[batch, : 2 * HEAD_SIZE], ones)
            part = dot_rows(g_all[batch, :], v_win[pair, :, :HEAD_SIZE])
            for head in range(at_once):
                here = slice(batch.start + head * rows, batch.start + (head + 1) * rows)
                piece = part[head * rows : (head + 1) * rows] - jnp.concatenate([delta[here, :]] * repeats, axis=1)
                grads[here, :] = (weights[pair, here, :].astype(jnp.float32) * piece).astype(jnp.bfloat16)
            part = dot(grads[batch, :], k_win[pair])
            dq_acc[batch, :] = part if is_first else dq_acc[batch, :] + part
        dk = (dot(q_turned[...], grads[...]) * SCORE_SCALE).astype(jnp.bfloat16)
        dv = dot(g_turned[...], weights[pair]).astype(jnp.bfloat16)
        even[pair, 0] = dk[:, :rows]
        even[pair, 1] = dv[:, :rows]
        odd[pair, 0] = dk[:, rows:]
        odd[pair, 1] = dv[:, rows:]
        for copy in grad_copies(pair) + ([out_copy] if is_first else []):
            copy.start()

    each_pair(grad_pair)

    def clear_pair(pair, carry):
        even[pair] = jnp.zeros(even.shape[1:], jnp.bfloat16)
        odd[pair] = jnp.zeros(odd.shape[1:], jnp.bfloat16)
        for copy in grad_copies(pair):
            copy.start()
        return carry

    lax.fori_loop(trips, half, clear_pair, 0)
    for span, column in zip(spans, columns):
        q_in[:, column] = (dq_acc[span, :] * SCORE_SCALE).astype(jnp.bfloat16)
    dq_copy.start()
    for copy in [out_copy] + [copy for pair in range(half) for copy in grad_copies(pair)] + [dq_copy]:
        copy.wait()


def attend_group(
    group, groups, own, doc_lengths, queries, gradient, window, place, buffers, before
):
    rows, width = queries.shape
    columns = width // groups
    heads = columns // HEAD_SIZE
    keys = WINDOW * rows
    stacked = heads * rows
    half = WINDOW // 2
    grads = jax.ShapeDtypeStruct((half, 2, HEAD_SIZE, rows), jnp.bfloat16)
    unread = len(buffers) + len(before)
    anywhere = pl.BlockSpec(memory_space=pl.ANY)
    short = lambda *shape: pltpu.VMEM(shape, jnp.bfloat16)
    full = lambda *shape: pltpu.VMEM(shape, jnp.float32)
    sems = lambda count: pltpu.SemaphoreType.DMA((count,))
    return pl.pallas_call(
        functools.partial(group_kernel, group, place, heads, unread),
        grid_spec=pltpu.PrefetchScalarGridSpec(
            num_scalar_prefetch=2,
            grid=(1,),
            in_specs=[anywhere] * (6 + unread),
            out_specs=[anywhere] * 4,
            scratch_shapes=[
                short(rows, columns),
                short(stacked, HEAD_SIZE),
                short(HEAD_SIZE, stacked),
                short(rows, columns),
                short(stacked, HEAD_SIZE),
                short(HEAD_SIZE, stacked),
                short(half, 2 * rows, HEAD_SIZE),
                short(half, 2 * rows, 2 * HEAD_SIZE),
                short(rows, columns),
                short(*grads.shape),
                short(*grads.shape),
                full(rows, 2 * rows),
                full(half, stacked, 2 * rows),
                short(half, stacked, 2 * rows),
                short(stacked, 2 * rows),
                full(stacked, HEAD_SIZE),
                full(stacked, 2 * HEAD_SIZE),
                full(stacked, HEAD_SIZE),
                full(stacked, HEAD_SIZE),
                sems(4), sems(WINDOW), sems(WINDOW), sems(WINDOW),
            ],
        ),
        out_shape=[
            jax.ShapeDtypeStruct(queries.shape, jnp.bfloat16),
            jax.ShapeDtypeStruct(queries.shape, jnp.bfloat16),
            grads,
            grads,
        ],
        input_output_aliases={8 + number: number for number in range(len(buffers))},
        compiler_params=pltpu.CompilerParams(vmem_limit_bytes=KERNEL_VMEM),
        cost_estimate=pl.CostEstimate(
            flops=4 * 6 * 2 * heads * rows * keys * HEAD_SIZE,
            bytes_accessed=8 * rows * columns + 8 * keys * HEAD_SIZE,
            transcendentals=heads * rows * keys,
        ),
        name=f"attend_group_{group}",
    )(own, doc_lengths, queries, gradient, *window, *buffers, *before)


def shifted(value, steps):
    count = lax.axis_size("ctx")
    sources = range(max(0, -steps), min(count, count - steps))
    return lax.ppermute(value, "ctx", [(source, source + steps) for source in sources])


def swapped(value, bit):
    return lax.ppermute(value, "ctx", [(place, place ^ bit) for place in range(lax.axis_size("ctx"))])


def tp_received(block_for):
    count = lax.axis_size("tp")
    own = lax.axis_index("tp")
    received = []
    for step in range(1, count):
        sent = block_for(lax.rem(own + step, count), step)
        received.append(lax.ppermute(sent, "tp", [(place, (place + step) % count) for place in range(count)]))
    return received


def in_tp_order(mine, received):
    count = lax.axis_size("tp")
    own = lax.axis_index("tp")
    parts = [mine, *received]
    ordered = []
    for place in range(count):
        part = parts[0]
        for step in range(1, count):
            part = jnp.where(lax.rem(own - step + count, count) == place, parts[step], part)
        ordered.append(part)
    return ordered


def whole_block(shape):
    return pl.BlockSpec(shape, lambda i, *_: (0,) * len(shape))


def small_kernel(kernel, scalars, operands, specs, outs, before, name, through=(), cost=1):
    if through:
        inner, handed = kernel, len(through)
        kernel = lambda *refs: inner(*refs[:-handed])
    first = 1 + len(operands) + len(before)
    return pl.pallas_call(
        kernel,
        grid_spec=pltpu.PrefetchScalarGridSpec(
            num_scalar_prefetch=1,
            grid=(1,),
            in_specs=specs + [pl.BlockSpec(memory_space=pl.ANY)] * (len(before) + len(through)),
            out_specs=[whole_block(shape) for shape in outs] + [pl.BlockSpec(memory_space=pl.ANY)] * len(through),
        ),
        out_shape=[jax.ShapeDtypeStruct(shape, jnp.bfloat16) for shape in outs]
        + [jax.ShapeDtypeStruct(part.shape, part.dtype) for part in through],
        input_output_aliases={first + number: len(outs) + number for number in range(len(through))},
        compiler_params=pltpu.CompilerParams(vmem_limit_bytes=32 * 1024 * 1024),
        cost_estimate=pl.CostEstimate(flops=cost, bytes_accessed=1, transcendentals=0),
        name=name,
    )(scalars, *operands, *before, *through)


def pack_for_tp(key_vectors, value_vectors, groups, bounds, tp_own):
    count = lax.axis_size("tp")
    local = key_vectors.shape[0]

    def kernel(own, key_hbm, value_hbm, *refs):
        outs, sems = refs[:-1], refs[-1]
        copies = []
        for chunk, (first, last) in enumerate(bounds):
            for step in range(count):
                place = lax.rem(own[0] + step, count) * groups + first
                block = pl.ds(pl.multiple_of(place * HEAD_SIZE, HEAD_SIZE), (last - first) * HEAD_SIZE)
                out = outs[chunk * count + step]
                for kind, source in enumerate((key_hbm, value_hbm)):
                    target = out.at[kind]
                    if step == 0:
                        target = out.at[kind, pl.ds(pl.multiple_of(own[0] * local, local), local)]
                    copies.append(pltpu.make_async_copy(source.at[:, block], target, sems.at[len(copies)]))
        for copy in copies:
            copy.start()
        for copy in copies:
            copy.wait()

    shapes = [
        (2, local * (1 if step else count), (last - first) * HEAD_SIZE)
        for first, last in bounds
        for step in range(count)
    ]
    packed = pl.pallas_call(
        kernel,
        grid_spec=pltpu.PrefetchScalarGridSpec(
            num_scalar_prefetch=1,
            grid=(1,),
            in_specs=[pl.BlockSpec(memory_space=pltpu.HBM)] * 2,
            out_specs=[whole_block(shape) for shape in shapes],
            scratch_shapes=[pltpu.SemaphoreType.DMA((2 * len(shapes),))],
        ),
        out_shape=[jax.ShapeDtypeStruct(shape, jnp.bfloat16) for shape in shapes],
        name="pack_for_tp",
    )(tp_own, key_vectors, value_vectors)
    return [packed[chunk * count : (chunk + 1) * count] for chunk in range(len(bounds))]


def join_tokens(tokens, received, tp_own, name):
    count = len(received) + 1
    local = tokens.shape[1] // count

    def kernel(own, *refs):
        parts, out, sems = refs[: count - 1], refs[count], refs[-1]
        copies = []
        for step, part in enumerate(parts, 1):
            source = lax.rem(own[0] - step + count, count)
            rows = pl.ds(pl.multiple_of(source * local, local), local)
            for kind in range(2):
                sem = sems.at[len(copies)]
                copies.append(pltpu.make_async_copy(part.at[kind], out.at[kind, rows], sem))
        for copy in copies:
            copy.start()
        for copy in copies:
            copy.wait()

    anywhere = pl.BlockSpec(memory_space=pl.ANY)
    return pl.pallas_call(
        kernel,
        grid_spec=pltpu.PrefetchScalarGridSpec(
            num_scalar_prefetch=1,
            grid=(1,),
            in_specs=[anywhere] * count,
            out_specs=anywhere,
            scratch_shapes=[pltpu.SemaphoreType.DMA((2 * count,))],
        ),
        out_shape=jax.ShapeDtypeStruct(tokens.shape, tokens.dtype),
        input_output_aliases={count: 0},
        name=name,
    )(tp_own, *received, tokens)


def even_window(own_pair):
    far = shifted(own_pair, WINDOW // 2)
    return own_pair, far, shifted(far, WINDOW // 2)


def for_x_swap(evens, own, before, name):
    def kernel(own, *refs):
        out = refs[-1]
        for bit in range(2):

            @pl.when(lax.rem(own[0] // 2, 2) == bit)
            def _(bit=bit):
                for place in range(2):
                    out[place] = refs[place + bit][...]

    return small_kernel(
        kernel, own, evens, [whole_block(part.shape) for part in evens], [(2, *evens[0].shape)], before, name
    )[0]


def whole_window(evens, x_sent, own, before, name):
    own_pair, far, beyond = evens
    x_pairs = swapped(x_sent, 2)
    half = WINDOW // 2

    def kernel(own, own_ref, far_ref, beyond_ref, x_ref, *refs):
        out = refs[-1]
        evens = [own_ref, x_ref.at[0], far_ref, x_ref.at[1], beyond_ref]
        low_c = lax.rem(own[0], 2)
        for bit in range(2):

            @pl.when(low_c == bit)
            def _(bit=bit):
                for place in range(half):
                    out[place] = evens[place + bit][...]

    operands = [own_pair, far, beyond, x_pairs]
    (c_sent,) = small_kernel(
        kernel, own, operands, [whole_block(part.shape) for part in operands],
        [(half, *own_pair.shape)], before, name,
    )
    return own_pair, far, x_pairs, swapped(c_sent, 1)


def wide(part):
    return part.astype(jnp.float32)


def fold_cores(even, got, own, before, name):
    half = WINDOW // 2

    def kernel(own, even_ref, got_ref, *refs):
        sent, kept = refs[-2:]
        for bit in range(2):

            @pl.when(lax.rem(own[0], 2) == bit)
            def _(bit=bit):
                for place in range(half + 1):
                    out = sent.at[place // 2] if place % 2 else kept.at[place // 2]
                    total = None
                    if place < half:
                        total = wide(even_ref[place])
                    if 0 <= place - bit < half:
                        more = wide(got_ref[place - bit])
                        total = more if total is None else total + more
                    out[...] = jnp.zeros(out.shape, out.dtype) if total is None else total.astype(out.dtype)

    shape = even.shape[1:]
    return small_kernel(
        kernel, own, [even, got], [whole_block(even.shape)] * 2,
        [(half // 2, *shape), (half // 2 + 1, *shape)], before, name,
    )


def fold_x(parts, own, before, name, through=()):
    count = len(parts)
    operands = [array for sent, kept in parts for array in (kept, swapped(sent, 2))]
    shape = operands[0].shape[1:]

    def kernel(own, *refs):
        outs = refs[-3:]
        for bit in range(2):

            @pl.when(lax.rem(own[0] // 2, 2) == bit)
            def _(bit=bit):
                for index in range(count):
                    kept, got = refs[2 * index : 2 * index + 2]
                    for place, out in enumerate(outs):
                        total = wide(kept[place])
                        if 0 <= place - bit < got.shape[0]:
                            total = total + wide(got[place - bit])
                        out[index] = total.astype(out.dtype)

    return small_kernel(
        kernel, own, operands, [whole_block(part.shape) for part in operands], [(count, *shape)] * 3,
        before, name, through,
    )


def groups_of(refs, sizes):
    return [ref.at[index] for ref, size in zip(refs, sizes) for index in range(size)]


def fold_z(parts, own, before, name, cost):
    sizes = [part[0].shape[0] for part in parts]
    operands = [part[0] for part in parts] + [part[1] for part in parts]

    def kernel(own, *refs):
        out = refs[-1]
        shares, others = groups_of(refs, sizes), groups_of(refs[len(sizes) :], sizes)
        for index, (share, other) in enumerate(zip(shares, others)):
            out[index] = (wide(share[...]) + wide(other[...])).astype(out.dtype)

    return small_kernel(
        kernel, own, operands, [whole_block(part.shape) for part in operands],
        [(sum(sizes), *operands[0].shape[1:])], before, name, cost=cost,
    )[0]


def finish(terms, count, own, before, name):
    operands = [array for array, _ in terms]
    kinds, depth, rows = operands[0].shape[1:]

    def kernel(own, *refs):
        out = refs[-1]
        for index in range(count):
            parts = [
                ref.at[index - first]
                for ref, (array, first) in zip(refs, terms)
                if 0 <= index - first < array.shape[0]
            ]
            for kind in range(kinds):
                total = functools.reduce(jnp.add, [wide(part[kind]) for part in parts])
                out[index, kind] = total.T.astype(out.dtype)

    return small_kernel(
        kernel, own, operands, [whole_block(part.shape) for part in operands],
        [(count, kinds, rows, depth)], before, name,
    )[0]


def body(queries, key_vectors, value_vectors, output_gradient, doc_lengths):
    own = lax.axis_index("ctx")
    own_info = own.reshape(1).astype(jnp.int32)
    local = key_vectors.shape[0]
    all_groups = key_vectors.shape[1] // HEAD_SIZE
    tp_count = lax.axis_size("tp")
    groups = all_groups // tp_count
    tp_own = lax.axis_index("tp")
    tp_info = tp_own.reshape(1).astype(jnp.int32)

    middle = (groups + 1) // 2
    bounds = [(0, middle)] + ([(middle, groups)] if groups > 1 else [])
    chunks = []
    received = []
    for number, (tokens, *sent) in enumerate(pack_for_tp(key_vectors, value_vectors, groups, bounds, tp_info)):
        if number:
            sent = small_kernel(lambda *refs: None, tp_info, [], [], [], received, "second_exchange", sent)
        received = tp_received(lambda place, step: sent[step - 1])
        chunks.append(join_tokens(tokens, received, tp_info, f"join_tokens_{number}"))
    evens = [even_window(chunk) for chunk in chunks]
    x_sent = [
        for_x_swap(part, own_info, [other[1] for other in evens[1:]] if chunk == 0 else [], f"x_swap_{chunk}")
        for chunk, part in enumerate(evens)
    ]
    windows = [whole_window(evens[0], x_sent[0], own_info, x_sent[1:], "core_swap_0")]
    buffers = ()
    results, got, folded, nears, passing = [], [], [], [], []

    def fold_next_cores(before):
        group = len(folded)
        folded.append(fold_cores(results[group][2], got[group], own_info, before, f"fold_cores_{group}"))

    def fold_next_x(last, before, through=()):
        first = sum(part.shape[0] for part in nears)
        near, far, beyond, *handed = fold_x(folded[first : last + 1], own_info, before, f"fold_x_{first}", through)
        nears.append(near)
        if first == 0 and groups > 2:
            passing.append((shifted(far, -(WINDOW // 2)), shifted(beyond, -WINDOW)))
        else:
            passing.append((far, shifted(beyond, -(WINDOW // 2))))
        return handed

    for group in range(groups):
        waits = []
        if group >= 2:
            waits.append(folded[group - 2][0])
        if group >= 2 and group == groups - 1:
            waits.append(folded[group - 1][0])
        if group >= 3:
            waits.append(nears[-1])
        chunk = 0 if group < middle else 1
        results.append(
            attend_group(
                group, groups, own_info, doc_lengths, queries, output_gradient,
                windows[chunk], group - bounds[chunk][0], buffers, waits,
            )
        )
        *buffers, even, odd = results[-1]
        if 3 <= groups == group + 1:
            (odd,) = fold_next_x(group - 1, [part for pair in passing for part in pair], [odd])
        elif group >= 2:
            (odd,) = fold_next_x(group - 2, [], [odd])
        got.append(swapped(odd, 1))
        if group == 0 and groups > 1:
            windows.append(whole_window(evens[1], x_sent[1], own_info, [even], "core_swap_1"))
        if group >= 1 and len(folded) < group:
            fold_next_cores([even])
        if 2 <= group == groups - 2:
            fold_next_cores([])
    while len(folded) < groups:
        fold_next_cores([])
    while sum(part.shape[0] for part in nears) < groups:
        fold_next_x(sum(part.shape[0] for part in nears), [])

    def exchanged(total):
        def tokens_of(place, step=0):
            return lax.dynamic_slice_in_dim(total, place * local, local, total.ndim - 2)

        return in_tp_order(tokens_of(tp_own), tp_received(tokens_of))

    direct = 1 if groups > 2 else 0
    terms = [(part, 0) for part in (nears[0], *passing[0])] if direct else []
    split = len(passing) - 1
    early = groups - nears[-1].shape[0]
    late = fold_z(passing[split:], own_info, [], "fold_z_late", 1)
    if split > direct:
        joint = fold_z(passing[direct:split], own_info, nears[-1:], "fold_z_early", 1 << 34)
        terms += [(part, direct) for part in (nears[direct], shifted(joint, -(WINDOW // 2)))]
    finished = [finish(terms, early, own_info, [late], "finish_early")] if early else []
    terms = [(nears[-1], 0), (shifted(late, -(WINDOW // 2)), 0)]
    finished.append(finish(terms, groups - early, own_info, finished, "finish_late"))
    totals = [exchanged(part) for part in finished]
    ordered = [
        [part[source][group] for part in totals for group in range(part[source].shape[0])]
        for source in range(tp_count)
    ]

    def output(which):
        return jnp.concatenate([part[which] for source in ordered for part in source], axis=1)

    out, dq = buffers
    return out, dq, output(0), output(1)


def solution(mesh):
    tokens = P(("ctx", "tp"), None)
    heads = P("ctx", "tp")
    return jax.shard_map(
        body,
        mesh=mesh,
        in_specs=(heads, tokens, tokens, heads, P()),
        out_specs=(heads, heads, tokens, tokens),
        check_vma=False,
    )
```

```python
import functools
import math

import jax
import jax.numpy as jnp
from jax import lax
from jax.experimental import pallas as pl
from jax.experimental.pallas import tpu as pltpu
from jax.sharding import PartitionSpec as P

HEAD_SIZE = 128
WINDOW = 8
HEADS_AT_ONCE = 2
KERNEL_VMEM = 44 * 1024 * 1024
SCORE_SCALE = 1.0 / math.sqrt(HEAD_SIZE)
LOG2E = math.log2(math.e)
MASKED = -1e30


def dot(a, b):
    return jnp.dot(a, b, preferred_element_type=jnp.float32)


def dot_rows(a, b):
    return lax.dot_general(a, b, (((1,), (1,)), ((), ())), preferred_element_type=jnp.float32)


def group_kernel(
    group, place, heads, unread, own, doc_lengths,
    q_hbm, g_hbm, own_hbm, far_hbm, near_x_hbm, far_x_hbm, c_hbm, *rest,
):
    out_hbm, dq_hbm, even_hbm, odd_hbm, *scratch = rest[unread:]
    (
        q_in, q_all, q_turned, g_in, g_all, g_turned, k_win, v_win, outs, even, odd,
        bias, scores, weights, grads, highest, summed, delta, dq_acc,
        sems, k_sems, v_sems, grad_sems,
    ) = scratch
    rows = q_hbm.shape[0]
    at_once = min(heads, HEADS_AT_ONCE)
    repeats = 2 * rows // HEAD_SIZE
    half = WINDOW // 2
    spans = [slice(head * rows, (head + 1) * rows) for head in range(heads)]
    batches = [slice(head * rows, (head + at_once) * rows) for head in range(0, heads, at_once)]

    width = heads * HEAD_SIZE
    own_columns = pl.ds(group * width, width)
    columns = [slice(head * HEAD_SIZE, (head + 1) * HEAD_SIZE) for head in range(heads)]
    q_copy = pltpu.make_async_copy(q_hbm.at[:, own_columns], q_in, sems.at[0])
    g_copy = pltpu.make_async_copy(g_hbm.at[:, own_columns], g_in, sems.at[1])
    out_copy = pltpu.make_async_copy(outs, out_hbm.at[:, own_columns], sems.at[2])
    dq_copy = pltpu.make_async_copy(q_in, dq_hbm.at[:, own_columns], sems.at[3])
    window = [
        own_hbm, c_hbm.at[0], near_x_hbm, c_hbm.at[1], far_hbm, c_hbm.at[2], far_x_hbm, c_hbm.at[3]
    ]

    def window_copy(kind, pair, side, source):
        target, sems = (v_win.at[pair, pl.ds(side * rows, rows), pl.ds(0, HEAD_SIZE)], v_sems) if kind else (
            k_win.at[pair, pl.ds(side * rows, rows)], k_sems
        )
        block = source.at[kind, :, pl.ds(place * HEAD_SIZE, HEAD_SIZE)]
        return pltpu.make_async_copy(block, target, sems.at[2 * pair + side])

    def grad_copies(pair):
        return [
            pltpu.make_async_copy(even.at[pair], even_hbm.at[pair], grad_sems.at[2 * pair]),
            pltpu.make_async_copy(odd.at[pair], odd_hbm.at[pair], grad_sems.at[2 * pair + 1]),
        ]

    first = own[0] * rows
    doc_start = 0
    start = 0
    for doc in range(doc_lengths.shape[0]):
        doc_start = jnp.where(first >= start, start, doc_start)
        start = start + doc_lengths[doc]
    needed = jnp.clip(own[0] - doc_start // rows + 1, 1, WINDOW)
    trips = (needed + 1) // 2
    q_copy.start()
    for kind in range(2):
        for pair in range(half):

            @pl.when(pair < trips)
            def _(kind=kind, pair=pair):
                for side in range(2):
                    window_copy(kind, pair, side, window[2 * pair + side]).start()

    g_copy.start()
    query_pos = first + lax.broadcasted_iota(jnp.int32, (rows, HEAD_SIZE), 0)
    low = jnp.zeros((rows, HEAD_SIZE), jnp.int32)
    start = 0
    for doc in range(doc_lengths.shape[0]):
        low = jnp.where(query_pos >= start, start, low)
        start = start + doc_lengths[doc]
    v_win[:, :, HEAD_SIZE:] = jnp.ones((half, 2 * rows, HEAD_SIZE), jnp.bfloat16)

    def each_pair(step):
        def body(pair, carry):
            step(pair, False)
            return carry

        step(0, True)
        lax.fori_loop(1, trips, body, 0)

    def score_pair(pair, is_first):
        for spot in range(repeats):
            offset = 2 * pair + spot // (repeats // 2)
            key_pos = (
                first - offset * rows + spot % (repeats // 2) * HEAD_SIZE
                + lax.broadcasted_iota(jnp.int32, (rows, HEAD_SIZE), 1)
            )
            allowed = (key_pos >= low) & (key_pos <= query_pos)
            bias[:, spot * HEAD_SIZE : (spot + 1) * HEAD_SIZE] = jnp.where(allowed, 0.0, MASKED)
        for side in range(2):
            window_copy(0, pair, side, own_hbm).wait()
        for batch in batches:
            part = dot_rows(q_all[batch, :], k_win[pair])
            for head in range(at_once):
                here = slice(batch.start + head * rows, batch.start + (head + 1) * rows)
                if is_first:
                    q_turned[:, here] = q_all[here, :].T
                piece = part[head * rows : (head + 1) * rows] * (SCORE_SCALE * LOG2E) + bias[...]
                scores[pair, here, :] = piece
                pieces = [piece[:, spot * HEAD_SIZE : (spot + 1) * HEAD_SIZE] for spot in range(repeats)]
                most = functools.reduce(jnp.maximum, pieces)
                highest[here, :] = most if is_first else jnp.maximum(highest[here, :], most)

    q_copy.wait()
    for span, column in zip(spans, columns):
        q_all[span, :] = q_in[:, column]
    each_pair(score_pair)

    def sum_pair(pair, is_first):
        for side in range(2):
            window_copy(1, pair, side, own_hbm).wait()
        for batch in batches:
            for head in range(at_once):
                here = slice(batch.start + head * rows, batch.start + (head + 1) * rows)
                top = highest[here, :]
                if is_first:
                    top = jnp.broadcast_to(jnp.max(top, axis=1, keepdims=True), (rows, HEAD_SIZE))
                    highest[here, :] = top
                top = jnp.concatenate([top] * repeats, axis=1)
                weights[pair, here, :] = jnp.exp2(scores[pair, here, :] - top).astype(jnp.bfloat16)
            part = dot(weights[pair, batch, :], v_win[pair])
            summed[batch, :] = part if is_first else summed[batch, :] + part

    each_pair(sum_pair)

    def close_head(head):
        span, column = spans[head], columns[head]
        inverse = 1.0 / summed[span, HEAD_SIZE:]
        output = (summed[span, :HEAD_SIZE] * inverse).astype(jnp.bfloat16)
        outs[:, column] = output
        scaled = (g_in[:, column].astype(jnp.float32) * inverse).astype(jnp.bfloat16)
        g_all[span, :] = scaled
        g_turned[:, span] = scaled.T
        terms = output.astype(jnp.float32) * scaled.astype(jnp.float32)
        upper = terms.astype(jnp.bfloat16)
        grads[span, :HEAD_SIZE] = upper
        grads[span, HEAD_SIZE : 2 * HEAD_SIZE] = (terms - upper.astype(jnp.float32)).astype(jnp.bfloat16)

    g_copy.wait()
    ones = jnp.ones((2 * HEAD_SIZE, HEAD_SIZE), jnp.bfloat16)

    def grad_pair(pair, is_first):
        for number, batch in enumerate(batches):
            if is_first:
                for head in range(number * at_once, (number + 1) * at_once):
                    close_head(head)
                delta[batch, :] = dot(grads[batch, : 2 * HEAD_SIZE], ones)
            part = dot_rows(g_all[batch, :], v_win[pair, :, :HEAD_SIZE])
            for head in range(at_once):
                here = slice(batch.start + head * rows, batch.start + (head + 1) * rows)
                piece = part[head * rows : (head + 1) * rows] - jnp.concatenate([delta[here, :]] * repeats, axis=1)
                grads[here, :] = (weights[pair, here, :].astype(jnp.float32) * piece).astype(jnp.bfloat16)
            part = dot(grads[batch, :], k_win[pair])
            dq_acc[batch, :] = part if is_first else dq_acc[batch, :] + part
        dk = (dot(q_turned[...], grads[...]) * SCORE_SCALE).astype(jnp.bfloat16)
        dv = dot(g_turned[...], weights[pair]).astype(jnp.bfloat16)
        even[pair, 0] = dk[:, :rows]
        even[pair, 1] = dv[:, :rows]
        odd[pair, 0] = dk[:, rows:]
        odd[pair, 1] = dv[:, rows:]
        for copy in grad_copies(pair) + ([out_copy] if is_first else []):
            copy.start()

    each_pair(grad_pair)

    def clear_pair(pair, carry):
        even[pair] = jnp.zeros(even.shape[1:], jnp.bfloat16)
        odd[pair] = jnp.zeros(odd.shape[1:], jnp.bfloat16)
        for copy in grad_copies(pair):
            copy.start()
        return carry

    lax.fori_loop(trips, half, clear_pair, 0)
    for span, column in zip(spans, columns):
        q_in[:, column] = (dq_acc[span, :] * SCORE_SCALE).astype(jnp.bfloat16)
    dq_copy.start()
    for copy in [out_copy] + [copy for pair in range(half) for copy in grad_copies(pair)] + [dq_copy]:
        copy.wait()


def attend_group(
    group, groups, own, doc_lengths, queries, gradient, window, place, buffers, before
):
    rows, width = queries.shape
    columns = width // groups
    heads = columns // HEAD_SIZE
    keys = WINDOW * rows
    stacked = heads * rows
    half = WINDOW // 2
    grads = jax.ShapeDtypeStruct((half, 2, HEAD_SIZE, rows), jnp.bfloat16)
    unread = len(buffers) + len(before)
    anywhere = pl.BlockSpec(memory_space=pl.ANY)
    short = lambda *shape: pltpu.VMEM(shape, jnp.bfloat16)
    full = lambda *shape: pltpu.VMEM(shape, jnp.float32)
    sems = lambda count: pltpu.SemaphoreType.DMA((count,))
    return pl.pallas_call(
        functools.partial(group_kernel, group, place, heads, unread),
        grid_spec=pltpu.PrefetchScalarGridSpec(
            num_scalar_prefetch=2,
            grid=(1,),
            in_specs=[anywhere] * (7 + unread),
            out_specs=[anywhere] * 4,
            scratch_shapes=[
                short(rows, columns),
                short(stacked, HEAD_SIZE),
                short(HEAD_SIZE, stacked),
                short(rows, columns),
                short(stacked, HEAD_SIZE),
                short(HEAD_SIZE, stacked),
                short(half, 2 * rows, HEAD_SIZE),
                short(half, 2 * rows, 2 * HEAD_SIZE),
                short(rows, columns),
                short(*grads.shape),
                short(*grads.shape),
                full(rows, 2 * rows),
                full(half, stacked, 2 * rows),
                short(half, stacked, 2 * rows),
                short(stacked, 2 * rows),
                full(stacked, HEAD_SIZE),
                full(stacked, 2 * HEAD_SIZE),
                full(stacked, HEAD_SIZE),
                full(stacked, HEAD_SIZE),
                sems(4), sems(WINDOW), sems(WINDOW), sems(WINDOW),
            ],
        ),
        out_shape=[
            jax.ShapeDtypeStruct(queries.shape, jnp.bfloat16),
            jax.ShapeDtypeStruct(queries.shape, jnp.bfloat16),
            grads,
            grads,
        ],
        input_output_aliases={9 + number: number for number in range(len(buffers))},
        compiler_params=pltpu.CompilerParams(vmem_limit_bytes=KERNEL_VMEM),
        cost_estimate=pl.CostEstimate(
            flops=4 * 6 * 2 * heads * rows * keys * HEAD_SIZE,
            bytes_accessed=8 * rows * columns + 8 * keys * HEAD_SIZE,
            transcendentals=heads * rows * keys,
        ),
        name=f"attend_group_{group}",
    )(own, doc_lengths, queries, gradient, *window, *buffers, *before)


def shifted(value, steps):
    count = lax.axis_size("ctx")
    sources = range(max(0, -steps), min(count, count - steps))
    return lax.ppermute(value, "ctx", [(source, source + steps) for source in sources])


def swapped(value, bit):
    return lax.ppermute(value, "ctx", [(place, place ^ bit) for place in range(lax.axis_size("ctx"))])


def tp_received(block_for):
    count = lax.axis_size("tp")
    own = lax.axis_index("tp")
    received = []
    for step in range(1, count):
        sent = block_for(lax.rem(own + step, count), step)
        received.append(lax.ppermute(sent, "tp", [(place, (place + step) % count) for place in range(count)]))
    return received


def in_tp_order(mine, received):
    count = lax.axis_size("tp")
    own = lax.axis_index("tp")
    parts = [mine, *received]
    ordered = []
    for place in range(count):
        part = parts[0]
        for step in range(1, count):
            part = jnp.where(lax.rem(own - step + count, count) == place, parts[step], part)
        ordered.append(part)
    return ordered


def whole_block(shape):
    return pl.BlockSpec(shape, lambda i, *_: (0,) * len(shape))


def small_kernel(kernel, scalars, operands, specs, outs, before, name, through=(), cost=1):
    if through:
        inner, handed = kernel, len(through)
        kernel = lambda *refs: inner(*refs[:-handed])
    first = 1 + len(operands) + len(before)
    return pl.pallas_call(
        kernel,
        grid_spec=pltpu.PrefetchScalarGridSpec(
            num_scalar_prefetch=1,
            grid=(1,),
            in_specs=specs + [pl.BlockSpec(memory_space=pl.ANY)] * (len(before) + len(through)),
            out_specs=[whole_block(shape) for shape in outs] + [pl.BlockSpec(memory_space=pl.ANY)] * len(through),
        ),
        out_shape=[jax.ShapeDtypeStruct(shape, jnp.bfloat16) for shape in outs]
        + [jax.ShapeDtypeStruct(part.shape, part.dtype) for part in through],
        input_output_aliases={first + number: len(outs) + number for number in range(len(through))},
        compiler_params=pltpu.CompilerParams(vmem_limit_bytes=32 * 1024 * 1024),
        cost_estimate=pl.CostEstimate(flops=cost, bytes_accessed=1, transcendentals=0),
        name=name,
    )(scalars, *operands, *before, *through)


def pack_for_tp(key_vectors, value_vectors, groups, tp_own):
    count = lax.axis_size("tp")
    local = key_vectors.shape[0]
    columns = groups * HEAD_SIZE

    def kernel(own, key_hbm, value_hbm, *refs):
        outs, sems = refs[:-1], refs[-1]
        copies = []
        for step, out in enumerate(outs):
            block = pl.ds(pl.multiple_of(lax.rem(own[0] + step, count) * columns, HEAD_SIZE), columns)
            for kind, source in enumerate((key_hbm, value_hbm)):
                copies.append(pltpu.make_async_copy(source.at[:, block], out.at[kind], sems.at[2 * step + kind]))
        for copy in copies:
            copy.start()
        for copy in copies:
            copy.wait()

    shape = (2, local, columns)
    return pl.pallas_call(
        kernel,
        grid_spec=pltpu.PrefetchScalarGridSpec(
            num_scalar_prefetch=1,
            grid=(1,),
            in_specs=[pl.BlockSpec(memory_space=pltpu.HBM)] * 2,
            out_specs=[whole_block(shape)] * count,
            scratch_shapes=[pltpu.SemaphoreType.DMA((2 * count,))],
        ),
        out_shape=[jax.ShapeDtypeStruct(shape, jnp.bfloat16)] * count,
        name="pack_for_tp",
    )(tp_own, key_vectors, value_vectors)


def join_tokens(parts, bounds, tp_own):
    count = len(parts)
    local = parts[0].shape[1]

    def kernel(own, *refs):
        parts, outs = refs[:count], refs[count:]
        for (first, last), out in zip(bounds, outs):
            columns = slice(first * HEAD_SIZE, last * HEAD_SIZE)
            for step in range(count):
                source = lax.rem(own[0] - step + count, count)
                rows = pl.ds(pl.multiple_of(source * local, local), local)
                out[:, rows, :] = parts[step][:, :, columns]

    return small_kernel(
        kernel, tp_own, parts, [whole_block(part.shape) for part in parts],
        [(2, local * count, (last - first) * HEAD_SIZE) for first, last in bounds], [], "join_tokens",
    )


def even_window(own_pair):
    far = shifted(own_pair, WINDOW // 2)
    return own_pair, far, shifted(far, WINDOW // 2)


def for_x_swap(evens, place, own, before, name):
    def kernel(own, *refs):
        for bit in range(2):

            @pl.when(lax.rem(own[0] // 2, 2) == bit)
            def _(bit=bit):
                refs[-1][...] = refs[bit][...]

    pair = evens[place : place + 2]
    return small_kernel(
        kernel, own, pair, [whole_block(part.shape) for part in pair], [evens[0].shape], before, name
    )[0]


def whole_window(evens, x_sent, own, before, name):
    own_pair, far, beyond = evens
    x_pairs = [swapped(part, 2) for part in x_sent]
    half = WINDOW // 2

    def kernel(own, own_ref, far_ref, beyond_ref, near_x_ref, far_x_ref, *refs):
        out = refs[-1]
        evens = [own_ref, near_x_ref, far_ref, far_x_ref, beyond_ref]
        low_c = lax.rem(own[0], 2)
        for bit in range(2):

            @pl.when(low_c == bit)
            def _(bit=bit):
                for place in range(half):
                    out[place] = evens[place + bit][...]

    operands = [own_pair, far, beyond, *x_pairs]
    (c_sent,) = small_kernel(
        kernel, own, operands, [whole_block(part.shape) for part in operands],
        [(half, *own_pair.shape)], before, name,
    )
    return own_pair, far, *x_pairs, swapped(c_sent, 1)


def wide(part):
    return part.astype(jnp.float32)


def fold_cores(even, got, own, before, name):
    half = WINDOW // 2

    def kernel(own, even_ref, got_ref, *refs):
        sent, kept = refs[-2:]
        for bit in range(2):

            @pl.when(lax.rem(own[0], 2) == bit)
            def _(bit=bit):
                for place in range(half + 1):
                    out = sent.at[place // 2] if place % 2 else kept.at[place // 2]
                    total = None
                    if place < half:
                        total = wide(even_ref[place])
                    if 0 <= place - bit < half:
                        more = wide(got_ref[place - bit])
                        total = more if total is None else total + more
                    out[...] = jnp.zeros(out.shape, out.dtype) if total is None else total.astype(out.dtype)

    shape = even.shape[1:]
    return small_kernel(
        kernel, own, [even, got], [whole_block(even.shape)] * 2,
        [(half // 2, *shape), (half // 2 + 1, *shape)], before, name,
    )


def fold_x(parts, own, before, name, through=()):
    count = len(parts)
    operands = [array for sent, kept in parts for array in (kept, swapped(sent, 2))]
    shape = operands[0].shape[1:]

    def kernel(own, *refs):
        outs = refs[-3:]
        for bit in range(2):

            @pl.when(lax.rem(own[0] // 2, 2) == bit)
            def _(bit=bit):
                for index in range(count):
                    kept, got = refs[2 * index : 2 * index + 2]
                    for place, out in enumerate(outs):
                        total = wide(kept[place])
                        if 0 <= place - bit < got.shape[0]:
                            total = total + wide(got[place - bit])
                        out[index] = total.astype(out.dtype)

    return small_kernel(
        kernel, own, operands, [whole_block(part.shape) for part in operands], [(count, *shape)] * 3,
        before, name, through,
    )


def groups_of(refs, sizes):
    return [ref.at[index] for ref, size in zip(refs, sizes) for index in range(size)]


def fold_z(parts, own, before, name, cost):
    sizes = [part[0].shape[0] for part in parts]
    operands = [part[0] for part in parts] + [part[1] for part in parts]

    def kernel(own, *refs):
        out = refs[-1]
        shares, others = groups_of(refs, sizes), groups_of(refs[len(sizes) :], sizes)
        for index, (share, other) in enumerate(zip(shares, others)):
            out[index] = (wide(share[...]) + wide(other[...])).astype(out.dtype)

    return small_kernel(
        kernel, own, operands, [whole_block(part.shape) for part in operands],
        [(sum(sizes), *operands[0].shape[1:])], before, name, cost=cost,
    )[0]


def finish(terms, count, own, before, name):
    operands = [array for array, _ in terms]
    kinds, depth, rows = operands[0].shape[1:]

    def kernel(own, *refs):
        out = refs[-1]
        for index in range(count):
            parts = [
                ref.at[index - first]
                for ref, (array, first) in zip(refs, terms)
                if 0 <= index - first < array.shape[0]
            ]
            for kind in range(kinds):
                total = functools.reduce(jnp.add, [wide(part[kind]) for part in parts])
                out[index, kind] = total.T.astype(out.dtype)

    return small_kernel(
        kernel, own, operands, [whole_block(part.shape) for part in operands],
        [(count, kinds, rows, depth)], before, name,
    )[0]


def body(queries, key_vectors, value_vectors, output_gradient, doc_lengths):
    own = lax.axis_index("ctx")
    own_info = own.reshape(1).astype(jnp.int32)
    local = key_vectors.shape[0]
    all_groups = key_vectors.shape[1] // HEAD_SIZE
    tp_count = lax.axis_size("tp")
    groups = all_groups // tp_count
    tp_own = lax.axis_index("tp")
    tp_info = tp_own.reshape(1).astype(jnp.int32)

    middle = (groups + 1) // 2
    bounds = [(0, middle)] + ([(middle, groups)] if groups > 1 else [])
    packed = pack_for_tp(key_vectors, value_vectors, groups, tp_info)
    received = tp_received(lambda place, step: packed[step])
    chunks = join_tokens([packed[0], *received], bounds, tp_info)
    evens = [even_window(chunk) for chunk in chunks]
    x_sent = [[
        for_x_swap(evens[0], 0, own_info, [], "x_swap_0_near"),
        for_x_swap(evens[0], 1, own_info, [other[1] for other in evens[1:]], "x_swap_0_far"),
    ]]
    for later in evens[1:]:
        x_sent.append([
            for_x_swap(later, 0, own_info, [x_sent[0][1]], "x_swap_1_near"),
            for_x_swap(later, 1, own_info, [x_sent[0][1]], "x_swap_1_far"),
        ])
    windows = [whole_window(evens[0], x_sent[0], own_info, [part[1] for part in x_sent[1:]], "core_swap_0")]
    buffers = ()
    results, got, folded, nears, passing = [], [], [], [], []

    def fold_next_cores(before):
        group = len(folded)
        folded.append(fold_cores(results[group][2], got[group], own_info, before, f"fold_cores_{group}"))

    def fold_next_x(last, before, through=()):
        first = sum(part.shape[0] for part in nears)
        near, far, beyond, *handed = fold_x(folded[first : last + 1], own_info, before, f"fold_x_{first}", through)
        nears.append(near)
        if first == 0 and groups > 2:
            passing.append((shifted(far, -(WINDOW // 2)), shifted(beyond, -WINDOW)))
        else:
            passing.append((far, shifted(beyond, -(WINDOW // 2))))
        return handed

    for group in range(groups):
        waits = []
        if group >= 2:
            waits.append(folded[group - 2][0])
        if group >= 2 and group == groups - 1:
            waits.append(folded[group - 1][0])
        if group >= 3:
            waits.append(nears[-1])
        chunk = 0 if group < middle else 1
        results.append(
            attend_group(
                group, groups, own_info, doc_lengths, queries, output_gradient,
                windows[chunk], group - bounds[chunk][0], buffers, waits,
            )
        )
        *buffers, even, odd = results[-1]
        if 3 <= groups == group + 1:
            (odd,) = fold_next_x(group - 1, [part for pair in passing for part in pair], [odd])
        elif group >= 2:
            (odd,) = fold_next_x(group - 2, [], [odd])
        got.append(swapped(odd, 1))
        if group == 0 and groups > 1:
            windows.append(whole_window(evens[1], x_sent[1], own_info, [even], "core_swap_1"))
        if group >= 1 and len(folded) < group:
            fold_next_cores([even])
        if 2 <= group == groups - 2:
            fold_next_cores([])
    while len(folded) < groups:
        fold_next_cores([])
    while sum(part.shape[0] for part in nears) < groups:
        fold_next_x(sum(part.shape[0] for part in nears), [])

    def exchanged(total):
        def tokens_of(place, step=0):
            return lax.dynamic_slice_in_dim(total, place * local, local, total.ndim - 2)

        return in_tp_order(tokens_of(tp_own), tp_received(tokens_of))

    direct = 1 if groups > 2 else 0
    terms = [(part, 0) for part in (nears[0], *passing[0])] if direct else []
    split = len(passing) - 1
    early = groups - nears[-1].shape[0]
    late = fold_z(passing[split:], own_info, [], "fold_z_late", 1)
    if split > direct:
        joint = fold_z(passing[direct:split], own_info, nears[-1:], "fold_z_early", 1 << 34)
        terms += [(part, direct) for part in (nears[direct], shifted(joint, -(WINDOW // 2)))]
    finished = [finish(terms, early, own_info, [late], "finish_early")] if early else []
    terms = [(nears[-1], 0), (shifted(late, -(WINDOW // 2)), 0)]
    finished.append(finish(terms, groups - early, own_info, finished, "finish_late"))
    totals = [exchanged(part) for part in finished]
    ordered = [
        [part[source][group] for part in totals for group in range(part[source].shape[0])]
        for source in range(tp_count)
    ]

    def output(which):
        return jnp.concatenate([part[which] for source in ordered for part in source], axis=1)

    out, dq = buffers
    return out, dq, output(0), output(1)


def solution(mesh):
    tokens = P(("ctx", "tp"), None)
    heads = P("ctx", "tp")
    return jax.shard_map(
        body,
        mesh=mesh,
        in_specs=(heads, tokens, tokens, heads, P()),
        out_specs=(heads, heads, tokens, tokens),
        check_vma=False,
    )
```

```python
import functools
import math

import jax
import jax.numpy as jnp
from jax import lax
from jax.experimental import pallas as pl
from jax.experimental.pallas import tpu as pltpu
from jax.sharding import PartitionSpec as P

HEAD_SIZE = 128
WINDOW = 8
HEADS_AT_ONCE = 4
KERNEL_VMEM = 44 * 1024 * 1024
SCORE_SCALE = 1.0 / math.sqrt(HEAD_SIZE)
LOG2E = math.log2(math.e)
MASKED = -1e30


def dot(a, b):
    return jnp.dot(a, b, preferred_element_type=jnp.float32)


def dot_rows(a, b):
    return lax.dot_general(a, b, (((1,), (1,)), ((), ())), preferred_element_type=jnp.float32)


def group_kernel(
    group, place, heads, unread, own, doc_lengths,
    q_hbm, g_hbm, own_hbm, far_hbm, near_x_hbm, far_x_hbm, c_hbm, *rest,
):
    out_hbm, dq_hbm, even_hbm, odd_hbm, *scratch = rest[unread:]
    (
        q_in, q_all, q_turned, g_in, g_all, g_turned, k_win, v_win, outs, even, odd,
        bias, scores, weights, grads, highest, summed, delta, dq_acc,
        sems, k_sems, v_sems, grad_sems,
    ) = scratch
    rows = q_hbm.shape[0]
    at_once = min(heads, HEADS_AT_ONCE)
    repeats = 2 * rows // HEAD_SIZE
    half = WINDOW // 2
    spans = [slice(head * rows, (head + 1) * rows) for head in range(heads)]
    batches = [slice(head * rows, (head + at_once) * rows) for head in range(0, heads, at_once)]

    width = heads * HEAD_SIZE
    own_columns = pl.ds(group * width, width)
    columns = [slice(head * HEAD_SIZE, (head + 1) * HEAD_SIZE) for head in range(heads)]
    q_copy = pltpu.make_async_copy(q_hbm.at[:, own_columns], q_in, sems.at[0])
    g_copy = pltpu.make_async_copy(g_hbm.at[:, own_columns], g_in, sems.at[1])
    out_copy = pltpu.make_async_copy(outs, out_hbm.at[:, own_columns], sems.at[2])
    dq_copy = pltpu.make_async_copy(q_in, dq_hbm.at[:, own_columns], sems.at[3])
    window = [
        own_hbm, c_hbm.at[0], near_x_hbm, c_hbm.at[1], far_hbm, c_hbm.at[2], far_x_hbm, c_hbm.at[3]
    ]

    def window_copy(kind, pair, side, source):
        target, sems = (v_win.at[pair, pl.ds(side * rows, rows), pl.ds(0, HEAD_SIZE)], v_sems) if kind else (
            k_win.at[pair, pl.ds(side * rows, rows)], k_sems
        )
        block = source.at[kind, :, pl.ds(place * HEAD_SIZE, HEAD_SIZE)]
        return pltpu.make_async_copy(block, target, sems.at[2 * pair + side])

    def grad_copies(pair):
        return [
            pltpu.make_async_copy(even.at[pair], even_hbm.at[pair], grad_sems.at[2 * pair]),
            pltpu.make_async_copy(odd.at[pair], odd_hbm.at[pair], grad_sems.at[2 * pair + 1]),
        ]

    first = own[0] * rows
    doc_start = 0
    start = 0
    for doc in range(doc_lengths.shape[0]):
        doc_start = jnp.where(first >= start, start, doc_start)
        start = start + doc_lengths[doc]
    needed = jnp.clip(own[0] - doc_start // rows + 1, 1, WINDOW)
    trips = (needed + 1) // 2
    q_copy.start()
    for kind in range(2):
        for pair in range(half):

            @pl.when(pair < trips)
            def _(kind=kind, pair=pair):
                for side in range(2):
                    window_copy(kind, pair, side, window[2 * pair + side]).start()

    g_copy.start()
    query_pos = first + lax.broadcasted_iota(jnp.int32, (rows, HEAD_SIZE), 0)
    low = jnp.zeros((rows, HEAD_SIZE), jnp.int32)
    start = 0
    for doc in range(doc_lengths.shape[0]):
        low = jnp.where(query_pos >= start, start, low)
        start = start + doc_lengths[doc]
    v_win[:, :, HEAD_SIZE:] = jnp.ones((half, 2 * rows, HEAD_SIZE), jnp.bfloat16)

    def each_pair(step):
        def body(pair, carry):
            step(pair, False)
            return carry

        step(0, True)
        lax.fori_loop(1, trips, body, 0)

    def score_pair(pair, is_first):
        for spot in range(repeats):
            offset = 2 * pair + spot // (repeats // 2)
            key_pos = (
                first - offset * rows + spot % (repeats // 2) * HEAD_SIZE
                + lax.broadcasted_iota(jnp.int32, (rows, HEAD_SIZE), 1)
            )
            allowed = (key_pos >= low) & (key_pos <= query_pos)
            bias[:, spot * HEAD_SIZE : (spot + 1) * HEAD_SIZE] = jnp.where(allowed, 0.0, MASKED)
        for side in range(2):
            window_copy(0, pair, side, own_hbm).wait()
        for batch in batches:
            part = dot_rows(q_all[batch, :], k_win[pair])
            for head in range(at_once):
                here = slice(batch.start + head * rows, batch.start + (head + 1) * rows)
                if is_first:
                    q_turned[:, here] = q_all[here, :].T
                piece = part[head * rows : (head + 1) * rows] * (SCORE_SCALE * LOG2E) + bias[...]
                scores[pair, here, :] = piece
                pieces = [piece[:, spot * HEAD_SIZE : (spot + 1) * HEAD_SIZE] for spot in range(repeats)]
                most = functools.reduce(jnp.maximum, pieces)
                highest[here, :] = most if is_first else jnp.maximum(highest[here, :], most)

    q_copy.wait()
    for span, column in zip(spans, columns):
        q_all[span, :] = q_in[:, column]
    each_pair(score_pair)

    def sum_pair(pair, is_first):
        for side in range(2):
            window_copy(1, pair, side, own_hbm).wait()
        for batch in batches:
            for head in range(at_once):
                here = slice(batch.start + head * rows, batch.start + (head + 1) * rows)
                top = highest[here, :]
                if is_first:
                    top = jnp.broadcast_to(jnp.max(top, axis=1, keepdims=True), (rows, HEAD_SIZE))
                    highest[here, :] = top
                top = jnp.concatenate([top] * repeats, axis=1)
                weights[pair, here, :] = jnp.exp2(scores[pair, here, :] - top).astype(jnp.bfloat16)
            part = dot(weights[pair, batch, :], v_win[pair])
            summed[batch, :] = part if is_first else summed[batch, :] + part

    each_pair(sum_pair)

    def close_head(head):
        span, column = spans[head], columns[head]
        inverse = 1.0 / summed[span, HEAD_SIZE:]
        output = (summed[span, :HEAD_SIZE] * inverse).astype(jnp.bfloat16)
        outs[:, column] = output
        scaled = (g_in[:, column].astype(jnp.float32) * inverse).astype(jnp.bfloat16)
        g_all[span, :] = scaled
        g_turned[:, span] = scaled.T
        terms = output.astype(jnp.float32) * scaled.astype(jnp.float32)
        upper = terms.astype(jnp.bfloat16)
        grads[span, :HEAD_SIZE] = upper
        grads[span, HEAD_SIZE : 2 * HEAD_SIZE] = (terms - upper.astype(jnp.float32)).astype(jnp.bfloat16)

    g_copy.wait()
    ones = jnp.ones((2 * HEAD_SIZE, HEAD_SIZE), jnp.bfloat16)

    def grad_pair(pair, is_first):
        for number, batch in enumerate(batches):
            if is_first:
                for head in range(number * at_once, (number + 1) * at_once):
                    close_head(head)
                delta[batch, :] = dot(grads[batch, : 2 * HEAD_SIZE], ones)
            part = dot_rows(g_all[batch, :], v_win[pair, :, :HEAD_SIZE])
            for head in range(at_once):
                here = slice(batch.start + head * rows, batch.start + (head + 1) * rows)
                piece = part[head * rows : (head + 1) * rows] - jnp.concatenate([delta[here, :]] * repeats, axis=1)
                grads[here, :] = (weights[pair, here, :].astype(jnp.float32) * piece).astype(jnp.bfloat16)
            part = dot(grads[batch, :], k_win[pair])
            dq_acc[batch, :] = part if is_first else dq_acc[batch, :] + part
        dk = (dot(q_turned[...], grads[...]) * SCORE_SCALE).astype(jnp.bfloat16)
        dv = dot(g_turned[...], weights[pair]).astype(jnp.bfloat16)
        even[pair, 0] = dk[:, :rows]
        even[pair, 1] = dv[:, :rows]
        odd[pair, 0] = dk[:, rows:]
        odd[pair, 1] = dv[:, rows:]
        for copy in grad_copies(pair) + ([out_copy] if is_first else []):
            copy.start()

    each_pair(grad_pair)

    def clear_pair(pair, carry):
        even[pair] = jnp.zeros(even.shape[1:], jnp.bfloat16)
        odd[pair] = jnp.zeros(odd.shape[1:], jnp.bfloat16)
        for copy in grad_copies(pair):
            copy.start()
        return carry

    lax.fori_loop(trips, half, clear_pair, 0)
    for span, column in zip(spans, columns):
        q_in[:, column] = (dq_acc[span, :] * SCORE_SCALE).astype(jnp.bfloat16)
    dq_copy.start()
    for copy in [out_copy] + [copy for pair in range(half) for copy in grad_copies(pair)] + [dq_copy]:
        copy.wait()


def attend_group(
    group, groups, own, doc_lengths, queries, gradient, window, place, buffers, before
):
    rows, width = queries.shape
    columns = width // groups
    heads = columns // HEAD_SIZE
    keys = WINDOW * rows
    stacked = heads * rows
    half = WINDOW // 2
    grads = jax.ShapeDtypeStruct((half, 2, HEAD_SIZE, rows), jnp.bfloat16)
    unread = len(buffers) + len(before)
    anywhere = pl.BlockSpec(memory_space=pl.ANY)
    short = lambda *shape: pltpu.VMEM(shape, jnp.bfloat16)
    full = lambda *shape: pltpu.VMEM(shape, jnp.float32)
    sems = lambda count: pltpu.SemaphoreType.DMA((count,))
    return pl.pallas_call(
        functools.partial(group_kernel, group, place, heads, unread),
        grid_spec=pltpu.PrefetchScalarGridSpec(
            num_scalar_prefetch=2,
            grid=(1,),
            in_specs=[anywhere] * (7 + unread),
            out_specs=[anywhere] * 4,
            scratch_shapes=[
                short(rows, columns),
                short(stacked, HEAD_SIZE),
                short(HEAD_SIZE, stacked),
                short(rows, columns),
                short(stacked, HEAD_SIZE),
                short(HEAD_SIZE, stacked),
                short(half, 2 * rows, HEAD_SIZE),
                short(half, 2 * rows, 2 * HEAD_SIZE),
                short(rows, columns),
                short(*grads.shape),
                short(*grads.shape),
                full(rows, 2 * rows),
                full(half, stacked, 2 * rows),
                short(half, stacked, 2 * rows),
                short(stacked, 2 * rows),
                full(stacked, HEAD_SIZE),
                full(stacked, 2 * HEAD_SIZE),
                full(stacked, HEAD_SIZE),
                full(stacked, HEAD_SIZE),
                sems(4), sems(WINDOW), sems(WINDOW), sems(WINDOW),
            ],
        ),
        out_shape=[
            jax.ShapeDtypeStruct(queries.shape, jnp.bfloat16),
            jax.ShapeDtypeStruct(queries.shape, jnp.bfloat16),
            grads,
            grads,
        ],
        input_output_aliases={9 + number: number for number in range(len(buffers))},
        compiler_params=pltpu.CompilerParams(vmem_limit_bytes=KERNEL_VMEM),
        cost_estimate=pl.CostEstimate(
            flops=4 * 6 * 2 * heads * rows * keys * HEAD_SIZE,
            bytes_accessed=8 * rows * columns + 8 * keys * HEAD_SIZE,
            transcendentals=heads * rows * keys,
        ),
        name=f"attend_group_{group}",
    )(own, doc_lengths, queries, gradient, *window, *buffers, *before)


def shifted(value, steps):
    count = lax.axis_size("ctx")
    sources = range(max(0, -steps), min(count, count - steps))
    return lax.ppermute(value, "ctx", [(source, source + steps) for source in sources])


def swapped(value, bit):
    return lax.ppermute(value, "ctx", [(place, place ^ bit) for place in range(lax.axis_size("ctx"))])


def tp_received(block_for):
    count = lax.axis_size("tp")
    own = lax.axis_index("tp")
    received = []
    for step in range(1, count):
        sent = block_for(lax.rem(own + step, count), step)
        received.append(lax.ppermute(sent, "tp", [(place, (place + step) % count) for place in range(count)]))
    return received


def in_tp_order(mine, received):
    count = lax.axis_size("tp")
    own = lax.axis_index("tp")
    parts = [mine, *received]
    ordered = []
    for place in range(count):
        part = parts[0]
        for step in range(1, count):
            part = jnp.where(lax.rem(own - step + count, count) == place, parts[step], part)
        ordered.append(part)
    return ordered


def whole_block(shape):
    return pl.BlockSpec(shape, lambda i, *_: (0,) * len(shape))


def small_kernel(kernel, scalars, operands, specs, outs, before, name, through=(), cost=1):
    if through:
        inner, handed = kernel, len(through)
        kernel = lambda *refs: inner(*refs[:-handed])
    first = 1 + len(operands) + len(before)
    return pl.pallas_call(
        kernel,
        grid_spec=pltpu.PrefetchScalarGridSpec(
            num_scalar_prefetch=1,
            grid=(1,),
            in_specs=specs + [pl.BlockSpec(memory_space=pl.ANY)] * (len(before) + len(through)),
            out_specs=[whole_block(shape) for shape in outs] + [pl.BlockSpec(memory_space=pl.ANY)] * len(through),
        ),
        out_shape=[jax.ShapeDtypeStruct(shape, jnp.bfloat16) for shape in outs]
        + [jax.ShapeDtypeStruct(part.shape, part.dtype) for part in through],
        input_output_aliases={first + number: len(outs) + number for number in range(len(through))},
        compiler_params=pltpu.CompilerParams(vmem_limit_bytes=32 * 1024 * 1024),
        cost_estimate=pl.CostEstimate(flops=cost, bytes_accessed=1, transcendentals=0),
        name=name,
    )(scalars, *operands, *before, *through)


def pack_for_tp(key_vectors, value_vectors, groups, tp_own):
    count = lax.axis_size("tp")
    local = key_vectors.shape[0]
    columns = groups * HEAD_SIZE

    def kernel(own, key_hbm, value_hbm, *refs):
        outs, sems = refs[:-1], refs[-1]
        copies = []
        for step, out in enumerate(outs):
            block = pl.ds(pl.multiple_of(lax.rem(own[0] + step, count) * columns, HEAD_SIZE), columns)
            for kind, source in enumerate((key_hbm, value_hbm)):
                copies.append(pltpu.make_async_copy(source.at[:, block], out.at[kind], sems.at[2 * step + kind]))
        for copy in copies:
            copy.start()
        for copy in copies:
            copy.wait()

    shape = (2, local, columns)
    return pl.pallas_call(
        kernel,
        grid_spec=pltpu.PrefetchScalarGridSpec(
            num_scalar_prefetch=1,
            grid=(1,),
            in_specs=[pl.BlockSpec(memory_space=pltpu.HBM)] * 2,
            out_specs=[whole_block(shape)] * count,
            scratch_shapes=[pltpu.SemaphoreType.DMA((2 * count,))],
        ),
        out_shape=[jax.ShapeDtypeStruct(shape, jnp.bfloat16)] * count,
        name="pack_for_tp",
    )(tp_own, key_vectors, value_vectors)


def join_tokens(parts, bounds, tp_own):
    count = len(parts)
    local = parts[0].shape[1]

    def kernel(own, *refs):
        parts, outs = refs[:count], refs[count:]
        for (first, last), out in zip(bounds, outs):
            columns = slice(first * HEAD_SIZE, last * HEAD_SIZE)
            for step in range(count):
                source = lax.rem(own[0] - step + count, count)
                rows = pl.ds(pl.multiple_of(source * local, local), local)
                out[:, rows, :] = parts[step][:, :, columns]

    return small_kernel(
        kernel, tp_own, parts, [whole_block(part.shape) for part in parts],
        [(2, local * count, (last - first) * HEAD_SIZE) for first, last in bounds], [], "join_tokens",
    )


def even_window(own_pair):
    far = shifted(own_pair, WINDOW // 2)
    return own_pair, far, shifted(far, WINDOW // 2)


def for_x_swap(evens, place, own, before, name):
    def kernel(own, *refs):
        for bit in range(2):

            @pl.when(lax.rem(own[0] // 2, 2) == bit)
            def _(bit=bit):
                refs[-1][...] = refs[bit][...]

    pair = evens[place : place + 2]
    return small_kernel(
        kernel, own, pair, [whole_block(part.shape) for part in pair], [evens[0].shape], before, name
    )[0]


def whole_window(evens, x_sent, own, before, name):
    own_pair, far, beyond = evens
    x_pairs = [swapped(part, 2) for part in x_sent]
    half = WINDOW // 2

    def kernel(own, own_ref, far_ref, beyond_ref, near_x_ref, far_x_ref, *refs):
        out = refs[-1]
        evens = [own_ref, near_x_ref, far_ref, far_x_ref, beyond_ref]
        low_c = lax.rem(own[0], 2)
        for bit in range(2):

            @pl.when(low_c == bit)
            def _(bit=bit):
                for place in range(half):
                    out[place] = evens[place + bit][...]

    operands = [own_pair, far, beyond, *x_pairs]
    (c_sent,) = small_kernel(
        kernel, own, operands, [whole_block(part.shape) for part in operands],
        [(half, *own_pair.shape)], before, name,
    )
    return own_pair, far, *x_pairs, swapped(c_sent, 1)


def wide(part):
    return part.astype(jnp.float32)


def fold_cores(even, got, own, before, name):
    half = WINDOW // 2

    def kernel(own, even_ref, got_ref, *refs):
        sent, kept = refs[-2:]
        for bit in range(2):

            @pl.when(lax.rem(own[0], 2) == bit)
            def _(bit=bit):
                for place in range(half + 1):
                    out = sent.at[place // 2] if place % 2 else kept.at[place // 2]
                    total = None
                    if place < half:
                        total = wide(even_ref[place])
                    if 0 <= place - bit < half:
                        more = wide(got_ref[place - bit])
                        total = more if total is None else total + more
                    out[...] = jnp.zeros(out.shape, out.dtype) if total is None else total.astype(out.dtype)

    shape = even.shape[1:]
    return small_kernel(
        kernel, own, [even, got], [whole_block(even.shape)] * 2,
        [(half // 2, *shape), (half // 2 + 1, *shape)], before, name,
    )


def fold_x(parts, own, before, name, through=()):
    count = len(parts)
    operands = [array for sent, kept in parts for array in (kept, swapped(sent, 2))]
    shape = operands[0].shape[1:]

    def kernel(own, *refs):
        outs = refs[-3:]
        for bit in range(2):

            @pl.when(lax.rem(own[0] // 2, 2) == bit)
            def _(bit=bit):
                for index in range(count):
                    kept, got = refs[2 * index : 2 * index + 2]
                    for place, out in enumerate(outs):
                        total = wide(kept[place])
                        if 0 <= place - bit < got.shape[0]:
                            total = total + wide(got[place - bit])
                        out[index] = total.astype(out.dtype)

    return small_kernel(
        kernel, own, operands, [whole_block(part.shape) for part in operands], [(count, *shape)] * 3,
        before, name, through,
    )


def groups_of(refs, sizes):
    return [ref.at[index] for ref, size in zip(refs, sizes) for index in range(size)]


def fold_z(parts, own, before, name, cost):
    sizes = [part[0].shape[0] for part in parts]
    operands = [part[0] for part in parts] + [part[1] for part in parts]

    def kernel(own, *refs):
        out = refs[-1]
        shares, others = groups_of(refs, sizes), groups_of(refs[len(sizes) :], sizes)
        for index, (share, other) in enumerate(zip(shares, others)):
            out[index] = (wide(share[...]) + wide(other[...])).astype(out.dtype)

    return small_kernel(
        kernel, own, operands, [whole_block(part.shape) for part in operands],
        [(sum(sizes), *operands[0].shape[1:])], before, name, cost=cost,
    )[0]


def finish(terms, count, own, before, name):
    operands = [array for array, _ in terms]
    kinds, depth, rows = operands[0].shape[1:]

    def kernel(own, *refs):
        out = refs[-1]
        for index in range(count):
            parts = [
                ref.at[index - first]
                for ref, (array, first) in zip(refs, terms)
                if 0 <= index - first < array.shape[0]
            ]
            for kind in range(kinds):
                total = functools.reduce(jnp.add, [wide(part[kind]) for part in parts])
                out[index, kind] = total.T.astype(out.dtype)

    return small_kernel(
        kernel, own, operands, [whole_block(part.shape) for part in operands],
        [(count, kinds, rows, depth)], before, name,
    )[0]


def body(queries, key_vectors, value_vectors, output_gradient, doc_lengths):
    own = lax.axis_index("ctx")
    own_info = own.reshape(1).astype(jnp.int32)
    local = key_vectors.shape[0]
    all_groups = key_vectors.shape[1] // HEAD_SIZE
    tp_count = lax.axis_size("tp")
    groups = all_groups // tp_count
    tp_own = lax.axis_index("tp")
    tp_info = tp_own.reshape(1).astype(jnp.int32)

    middle = (groups + 1) // 2
    bounds = [(0, middle)] + ([(middle, groups)] if groups > 1 else [])
    packed = pack_for_tp(key_vectors, value_vectors, groups, tp_info)
    received = tp_received(lambda place, step: packed[step])
    chunks = join_tokens([packed[0], *received], bounds, tp_info)
    evens = [even_window(chunk) for chunk in chunks]
    x_sent = [[
        for_x_swap(evens[0], 0, own_info, [], "x_swap_0_near"),
        for_x_swap(evens[0], 1, own_info, [other[1] for other in evens[1:]], "x_swap_0_far"),
    ]]
    for later in evens[1:]:
        x_sent.append([
            for_x_swap(later, 0, own_info, [x_sent[0][1]], "x_swap_1_near"),
            for_x_swap(later, 1, own_info, [x_sent[0][1]], "x_swap_1_far"),
        ])
    windows = [whole_window(evens[0], x_sent[0], own_info, [part[1] for part in x_sent[1:]], "core_swap_0")]
    buffers = ()
    results, got, folded, nears, passing = [], [], [], [], []

    def fold_next_cores(before):
        group = len(folded)
        folded.append(fold_cores(results[group][2], got[group], own_info, before, f"fold_cores_{group}"))

    def fold_next_x(last, before, through=()):
        first = sum(part.shape[0] for part in nears)
        near, far, beyond, *handed = fold_x(folded[first : last + 1], own_info, before, f"fold_x_{first}", through)
        nears.append(near)
        if first == 0 and groups > 2:
            passing.append((shifted(far, -(WINDOW // 2)), shifted(beyond, -WINDOW)))
        else:
            passing.append((far, shifted(beyond, -(WINDOW // 2))))
        return handed

    for group in range(groups):
        waits = []
        if group >= 2:
            waits.append(folded[group - 2][0])
        if group >= 2 and group == groups - 1:
            waits.append(folded[group - 1][0])
        if group >= 3:
            waits.append(nears[-1])
        chunk = 0 if group < middle else 1
        results.append(
            attend_group(
                group, groups, own_info, doc_lengths, queries, output_gradient,
                windows[chunk], group - bounds[chunk][0], buffers, waits,
            )
        )
        *buffers, even, odd = results[-1]
        if 3 <= groups == group + 1:
            (odd,) = fold_next_x(group - 1, [part for pair in passing for part in pair], [odd])
        elif group >= 2:
            (odd,) = fold_next_x(group - 2, [], [odd])
        got.append(swapped(odd, 1))
        if group == 0 and groups > 1:
            windows.append(whole_window(evens[1], x_sent[1], own_info, [even], "core_swap_1"))
        if group >= 1 and len(folded) < group:
            fold_next_cores([even])
        if 2 <= group == groups - 2:
            fold_next_cores([])
    while len(folded) < groups:
        fold_next_cores([])
    while sum(part.shape[0] for part in nears) < groups:
        fold_next_x(sum(part.shape[0] for part in nears), [])

    def exchanged(total):
        def tokens_of(place, step=0):
            return lax.dynamic_slice_in_dim(total, place * local, local, total.ndim - 2)

        return in_tp_order(tokens_of(tp_own), tp_received(tokens_of))

    direct = 1 if groups > 2 else 0
    terms = [(part, 0) for part in (nears[0], *passing[0])] if direct else []
    split = len(passing) - 1
    early = groups - nears[-1].shape[0]
    late = fold_z(passing[split:], own_info, [], "fold_z_late", 1)
    if split > direct:
        joint = fold_z(passing[direct:split], own_info, nears[-1:], "fold_z_early", 1 << 34)
        terms += [(part, direct) for part in (nears[direct], shifted(joint, -(WINDOW // 2)))]
    finished = [finish(terms, early, own_info, [late], "finish_early")] if early else []
    terms = [(nears[-1], 0), (shifted(late, -(WINDOW // 2)), 0)]
    finished.append(finish(terms, groups - early, own_info, finished, "finish_late"))
    totals = [exchanged(part) for part in finished]
    ordered = [
        [part[source][group] for part in totals for group in range(part[source].shape[0])]
        for source in range(tp_count)
    ]

    def output(which):
        return jnp.concatenate([part[which] for source in ordered for part in source], axis=1)

    out, dq = buffers
    return out, dq, output(0), output(1)


def solution(mesh):
    tokens = P(("ctx", "tp"), None)
    heads = P("ctx", "tp")
    return jax.shard_map(
        body,
        mesh=mesh,
        in_specs=(heads, tokens, tokens, heads, P()),
        out_specs=(heads, heads, tokens, tokens),
        check_vma=False,
    )
```
